32 devices in a mesh: dp: 4 (over x, core), seq: 8 (over z, y).
Axes of the slice: x: 2, y: 2, z: 4, core: 2. Of those that a mesh axis runs over, the one named last changes fastest.
Arguments:
- tokens: bfloat16 [16, 1024, 1152], P('dp', 'seq'), may hold values from -6 to 6
- segment_ids: int32 [16, 1024], P('dp', 'seq'), may hold values from 0 to 3, never falling along the last dimension, each value on 1 to 512 neighbouring positions
- w_query: float32 [1152, 1024], P(('dp', 'seq')), may hold values from -0.1875 to 0.1875
- w_key: float32 [1152, 256], P(('dp', 'seq')), may hold values from -0.1875 to 0.1875
- w_value: float32 [1152, 256], P(('dp', 'seq')), may hold values from -0.1875 to 0.1875
- w_out: float32 [1024, 1152], P(('dp', 'seq')), may hold values from -0.1875 to 0.1875
- w_gate: float32 [1152, 6912], P(('dp', 'seq')), may hold values from -0.1875 to 0.1875
- w_up: float32 [1152, 6912], P(('dp', 'seq')), may hold values from -0.1875 to 0.1875
- w_down: float32 [6912, 1152], P(('dp', 'seq')), may hold values from -0.078125 to 0.078125
- g_in: float32 [1152], P(('dp', 'seq')), may hold values from 0.25 to 1.75
- g_post_attn: float32 [1152], P(('dp', 'seq')), may hold values from 0.25 to 1.75
- g_pre_ffn: float32 [1152], P(('dp', 'seq')), may hold values from 0.25 to 1.75
- g_post_ffn: float32 [1152], P(('dp', 'seq')), may hold values from 0.25 to 1.75
- g_query: float32 [256], P(('dp', 'seq')), may hold values from 0.25 to 1.75
- g_key: float32 [256], P(('dp', 'seq')), may hold values from 0.25 to 1.75
- cotangent: bfloat16 [16, 1024, 1152], P('dp', 'seq'), may hold values from -6 to 6
Outputs:
- output: bfloat16 [16, 1024, 1152], P('dp', 'seq')
- grad_tokens: bfloat16 [16, 1024, 1152], P('dp', 'seq')
- grad_query: float32 [1152, 1024], P(('dp', 'seq'))
- grad_key: float32 [1152, 256], P(('dp', 'seq'))
- grad_value: float32 [1152, 256], P(('dp', 'seq'))
- grad_out: float32 [1024, 1152], P(('dp', 'seq'))
- grad_gate: float32 [1152, 6912], P(('dp', 'seq'))
- grad_up: float32 [1152, 6912], P(('dp', 'seq'))
- grad_down: float32 [6912, 1152], P(('dp', 'seq'))
- grad_in_norm: float32 [1152], P(('dp', 'seq'))
- grad_post_attn_norm: float32 [1152], P(('dp', 'seq'))
- grad_pre_ffn_norm: float32 [1152], P(('dp', 'seq'))
- grad_post_ffn_norm: float32 [1152], P(('dp', 'seq'))
- grad_query_norm: float32 [256], P(('dp', 'seq'))
- grad_key_norm: float32 [256], P(('dp', 'seq'))
The draws below stay inside these ranges and needn't reach their ends.
Inputs may be any that keep to these rules, and one draw needn't show every extreme that they name: `segment_ids`: in each row the ids start at 0 and never fall; every id of 0 to 3 appears, and each document has 1 to 512 positions.
All inputs are finite; a program needn't handle non-finite values.
Results may differ from the reference program's by a relative error of at most 0.018.
The reference program's roundings to bfloat16 on the way count: a program that leaves them out, or rounds other values in their place, can miss the bound.
Values may be sent and summed in bfloat16 or wider, within the bound.
No kernel may reach another device: no remote copies, remote signals or barrier semaphores. Data moves between devices by JAX's collectives and lax.ppermute only.
A program may use at most 320 MiB of HBM per device.

```python
import math
import jax
import jax.numpy as jnp
import numpy as np
from jax import lax

D = 1152
HEADS = 4
HEAD = 256
FF = 6912
LEN = 1024
DOCS = 4
ROWS = 16


def shard_levels(stream_key, dims, pieces, smallest, top_value):
    def one(position, parts):
        draws = jax.random.uniform(jax.random.fold_in(jax.random.fold_in(stream_key, 6), position), (parts,), jnp.float32, smallest / len(pieces), top_value / len(pieces))
        return jnp.repeat(jnp.exp(draws), dims[position] // parts).reshape((-1,) + (1,) * (len(dims) - position - 1))

    level = one(*pieces[0])
    for cut in pieces[1:]:
        level = level * one(*cut)
    return level


def length_profile(amount, total, limit, slope):
    loads = [(1 << 20) // math.isqrt(grade ** slope) + 1 for grade in range(2, amount + 1)]
    rest, counts = total - limit - (amount - 1), [1] * (amount - 1)
    while rest > 0:
        free = [i for i in range(amount - 1) if counts[i] < limit]
        pool, left = sum([loads[i] for i in free]), rest
        for i in free:
            extra = min(limit - counts[i], max(1, left * loads[i] // pool), rest)
            counts[i] = counts[i] + extra
            rest = rest - extra
    return np.array([limit] + counts)


def ragged(key, number_of, total, limit, lean):
    if number_of == 2:
        one = jax.random.randint(key, (), max(1, total - limit), min(limit, total - 1) + 1)
        return jnp.stack([one, total - one])
    lengths = jnp.asarray(length_profile(number_of, total, limit, lean), jnp.int32)
    couples = (number_of - 1) // 2
    source_of, taker = lengths[1:1 + 2 * couples:2], lengths[2:2 + 2 * couples:2]
    margin = jnp.minimum(source_of - 1, limit - taker)
    shifted = jax.random.randint(jax.random.fold_in(key, 1), (couples,), 0, 1 << 20) % (margin + 1)
    lengths = lengths.at[1:1 + 2 * couples:2].set(source_of - shifted).at[2:2 + 2 * couples:2].set(taker + shifted)
    return lengths[jax.random.permutation(jax.random.fold_in(key, 2), number_of)]


def bell_draw(rng, extent, spread, reach, pieces=(), kind=jnp.bfloat16):
    array = jax.random.normal(rng, extent, jnp.float32) * spread
    if len(pieces) > 0:
        array = shard_levels(rng, extent, pieces, -0.22, 0.18) * array
    return jnp.clip(array, min=-reach, max=reach).astype(kind)


def setup_inputs(seed: int = 0) -> dict:
    arg_keys = jax.random.split(jax.random.key(seed), 17)
    tokens = bell_draw(arg_keys[0], (ROWS, LEN, D), 1.0, 6.0, ((0, 4), (1, 8)))
    segment_ids = jax.vmap(lambda own: jnp.searchsorted(jnp.cumsum(ragged(own, DOCS, LEN, LEN // 2, 2)), jnp.arange(LEN), side="right"))(jax.random.split(arg_keys[1], ROWS)).reshape((ROWS, LEN)).astype(jnp.int32)
    w_query = bell_draw(arg_keys[2], (D, HEADS * HEAD), D ** -0.5, 0.1875, ((0, 32),), jnp.float32)
    w_key = bell_draw(arg_keys[3], (D, HEAD), D ** -0.5, 0.1875, ((0, 32),), jnp.float32)
    w_value = bell_draw(arg_keys[4], (D, HEAD), D ** -0.5, 0.1875, ((0, 32),), jnp.float32)
    w_out = bell_draw(arg_keys[5], (HEADS * HEAD, D), (HEADS * HEAD) ** -0.5, 0.1875, ((0, 32),), jnp.float32)
    w_gate = bell_draw(arg_keys[6], (D, FF), D ** -0.5, 0.1875, ((0, 32),), jnp.float32)
    w_up = bell_draw(arg_keys[7], (D, FF), D ** -0.5, 0.1875, ((0, 32),), jnp.float32)
    w_down = bell_draw(arg_keys[8], (FF, D), FF ** -0.5, 0.078125, ((0, 32),), jnp.float32)
    g_in = jnp.clip(1.0 + 0.15 * jax.random.normal(arg_keys[9], (D,), jnp.float32), 0.25, 1.75)
    g_post_attn = jnp.clip(1.0 + 0.15 * jax.random.normal(arg_keys[10], (D,), jnp.float32), 0.25, 1.75)
    g_pre_ffn = jnp.clip(1.0 + 0.15 * jax.random.normal(arg_keys[11], (D,), jnp.float32), 0.25, 1.75)
    g_post_ffn = jnp.clip(1.0 + 0.15 * jax.random.normal(arg_keys[12], (D,), jnp.float32), 0.25, 1.75)
    g_query = jnp.clip(1.0 + 0.15 * jax.random.normal(arg_keys[13], (HEAD,), jnp.float32), 0.25, 1.75)
    g_key = jnp.clip(1.0 + 0.15 * jax.random.normal(arg_keys[14], (HEAD,), jnp.float32), 0.25, 1.75)
    cotangent = bell_draw(arg_keys[15], (ROWS, LEN, D), 1.0, 6.0, ((0, 4), (1, 8)))
    return dict(tokens=tokens, segment_ids=segment_ids, w_query=w_query, w_key=w_key, w_value=w_value, w_out=w_out, w_gate=w_gate, w_up=w_up, w_down=w_down, g_in=g_in, g_post_attn=g_post_attn, g_pre_ffn=g_pre_ffn, g_post_ffn=g_post_ffn, g_query=g_query, g_key=g_key, cotangent=cotangent)


@jax.custom_vjp
def low(v):
    return lax.optimization_barrier(v.astype(jnp.bfloat16)).astype(jnp.float32)

@jax.custom_vjp
def low_back(v):
    return v

def low_keep(v):
    return (low(v), None)

def low_pass(kept, grad):
    return (grad,)

def back_keep(v):
    return (v, None)

def back_low(kept, grad):
    return (low(grad),)
low.defvjp(low_keep, low_pass)
low_back.defvjp(back_keep, back_low)
EPSILON = 1e-06
ROPE_BASE = 1000000.0
HIGHEST = lax.Precision.HIGHEST

def matmul_high(left, right):
    return jnp.dot(left, right, precision=HIGHEST)

def rms_scale(values, gain_vec):
    return values * lax.rsqrt(lax.optimization_barrier(jnp.mean(values * values, axis=-1, keepdims=True)) + EPSILON) * gain_vec

def rope_tables(positions, head_width):
    half_width = head_width // 2
    inverse = ROPE_BASE ** (-(jnp.arange(half_width, dtype=jnp.float32) * 2.0 / head_width))
    angles = positions.astype(jnp.float32)[..., None] * inverse
    return (jnp.cos(angles), jnp.sin(angles))

def rotate(values, cosine, sine_part):
    half_width = values.shape[-1] // 2
    first_half = values[..., :half_width]
    second_half = values[..., half_width:]
    return jnp.concatenate([first_half * cosine - second_half * sine_part, second_half * cosine + first_half * sine_part], axis=-1)

def row_layer(inputs_row, segments_row, weights):
    w_query, w_key, w_value, w_out, w_gate, w_up, w_down, g_in, g_post_attn, g_pre_ffn, g_post_ffn, g_query, g_key = weights
    row_length = inputs_row.shape[0]
    key_order = jnp.arange(row_length, dtype=jnp.int32)
    starts = lax.optimization_barrier(jnp.sum((segments_row[None, :] < segments_row[:, None]).astype(jnp.int32), axis=1))
    cosine, sine_part = rope_tables(key_order - starts, HEAD)
    h_in = low(rms_scale(inputs_row, g_in))
    q_proj = low_back(matmul_high(h_in, w_query)).reshape(row_length, HEADS, HEAD)
    k_proj = low_back(matmul_high(h_in, w_key))
    value_low = low(low_back(matmul_high(h_in, w_value)))
    query_low = low(rotate(rms_scale(q_proj, g_query), cosine[:, None, :], sine_part[:, None, :]))
    key_low = low(rotate(rms_scale(k_proj, g_key), cosine, sine_part))
    scores = low_back(jnp.einsum('qhd,kd->hqk', query_low, key_low, precision=HIGHEST) * HEAD ** (-0.5))
    allowed = (segments_row[None, :] == segments_row[:, None]) & (key_order[None, :] <= key_order[:, None])
    probs_low = low(jax.nn.softmax(jnp.where(allowed[None], scores, -1e+30), axis=-1))
    mixed_low = low(low_back(jnp.einsum('hqk,kd->qhd', probs_low, value_low, precision=HIGHEST)))
    attn_out = low_back(matmul_high(mixed_low.reshape(row_length, HEADS * HEAD), w_out))
    residual = inputs_row + rms_scale(attn_out, g_post_attn)
    h_ffn = low(rms_scale(residual, g_pre_ffn))
    gate_proj = low_back(matmul_high(h_ffn, w_gate))
    up_proj = low_back(matmul_high(h_ffn, w_up))
    hidden = low(jax.nn.gelu(gate_proj, approximate=True) * up_proj)
    ffn_out = low_back(matmul_high(hidden, w_down))
    return residual + rms_scale(ffn_out, g_post_ffn)

def reference(tokens, segment_ids, w_query, w_key, w_value, w_out, w_gate, w_up, w_down, g_in, g_post_attn, g_pre_ffn, g_post_ffn, g_query, g_key, cotangent):
    weights = (w_query, w_key, w_value, w_out, w_gate, w_up, w_down, g_in, g_post_attn, g_pre_ffn, g_post_ffn, g_query, g_key)

    def forward(inputs_all, weight_set):
        rounded = tuple((low(weight_item) for weight_item in weight_set))

        def one_row(row_pair):
            return row_layer(row_pair[0], row_pair[1], rounded)
        return lax.map(jax.checkpoint(one_row), (inputs_all, segment_ids))
    outputs, pullback = jax.vjp(forward, tokens.astype(jnp.float32), weights)
    grad_inputs, grad_weights = pullback(cotangent.astype(jnp.float32))
    return (outputs.astype(jnp.bfloat16), grad_inputs.astype(jnp.bfloat16), grad_weights[0], grad_weights[1], grad_weights[2], grad_weights[3], grad_weights[4], grad_weights[5], grad_weights[6], grad_weights[7], grad_weights[8], grad_weights[9], grad_weights[10], grad_weights[11], grad_weights[12])
```

```python
import math

import jax
import jax.numpy as jnp
from jax import lax
from jax.sharding import Mesh
from jax.sharding import PartitionSpec as P

HEADS = 4
HEAD = 256
DOC_LIMIT = 512
EPSILON = 1e-06
ROPE_BASE = 1000000.0
NEG_FILL = -1e30
F32 = jnp.float32
BF16 = jnp.bfloat16
PLANE = ("x", "y")
AXES = ("x", "core", "z", "y")
SWAP = [(0, 1), (1, 0)]


def dot(left, right, dims):
    return lax.dot_general(left, right, (dims, ((), ())), preferred_element_type=F32)


def mm(left, right):
    return dot(left, right, ((1,), (0,)))


def mm_t(left, right):
    return dot(left, right, ((1,), (1,)))


def t_mm(left, right):
    return dot(left, right, ((0,), (0,)))


def inv_rms(values):
    return lax.rsqrt(jnp.mean(values * values, axis=-1, keepdims=True) + EPSILON)


def rms_back(values, gain_vec, d_norm):
    scale = inv_rms(values)
    unit = values * scale
    weighted = d_norm * gain_vec
    d_values = scale * (weighted - unit * jnp.mean(weighted * unit, axis=-1, keepdims=True))
    return d_values, d_norm * unit


def rope_tables(positions):
    half_width = HEAD // 2
    inverse = ROPE_BASE ** (-(jnp.arange(half_width, dtype=F32) * 2.0 / HEAD))
    angles = positions.astype(F32)[..., None] * inverse
    return jnp.cos(angles), jnp.sin(angles)


def rotate(values, cosine, sine):
    half_width = values.shape[-1] // 2
    first, second = values[..., :half_width], values[..., half_width:]
    return jnp.concatenate([first * cosine - second * sine, second * cosine + first * sine], axis=-1)


class Links:
    def __init__(self, mesh):
        self.size = dict(mesh.shape)
        self.pairs_only = self.size["x"] == 2 and self.size["y"] == 2

    def index(self, axis):
        return lax.axis_index(axis)

    def swap(self, array, axis):
        return lax.ppermute(array, axis, SWAP)

    def shift(self, array, step):
        depth = self.size["z"]
        pairs = [(i, i + step) for i in range(depth) if 0 <= i + step < depth]
        return lax.ppermute(array, "z", pairs)

    def turn(self, array, step):
        depth = self.size["z"]
        return lax.ppermute(array, "z", [(i, (i + step) % depth) for i in range(depth)])

    def ordered(self, own, other, axis):
        first = self.index(axis) == 0
        return jnp.where(first, jnp.stack([own, other]), jnp.stack([other, own]))

    def gather_axis(self, array, axis):
        if self.size[axis] == 2:
            return self.ordered(array, self.swap(array, axis), axis)
        return lax.all_gather(array, axis, axis=0)

    def unrolled(self, pieces):
        depth = self.size["z"]
        back = jnp.stack(pieces[::-1] + pieces[::-1])
        return lax.dynamic_slice_in_dim(back, depth - 1 - self.index("z"), depth)

    def gather_z(self, array):
        pieces = [array] + [self.turn(array, k) for k in range(1, self.size["z"])]
        return self.unrolled(pieces)

    def gather_all(self, array):
        along = self.gather_z(array)
        if self.pairs_only:
            half = array.shape[1] // 2 // 128 * 128
            left, right = along[..., :half], along[..., half:]
            left = self.gather_axis(self.gather_axis(left, "x"), "y")
            right = self.gather_axis(self.gather_axis(right, "y"), "x")
            plane = jnp.concatenate([left, jnp.swapaxes(right, 0, 1)], axis=-1)
        else:
            plane = self.gather_axis(self.gather_axis(along, "x"), "y")
        both = self.gather_axis(plane, "core")
        return jnp.transpose(both, (2, 0, 3, 1, 4, 5))

    def gather_cz(self, array):
        depth = self.size["z"]
        own = [array]
        for _ in range(depth - 1):
            own.append(self.turn(own[-1], 1))
        other = [self.swap(piece, "core") for piece in own]
        z, core = self.index("z"), self.index("core")
        out = jnp.zeros((2, depth) + array.shape, array.dtype)
        for k in range(depth):
            place = jnp.remainder(z - k, depth)
            rest = (0,) * array.ndim
            out = lax.dynamic_update_slice(out, own[k][None, None], (core, place) + rest)
            out = lax.dynamic_update_slice(out, other[k][None, None], (1 - core, place) + rest)
        return out

    def sum_halves(self, array, axis, dim):
        if self.size[axis] == 2:
            at = self.index(axis)
            sent = self.swap(lax.dynamic_index_in_dim(array, 1 - at, dim, False), axis)
            kept = lax.dynamic_index_in_dim(array, at, dim, False)
            return (kept.astype(F32) + sent.astype(F32)).astype(array.dtype)
        return lax.psum_scatter(array, axis, scatter_dimension=dim, tiled=False)

    def sum_ring(self, array, dim):
        depth = self.size["z"]
        z = self.index("z")

        def block(k):
            return lax.dynamic_index_in_dim(array, jnp.remainder(z + k, depth), dim, False)

        total = block(depth - 1)
        for k in range(depth - 1):
            moved = self.turn(total, 1)
            total = (moved.astype(F32) + block(2 * depth - 2 - k).astype(F32)).astype(array.dtype)
        return total

    def sum_cz(self, array):
        return self.sum_ring(self.sum_halves(array, "core", 0), 0)

    def sum_all(self, array):
        array = self.sum_halves(array, "core", 1)
        array = self.sum_halves(array, "x", 0)
        return self.sum_halves(self.sum_ring(array, 0), "y", 0)

    def exchange(self, array):
        if self.pairs_only:
            x, y = self.index("x"), self.index("y")
            sent = self.swap(lax.dynamic_index_in_dim(array, 1 - x, 0, False), "x")
            array = self.ordered(lax.dynamic_index_in_dim(array, x, 0, False), sent, "x")
            sent = self.swap(lax.dynamic_index_in_dim(array, 1 - y, 1, False), "y")
            array = self.ordered(lax.dynamic_index_in_dim(array, y, 1, False), sent, "y")
            return jnp.swapaxes(array, 0, 1)
        count = self.size["x"] * self.size["y"]
        flat = array.reshape((count,) + array.shape[2:])
        return lax.all_to_all(flat, PLANE, 0, 0, tiled=True).reshape(array.shape)

    def gather_plane(self, rows):
        if not self.pairs_only:
            return lax.all_gather(rows, PLANE, axis=0, tiled=True)
        half = rows.shape[0] // 2
        upper, lower = rows[:half], rows[half:]
        upper = jnp.concatenate([upper, self.swap(upper, "x")])
        lower = jnp.concatenate([lower, self.swap(lower, "y")])
        return jnp.concatenate([upper, self.swap(upper, "y"), lower, self.swap(lower, "x")])

    def sum_plane(self, rows):
        if not self.pairs_only:
            return lax.psum_scatter(rows, PLANE, scatter_dimension=0, tiled=True).astype(F32)
        part = rows.shape[0] // 8
        at = [rows[k * part : (k + 1) * part] for k in range(8)]
        up = self.swap(rows[2 * part : 4 * part], "y").astype(F32)
        low = self.swap(rows[6 * part :], "x").astype(F32)
        up_far = self.swap((at[1].astype(F32) + up[part:]).astype(BF16), "x")
        low_far = self.swap((at[5].astype(F32) + low[part:]).astype(BF16), "y")
        return jnp.concatenate(
            [
                at[0].astype(F32) + up[:part] + up_far.astype(F32),
                at[4].astype(F32) + low[:part] + low_far.astype(F32),
            ]
        )

    def window(self, array, length):
        z, y, wide = self.index("z"), self.index("y"), self.size["y"]
        span = wide * length
        reach = -(-(DOC_LIMIT - 1) // span)
        base = z * span + y * length
        if wide == 2 and reach == 2:
            first = y == 0
            one = self.shift(array, 1)
            two = self.shift(one, 1)
            near = self.swap(jnp.where(first, array, one), "y")
            far = self.swap(jnp.where(first, one, two), "y")
            cross = jnp.where(first, z * span - length, z * span)
            bases = [base, base - span, base - 2 * span, cross, cross - span]
            return [array, one, two, near, far], bases
        along = lax.all_gather(array, "y", axis=0)
        blocks, bases = [], []
        for k in range(reach + 1):
            moved = along if k == 0 else self.shift(moved, 1)
            blocks += [moved[j] for j in range(wide)]
            bases += [(z - k) * span + j * length for j in range(wide)]
        return blocks, bases

    def window_back(self, terms, length):
        wide = self.size["y"]
        span = wide * length
        reach = -(-(DOC_LIMIT - 1) // span)
        y = self.index("y")

        def send(array, axis, step):
            low = array.astype(BF16)
            moved = self.swap(low, "y") if axis == "y" else self.shift(low, step)
            return moved.astype(F32)

        if wide == 2 and reach == 2:
            first = y == 0
            own, one, two, near, far = terms
            far = send(far, "y", 0)
            near = send(near, "y", 0)
            two = two + jnp.where(first, 0.0, far)
            one = one + jnp.where(first, far, near)
            own = own + jnp.where(first, near, 0.0)
            one = one + send(two, "z", -1)
            return own + send(one, "z", -1)
        total = None
        for k in range(reach, -1, -1):
            level = jnp.stack(terms[k * wide : (k + 1) * wide])
            total = level if total is None else level + send(total, "z", -1)
        return lax.psum_scatter(total.astype(BF16), "y", scatter_dimension=0, tiled=False).astype(F32)


def on_device(
    links,
    tokens,
    segment_ids,
    w_query,
    w_key,
    w_value,
    w_out,
    w_gate,
    w_up,
    w_down,
    g_in,
    g_post_attn,
    g_pre_ffn,
    g_post_ffn,
    g_query,
    g_key,
    cotangent,
):
    rows, length, width = tokens.shape
    count = rows * length
    size = links.size
    sx, sc, sz, sy = (size[axis] for axis in AXES)
    parts = sx * sc * sz * sy
    score_scale = HEAD ** (-0.5)
    shard = w_gate.shape[0]
    hidden_shard = w_down.shape[0]
    hidden_own = sc * sz * hidden_shard
    head_shard = g_query.shape[0]
    qkv = HEADS * HEAD + 2 * HEAD

    seg_blocks, bases = links.window(segment_ids, length)
    seg_window = jnp.concatenate(seg_blocks, axis=1)
    pos_window = jnp.concatenate([base + jnp.arange(length, dtype=jnp.int32) for base in bases])
    pos_own = bases[0] + jnp.arange(length, dtype=jnp.int32) if size["y"] == 2 else (
        links.index("z") * sy * length + links.index("y") * length + jnp.arange(length, dtype=jnp.int32)
    )
    same = (segment_ids[:, :, None] == seg_window[:, None, :]) & (pos_window >= 0)[None, None, :]
    allowed = same & (pos_window[None, None, :] <= pos_own[None, :, None])
    positions = jnp.sum(allowed.astype(jnp.int32), axis=2) - 1
    cosine, sine = rope_tables(positions.reshape(count))

    gains_low = jnp.concatenate([g_in, g_post_attn, g_pre_ffn, g_post_ffn, g_query, g_key]).astype(BF16)
    packed = -(-gains_low.shape[0] // 256) * 256
    gains_low = jnp.pad(gains_low, (0, packed - gains_low.shape[0]))[None]
    gains = links.gather_all(gains_low).reshape(parts, packed)
    gain_in, gain_post_attn, gain_pre_ffn, gain_post_ffn = (
        gains[:, k * shard : (k + 1) * shard].reshape(1, width).astype(F32) for k in range(4)
    )
    gain_query, gain_key = (
        gains[:, 4 * shard + k * head_shard : 4 * shard + (k + 1) * head_shard].reshape(1, HEAD).astype(F32)
        for k in range(2)
    )
    kv_shard = jnp.concatenate([w_key.astype(BF16), w_value.astype(BF16)], axis=1)
    full_kv = links.gather_all(kv_shard).reshape(width, 2 * HEAD)
    full_query = links.gather_all(w_query.astype(BF16)).reshape(width, HEADS * HEAD)
    full_out = links.gather_all(w_out.astype(BF16)).reshape(HEADS * HEAD, width)
    full_down = links.gather_cz(w_down.astype(BF16)).reshape(hidden_own, width)

    def columns(weight):
        split = weight.astype(BF16).reshape(shard, sx, sc, sz, sy, hidden_shard)
        return jnp.transpose(split, (1, 4, 0, 2, 3, 5)).reshape(sx, sy, shard, hidden_own)

    def whole_columns(pieces):
        gathered = links.gather_cz(pieces.reshape(sx, sy * shard, hidden_own))
        return jnp.transpose(gathered, (2, 0, 1, 3, 4)).reshape(width, hidden_own)

    full_gate = whole_columns(links.exchange(columns(w_gate)))
    full_up = whole_columns(links.exchange(columns(w_up)))

    inputs_f = tokens.astype(F32).reshape(count, width)
    h_in = (inputs_f * inv_rms(inputs_f) * gain_in).astype(BF16)
    kv_proj = mm(h_in, full_kv)
    k_proj = kv_proj[:, :HEAD]
    value_low = kv_proj[:, HEAD:].astype(BF16)
    key_low = rotate(k_proj * inv_rms(k_proj) * gain_key, cosine, sine).astype(BF16)
    kv_low = jnp.concatenate([key_low, value_low], axis=1).reshape(rows, length, 2 * HEAD)
    kv_window = jnp.concatenate(links.window(kv_low, length)[0], axis=1)
    q_proj = mm(h_in, full_query).reshape(count, HEADS, HEAD)
    query_low = rotate(
        q_proj * inv_rms(q_proj) * gain_query, cosine[:, None, :], sine[:, None, :]
    ).astype(BF16).reshape(rows, length, HEADS, HEAD)
    keys, values = kv_window[..., :HEAD], kv_window[..., HEAD:]
    raw = jnp.einsum("rchd,rkd->rhck", query_low, keys, preferred_element_type=F32) * score_scale
    scores = jnp.where(allowed[:, None], raw, NEG_FILL)
    top = jnp.max(scores, axis=-1, keepdims=True)
    powers = jnp.exp(scores - top)
    probs = powers / jnp.sum(powers, axis=-1, keepdims=True)
    probs_low = probs.astype(BF16)
    mixed = jnp.einsum("rhck,rkd->rchd", probs_low, values, preferred_element_type=F32).astype(BF16)
    mixed_flat = mixed.reshape(count, HEADS * HEAD)
    attn_out = mm(mixed_flat, full_out)
    residual = inputs_f + attn_out * inv_rms(attn_out) * gain_post_attn
    h_ffn = (residual * inv_rms(residual) * gain_pre_ffn).astype(BF16)

    h_all = links.gather_plane(h_ffn)
    gate = mm(h_all, full_gate)
    up = mm(h_all, full_up)
    slope = math.sqrt(2.0 / math.pi)
    bent = jnp.tanh(slope * (gate + 0.044715 * gate * gate * gate))
    act = 0.5 * gate * (1.0 + bent)
    d_act = 0.5 * (1.0 + bent) + 0.5 * gate * (1.0 - bent * bent) * slope * (1.0 + 3 * 0.044715 * gate * gate)
    hidden = (act * up).astype(BF16)
    act_low = act.astype(BF16)
    turn_low = (up * d_act).astype(BF16)
    ffn = links.sum_plane(mm(hidden, full_down).astype(BF16))
    output = (residual + ffn * inv_rms(ffn) * gain_post_ffn).astype(BF16).reshape(tokens.shape)

    d_final = cotangent.astype(F32).reshape(count, width)
    d_ffn_f, post_ffn_terms = rms_back(ffn, gain_post_ffn, d_final)
    d_all = links.gather_plane(d_ffn_f.astype(BF16))
    d_hidden = mm_t(d_all, full_down)
    d_gate = (d_hidden * turn_low.astype(F32)).astype(BF16)
    d_up = (d_hidden * act_low.astype(F32)).astype(BF16)
    d_hffn = links.sum_plane((mm_t(d_gate, full_gate) + mm_t(d_up, full_up)).astype(BF16))

    def by_owner(grad):
        split = grad.astype(BF16).reshape(sx, sc, sz, sy * shard, hidden_own)
        return links.sum_cz(jnp.transpose(split, (1, 2, 0, 3, 4)))

    def own_rows(sums):
        got = links.exchange(sums.reshape(sx, sy, shard, hidden_own))
        got = got.reshape(sx, sy, shard, sc, sz, hidden_shard)
        return jnp.transpose(got, (2, 0, 3, 4, 1, 5)).reshape(shard, parts * hidden_shard).astype(F32)

    grad_down = links.sum_cz(t_mm(hidden, d_all).astype(BF16).reshape(sc, sz, hidden_shard, width)).astype(F32)
    grad_gate = own_rows(by_owner(t_mm(h_all, d_gate)))
    grad_up = own_rows(by_owner(t_mm(h_all, d_up)))

    d_normed, pre_ffn_terms = rms_back(residual, gain_pre_ffn, d_hffn)
    d_residual = d_final + d_normed
    d_attn_f, post_attn_terms = rms_back(attn_out, gain_post_attn, d_residual)
    d_attn = d_attn_f.astype(BF16)

    def summed(grad):
        split = grad.astype(BF16).reshape(sx, sc, sz, sy, -1, grad.shape[1])
        return links.sum_all(split).astype(F32)

    grad_out = summed(t_mm(mixed_flat, d_attn))
    d_mixed = mm_t(d_attn, full_out).astype(BF16).reshape(rows, length, HEADS, HEAD)
    d_probs = jnp.einsum("rchd,rkd->rhck", d_mixed, values, preferred_element_type=F32)
    d_scores = (probs * (d_probs - jnp.sum(d_probs * probs, axis=-1, keepdims=True))).astype(BF16)
    d_query = jnp.einsum("rhck,rkd->rchd", d_scores, keys, preferred_element_type=F32) * score_scale
    key_terms = jnp.einsum("rhck,rchd->rkd", d_scores, query_low, preferred_element_type=F32) * score_scale
    value_terms = jnp.einsum("rhck,rchd->rkd", probs_low, d_mixed, preferred_element_type=F32)
    terms = jnp.concatenate([key_terms, value_terms], axis=-1)
    d_kv = links.window_back(
        [terms[:, k * length : (k + 1) * length] for k in range(terms.shape[1] // length)], length
    ).reshape(count, 2 * HEAD)
    d_value = d_kv[:, HEAD:].astype(BF16)
    d_qproj_f, query_norm_terms = rms_back(
        q_proj, gain_query, rotate(d_query.reshape(count, HEADS, HEAD), cosine[:, None, :], -sine[:, None, :])
    )
    d_kproj_f, key_norm_terms = rms_back(k_proj, gain_key, rotate(d_kv[:, :HEAD], cosine, -sine))
    d_qkv = jnp.concatenate(
        [d_qproj_f.reshape(count, HEADS * HEAD).astype(BF16), d_kproj_f.astype(BF16), d_value], axis=1
    )
    grad_qkv = summed(t_mm(h_in, d_qkv))
    d_hin = mm_t(d_qkv[:, : HEADS * HEAD], full_query) + mm_t(d_qkv[:, HEADS * HEAD :], full_kv)
    d_inputs, in_terms = rms_back(inputs_f, gain_in, d_hin)
    grad_tokens = (d_residual + d_inputs).astype(BF16).reshape(tokens.shape)

    gain_grads = [
        jnp.sum(terms, axis=0).reshape(parts, shard)
        for terms in (in_terms, post_attn_terms, pre_ffn_terms, post_ffn_terms)
    ] + [
        jnp.sum(query_norm_terms, axis=(0, 1)).reshape(parts, head_shard),
        jnp.sum(key_norm_terms, axis=0).reshape(parts, head_shard),
    ]
    gain_grads = jnp.concatenate(gain_grads, axis=1)
    gain_grads = jnp.pad(gain_grads, ((0, 0), (0, packed - gain_grads.shape[1])))
    own = links.sum_all(gain_grads.reshape(sx, sc, sz, sy, 1, packed))[0]
    gain_out = [own[k * shard : (k + 1) * shard] for k in range(4)]
    gain_out += [own[4 * shard + k * head_shard : 4 * shard + (k + 1) * head_shard] for k in range(2)]
    return (
        output,
        grad_tokens,
        grad_qkv[:, : HEADS * HEAD],
        grad_qkv[:, HEADS * HEAD : HEADS * HEAD + HEAD],
        grad_qkv[:, HEADS * HEAD + HEAD :],
        grad_out,
        grad_gate,
        grad_up,
        grad_down,
        *gain_out,
    )


def solution(mesh):
    plane = mesh.shape["dp"] // 2
    by_chip = Mesh(mesh.devices.reshape(plane, 2, -1, plane), AXES)
    links = Links(by_chip)
    placed = P(("x", "core"), ("z", "y"), None)
    matrix = P(AXES, None)
    vector = P(AXES)
    in_specs = (placed, P(("x", "core"), ("z", "y"))) + (matrix,) * 7 + (vector,) * 6 + (placed,)
    out_specs = (placed, placed) + (matrix,) * 7 + (vector,) * 6

    def step(*arguments):
        return on_device(links, *arguments)

    return jax.shard_map(step, mesh=by_chip, in_specs=in_specs, out_specs=out_specs, check_vma=False)
```

```python
import functools
import math

import jax
import jax.numpy as jnp
from jax import lax
from jax.experimental import pallas as pl
from jax.experimental.pallas import tpu as pltpu
from jax.sharding import Mesh
from jax.sharding import PartitionSpec as P

HEADS = 4
HEAD = 256
HALF = HEAD // 2
DOC_LIMIT = 512
EPSILON = 1e-06
ROPE_BASE = 1000000.0
NEG_FILL = -1e30
SCORE_SCALE = HEAD ** (-0.5)
SLOPE = math.sqrt(2.0 / math.pi)
F32 = jnp.float32
BF16 = jnp.bfloat16
PLANE = ("x", "y")
AXES = ("x", "core", "z", "y")
SWAP = [(0, 1), (1, 0)]
IN, POST_ATTN, PRE_FFN, POST_FFN = range(4)
SMALL = 128
ROOM = 58 << 20


def dot(left, right, dims):
    return lax.dot_general(left, right, (dims, ((), ())), preferred_element_type=F32)


def mm(left, right):
    return dot(left, right, ((1,), (0,)))


def mm_t(left, right):
    return dot(left, right, ((1,), (1,)))


def t_mm(left, right):
    return dot(left, right, ((0,), (0,)))


def inv_rms(values):
    return lax.rsqrt(jnp.mean(values * values, axis=-1, keepdims=True) + EPSILON)


def rms_back(values, gain_vec, d_norm):
    scale = inv_rms(values)
    unit = values * scale
    weighted = d_norm * gain_vec
    d_values = scale * (weighted - unit * jnp.mean(weighted * unit, axis=-1, keepdims=True))
    return d_values, d_norm * unit


def rope_tables(positions):
    inverse = ROPE_BASE ** (-(jnp.arange(HALF, dtype=F32) * 2.0 / HEAD))
    angles = positions.astype(F32)[..., None] * inverse
    return jnp.cos(angles), jnp.sin(angles)


def rotate(values, cosine, sine):
    first, second = values[:, :HALF], values[:, HALF:]
    return jnp.concatenate([first * cosine - second * sine, second * cosine + first * sine], axis=-1)


def column_sum(terms):
    return jnp.sum(terms, axis=0, keepdims=True)


def call(body, grid, in_specs, out_specs, out_shape, flops, scratch=()):
    moved = sum(math.prod(one.shape) * one.dtype.itemsize for one in jax.tree.leaves(out_shape))
    return pl.pallas_call(
        body,
        grid=grid,
        in_specs=in_specs,
        out_specs=out_specs,
        out_shape=out_shape,
        scratch_shapes=list(scratch),
        compiler_params=pltpu.CompilerParams(vmem_limit_bytes=ROOM),
        cost_estimate=pl.CostEstimate(flops=flops, bytes_accessed=2 * moved, transcendentals=0),
    )


def shaped(*shape, dtype=F32):
    return jax.ShapeDtypeStruct(shape, dtype)


def whole(*shape):
    return pl.BlockSpec(shape, lambda i: (0,) * len(shape))


def rows_of(tile, width):
    return pl.BlockSpec((tile, width), lambda i: (i, 0))


def row_block(*shape):
    return pl.BlockSpec((1,) + shape, lambda i: (i,) + (0,) * len(shape))


def kv_body(tok_ref, wkv_ref, gains_ref, head_ref, cos_ref, sin_ref, h_ref, kproj_ref, kv_ref):
    tokens = tok_ref[...].astype(F32)
    h = (tokens * inv_rms(tokens) * gains_ref[IN : IN + 1]).astype(BF16)
    h_ref[...] = h
    proj = mm(h, wkv_ref[...])
    k_proj = proj[:, :HEAD]
    kproj_ref[...] = k_proj
    key = rotate(k_proj * inv_rms(k_proj) * head_ref[1:2], cos_ref[...], sin_ref[...])
    kv_ref[0, :, :HEAD] = key.astype(BF16)
    kv_ref[0, :, HEAD:] = proj[:, HEAD:].astype(BF16)


def kv_step(rows, length, tokens, wkv, gains, heads, cosine, sine):
    count, width = tokens.shape
    return call(
        kv_body,
        (rows,),
        [rows_of(length, width), whole(*wkv.shape), whole(*gains.shape), whole(*heads.shape)]
        + [rows_of(length, HALF)] * 2,
        [rows_of(length, width), rows_of(length, HEAD), row_block(length, 2 * HEAD)],
        [shaped(count, width, dtype=BF16), shaped(count, HEAD), shaped(rows, length, 2 * HEAD, dtype=BF16)],
        2 * count * width * 2 * HEAD,
    )(tokens, wkv, gains, heads, cosine, sine)


def by_head(array):
    return jnp.concatenate([array[:, h * HEAD : (h + 1) * HEAD] for h in range(HEADS)], axis=0)


def by_lane(array):
    part = array.shape[0] // HEADS
    return jnp.concatenate([array[h * part : (h + 1) * part] for h in range(HEADS)], axis=1)


def probs_of(query, keys, segq_ref, posq_ref, segk_ref, posk_ref):
    allowed = (segq_ref[...] == segk_ref[0]) & (posk_ref[...] <= posq_ref[...])
    allowed = jnp.concatenate([allowed.astype(F32)] * HEADS, axis=0) > 0.5
    scores = jnp.where(allowed, mm_t(query, keys) * SCORE_SCALE, NEG_FILL)
    powers = jnp.exp(scores - jnp.max(scores, axis=-1, keepdims=True))
    return powers / jnp.sum(powers, axis=-1, keepdims=True)


def attend_body(blocks, *refs):
    (h_ref, tok_ref, wq_ref, wo_ref, gains_ref, head_ref, cos_ref, sin_ref) = refs[:8]
    masks, kv_refs = refs[8:12], refs[12 : 12 + blocks]
    qproj_ref, query_ref, mixed_ref, attn_ref, resid_ref, hffn_ref = refs[12 + blocks :]
    proj = mm(h_ref[...], wq_ref[...])
    qproj_ref[...] = proj
    cosine, sine = cos_ref[...], sin_ref[...]
    query = []
    for h in range(HEADS):
        one = proj[:, h * HEAD : (h + 1) * HEAD]
        query.append(rotate(one * inv_rms(one) * head_ref[0:1], cosine, sine).astype(BF16))
    query_ref[...] = jnp.concatenate(query, axis=1)
    keys = jnp.concatenate([one[0, :, :HEAD] for one in kv_refs], axis=0)
    values = jnp.concatenate([one[0, :, HEAD:] for one in kv_refs], axis=0)
    probs = probs_of(jnp.concatenate(query, axis=0), keys, *masks).astype(BF16)
    mixed = by_lane(mm(probs, values).astype(BF16))
    mixed_ref[...] = mixed
    attn = mm(mixed, wo_ref[...])
    attn_ref[...] = attn
    resid = tok_ref[...].astype(F32) + attn * inv_rms(attn) * gains_ref[POST_ATTN : POST_ATTN + 1]
    resid_ref[...] = resid
    hffn_ref[...] = (resid * inv_rms(resid) * gains_ref[PRE_FFN : PRE_FFN + 1]).astype(BF16)


def mask_specs(length, window):
    return [rows_of(length, 1), whole(length, 1), row_block(1, window), whole(1, window)]


def attend(rows, length, h, tokens, wq, wo, gains, heads, cosine, sine, masks, kv):
    count, width = tokens.shape
    wide = HEADS * HEAD
    window = len(kv) * length
    return call(
        functools.partial(attend_body, len(kv)),
        (rows,),
        [rows_of(length, width)] * 2
        + [whole(*one.shape) for one in (wq, wo, gains, heads)]
        + [rows_of(length, HALF)] * 2
        + mask_specs(length, window)
        + [row_block(length, 2 * HEAD)] * len(kv),
        [rows_of(length, wide)] * 3 + [rows_of(length, width)] * 3,
        [
            shaped(count, wide),
            shaped(count, wide, dtype=BF16),
            shaped(count, wide, dtype=BF16),
            shaped(count, width),
            shaped(count, width),
            shaped(count, width, dtype=BF16),
        ],
        4 * count * wide * (width + window),
    )(h, tokens, wq, wo, gains, heads, cosine, sine, *masks, *kv)


def attend_back_body(blocks, *refs):
    (dh_ref, cot_ref, resid_ref, attn_ref, qproj_ref, query_ref, wo_ref, gains_ref, head_ref, cos_ref, sin_ref) = refs[:11]
    masks, kv_refs = refs[11:15], refs[15 : 15 + blocks]
    dres_ref, dattn_ref, dq_ref, sums_ref, head_sums_ref = refs[15 + blocks : 20 + blocks]
    term_refs = refs[20 + blocks :]
    d_norm, pre_terms = rms_back(resid_ref[...], gains_ref[PRE_FFN : PRE_FFN + 1], dh_ref[...])
    d_res = cot_ref[...].astype(F32) + d_norm
    dres_ref[...] = d_res
    d_attn, post_terms = rms_back(attn_ref[...], gains_ref[POST_ATTN : POST_ATTN + 1], d_res)
    d_attn = d_attn.astype(BF16)
    dattn_ref[...] = d_attn
    d_mixed = by_head(mm_t(d_attn, wo_ref[...]).astype(BF16))
    query = by_head(query_ref[...])
    keys = jnp.concatenate([one[0, :, :HEAD] for one in kv_refs], axis=0)
    values = jnp.concatenate([one[0, :, HEAD:] for one in kv_refs], axis=0)
    probs = probs_of(query, keys, *masks)
    d_probs = mm_t(d_mixed, values)
    d_scores = (probs * (d_probs - jnp.sum(d_probs * probs, axis=-1, keepdims=True))).astype(BF16)
    key_terms = t_mm(d_scores, query) * SCORE_SCALE
    value_terms = t_mm(probs.astype(BF16), d_mixed)
    length = query_ref.shape[0]
    for k, ref in enumerate(term_refs):
        at = slice(k * length, (k + 1) * length)
        ref[0, :, :HEAD] = key_terms[at].astype(ref.dtype)
        ref[0, :, HEAD:] = value_terms[at].astype(ref.dtype)
    d_query = mm(d_scores, keys) * SCORE_SCALE
    cosine, sine = cos_ref[...], -sin_ref[...]
    head_sum = jnp.zeros((1, HEAD), F32)
    for h in range(HEADS):
        turned = rotate(d_query[h * length : (h + 1) * length], cosine, sine)
        lanes = slice(h * HEAD, (h + 1) * HEAD)
        d_proj, terms = rms_back(qproj_ref[:, lanes], head_ref[0:1], turned)
        dq_ref[:, lanes] = d_proj.astype(BF16)
        head_sum += column_sum(terms)

    @pl.when(pl.program_id(0) == 0)
    def _():
        sums_ref[...] = jnp.zeros_like(sums_ref)
        head_sums_ref[...] = jnp.zeros_like(head_sums_ref)

    sums_ref[POST_ATTN : POST_ATTN + 1] += column_sum(post_terms)
    sums_ref[PRE_FFN : PRE_FFN + 1] += column_sum(pre_terms)
    head_sums_ref[0:1] += head_sum


def attend_back(rows, length, dh, cot, resid, attn, qproj, query, wo, gains, heads, cosine, sine, masks, kv, kinds):
    count, width = dh.shape
    wide = HEADS * HEAD
    window = len(kv) * length
    return call(
        functools.partial(attend_back_body, len(kv)),
        (rows,),
        [rows_of(length, width)] * 4
        + [rows_of(length, wide)] * 2
        + [whole(*one.shape) for one in (wo, gains, heads)]
        + [rows_of(length, HALF)] * 2
        + mask_specs(length, window)
        + [row_block(length, 2 * HEAD)] * len(kv),
        [rows_of(length, width)] * 2
        + [rows_of(length, wide), whole(8, width), whole(8, HEAD)]
        + [row_block(length, 2 * HEAD)] * len(kv),
        [
            shaped(count, width),
            shaped(count, width, dtype=BF16),
            shaped(count, wide, dtype=BF16),
            shaped(8, width),
            shaped(8, HEAD),
        ]
        + [shaped(rows, length, 2 * HEAD, dtype=kind) for kind in kinds],
        2 * count * wide * (width + 5 * window),
    )(dh, cot, resid, attn, qproj, query, wo, gains, heads, cosine, sine, *masks, *kv)


def finish_body(dkv_ref, kproj_ref, dq_ref, tok_ref, dres_ref, wq_ref, wkv_ref, gains_ref, head_ref, cos_ref, sin_ref,
                dkvp_ref, grad_ref, sums_ref, head_sums_ref):
    d_kv = dkv_ref[0]
    turned = rotate(d_kv[:, :HEAD], cos_ref[...], -sin_ref[...])
    d_key, key_terms = rms_back(kproj_ref[...], head_ref[1:2], turned)
    d_proj = jnp.concatenate([d_key.astype(BF16), d_kv[:, HEAD:].astype(BF16)], axis=1)
    dkvp_ref[...] = d_proj
    d_hin = mm_t(dq_ref[...], wq_ref[...]) + mm_t(d_proj, wkv_ref[...])
    d_tokens, in_terms = rms_back(tok_ref[...].astype(F32), gains_ref[IN : IN + 1], d_hin)
    grad_ref[...] = (dres_ref[...] + d_tokens).astype(BF16)

    @pl.when(pl.program_id(0) == 0)
    def _():
        sums_ref[...] = jnp.zeros_like(sums_ref)
        head_sums_ref[...] = jnp.zeros_like(head_sums_ref)

    sums_ref[IN : IN + 1] += column_sum(in_terms)
    head_sums_ref[1:2] += column_sum(key_terms)


def finish(rows, length, dkv, kproj, dq, tokens, dres, wq, wkv, gains, heads, cosine, sine):
    count, width = tokens.shape
    wide = HEADS * HEAD
    return call(
        finish_body,
        (rows,),
        [row_block(length, 2 * HEAD), rows_of(length, HEAD), rows_of(length, wide)]
        + [rows_of(length, width)] * 2
        + [whole(*one.shape) for one in (wq, wkv, gains, heads)]
        + [rows_of(length, HALF)] * 2,
        [rows_of(length, 2 * HEAD), rows_of(length, width), whole(8, width), whole(8, HEAD)],
        [shaped(count, 2 * HEAD, dtype=BF16), shaped(count, width, dtype=BF16), shaped(8, width), shaped(8, HEAD)],
        2 * count * width * (wide + 2 * HEAD),
    )(dkv, kproj, dq, tokens, dres, wq, wkv, gains, heads, cosine, sine)


def pieces_of(total, step):
    return [(k, min(step, total - k)) for k in range(0, total, step)]


def up_body(step, h_ref, pair_ref, down_ref, hidden_ref, turn_ref, act_ref, out_ref):
    h = h_ref[...]
    for at, wide in pieces_of(hidden_ref.shape[1], step):
        cols = pl.ds(at, wide)
        gate = mm(h, pair_ref[0, :, cols])
        up = mm(h, pair_ref[1, :, cols])
        square = gate * gate
        bent = jnp.tanh(gate * (SLOPE + SLOPE * 0.044715 * square))
        half = 0.5 + 0.5 * bent
        act = gate * half
        d_act = half + 0.5 * gate * (1.0 - bent * bent) * (SLOPE + 3 * SLOPE * 0.044715 * square)
        hidden_ref[:, cols] = (act * up).astype(BF16)
        turn_ref[:, cols] = (up * d_act).astype(BF16)
        act_ref[:, cols] = act.astype(BF16)
    out_ref[...] = mm(hidden_ref[...], down_ref[...]).astype(BF16)


def ffn_forward(h, pair, down, tile=256, step=256):
    count, width = h.shape
    units = pair.shape[2]
    return call(
        functools.partial(up_body, step),
        (count // tile,),
        [rows_of(tile, width), whole(2, width, units), whole(units, width)],
        [rows_of(tile, units)] * 3 + [rows_of(tile, width)],
        [shaped(count, units, dtype=BF16)] * 3 + [shaped(count, width, dtype=BF16)],
        6 * count * width * units,
    )(h, pair, down)


def down_body(step, d_ref, turn_ref, act_ref, pair_ref, down_ref, pair_out, out_ref):
    d = d_ref[...]
    for at, wide in pieces_of(turn_ref.shape[1], step):
        cols = pl.ds(at, wide)
        d_hidden = mm_t(d, down_ref[cols, :])
        pair_out[0, :, cols] = (d_hidden * turn_ref[:, cols].astype(F32)).astype(BF16)
        pair_out[1, :, cols] = (d_hidden * act_ref[:, cols].astype(F32)).astype(BF16)
    out_ref[...] = (mm_t(pair_out[0], pair_ref[0]) + mm_t(pair_out[1], pair_ref[1])).astype(BF16)


def ffn_backward(d, turn, act, pair, down, tile=256, step=256):
    count, width = d.shape
    units = pair.shape[2]
    return call(
        functools.partial(down_body, step),
        (count // tile,),
        [rows_of(tile, width), rows_of(tile, units), rows_of(tile, units), whole(2, width, units), whole(units, width)],
        [pl.BlockSpec((2, tile, units), lambda i: (0, i, 0)), rows_of(tile, width)],
        [shaped(2, count, units, dtype=BF16), shaped(count, width, dtype=BF16)],
        6 * count * width * units,
    )(d, turn, act, pair, down)


def grads_body(left_ref, right_ref, out_ref):
    out_ref[0] = t_mm(left_ref[...], right_ref[0]).astype(BF16)


def weight_grads(left, right, tile):
    count, rows = left.shape
    many, _, cols = right.shape
    return call(
        grads_body,
        (many, rows // tile),
        [
            pl.BlockSpec((count, tile), lambda k, i: (0, i)),
            pl.BlockSpec((1, count, cols), lambda k, i: (k, 0, 0)),
        ],
        pl.BlockSpec((1, tile, cols), lambda k, i: (k, i, 0)),
        shaped(many, rows, cols, dtype=BF16),
        2 * many * count * rows * cols,
    )(left, right)


def middle_body(ffn_ref, resid_ref, cot_ref, gains_ref, out_ref, dffn_ref, sums_ref):
    ffn = ffn_ref[...]
    gain = gains_ref[POST_FFN : POST_FFN + 1]
    out_ref[...] = (resid_ref[...] + ffn * inv_rms(ffn) * gain).astype(BF16)
    d_ffn, terms = rms_back(ffn, gain, cot_ref[...].astype(F32))
    dffn_ref[...] = d_ffn.astype(BF16)

    @pl.when(pl.program_id(0) == 0)
    def _():
        sums_ref[...] = jnp.zeros_like(sums_ref)

    sums_ref[POST_FFN : POST_FFN + 1] += column_sum(terms)


def middle(rows, length, ffn, resid, cot, gains):
    count, width = ffn.shape
    return call(
        middle_body,
        (rows,),
        [rows_of(length, width)] * 3 + [whole(*gains.shape)],
        [rows_of(length, width)] * 2 + [whole(8, width)],
        [shaped(count, width, dtype=BF16), shaped(count, width, dtype=BF16), shaped(8, width)],
        20 * count * width,
    )(ffn, resid, cot, gains)


def place_body(links, shard, parts, own_ref, other_ref, *refs):
    outs, scratch = refs[:-1], refs[-1]
    depth = links.size["z"]
    at_x, at_c, at_z, at_y = (links.index(axis) for axis in AXES)
    total = scratch.shape[0]
    number = 0
    for x in range(2):
        for core in range(2):
            for z in range(depth):
                for y in range(2):
                    slot = jnp.abs(at_x - x) + 2 * jnp.abs(at_y - y)
                    slot = slot * depth + jnp.remainder(at_z - z + depth, depth)
                    mine = own_ref[slot].astype(F32)
                    theirs = other_ref[slot].astype(F32)
                    piece = jnp.where(at_c == core, mine, theirs)
                    scratch[number] = piece
                    number += 1
    for (first, count, lanes), out in zip(parts, outs, strict=True):
        for k in range(number):
            out[k * count : (k + 1) * count, :] = scratch[k, first : first + count, :lanes].astype(out.dtype)


def placed(links, own, other, parts):
    slots, rows, lanes = own.shape
    number = 2 * slots
    return pl.pallas_call(
        functools.partial(place_body, links, rows, parts),
        out_shape=[shaped(number * count, wide, dtype=BF16) for _, count, wide in parts],
        scratch_shapes=[pltpu.VMEM((number, rows, lanes), F32)],
        compiler_params=pltpu.CompilerParams(vmem_limit_bytes=ROOM),
    )(own, other)


class Links:
    def __init__(self, mesh):
        self.size = dict(mesh.shape)
        self.pairs_only = self.size["x"] == 2 and self.size["y"] == 2

    def index(self, axis):
        return lax.axis_index(axis)

    def swap(self, array, axis):
        return lax.ppermute(array, axis, SWAP)

    def shift(self, array, step):
        depth = self.size["z"]
        pairs = [(i, i + step) for i in range(depth) if 0 <= i + step < depth]
        return lax.ppermute(array, "z", pairs)

    def turn(self, array, step):
        depth = self.size["z"]
        return lax.ppermute(array, "z", [(i, (i + step) % depth) for i in range(depth)])

    def ordered(self, own, other, axis):
        first = self.index(axis) == 0
        return jnp.where(first, jnp.stack([own, other]), jnp.stack([other, own]))

    def gather_all(self, array, parts):
        depth = self.size["z"]
        along = jnp.stack([array] + [self.turn(array, k) for k in range(1, depth)])
        if self.pairs_only:
            across = lax.ppermute(along, PLANE, [(k, 3 - k) for k in range(4)])
            own = jnp.concatenate([along, self.swap(along, "x"), self.swap(along, "y"), across])
            return placed(self, own, self.swap(own, "core"), parts)
        full = lax.all_gather(array, AXES, axis=0)
        return [full[:, at : at + count, :lanes].reshape(-1, lanes) for at, count, lanes in parts]

    def gather_cz(self, array, dim):
        return lax.all_gather(array, ("core", "z"), axis=dim, tiled=True)

    def sum_halves(self, array, axis, dim):
        if self.size[axis] == 2:
            at = self.index(axis)
            sent = self.swap(lax.dynamic_index_in_dim(array, 1 - at, dim, False), axis)
            kept = lax.dynamic_index_in_dim(array, at, dim, False)
            return (kept.astype(F32) + sent.astype(F32)).astype(array.dtype)
        return lax.psum_scatter(array, axis, scatter_dimension=dim, tiled=False)

    def sum_z(self, array, dim):
        depth = self.size["z"]
        z = self.index("z")

        def block(k):
            return lax.dynamic_index_in_dim(array, jnp.remainder(z + k, depth), dim, False)

        total = block(0).astype(F32)
        for k in range(1, depth):
            total = total + self.turn(block(k), k).astype(F32)
        return total

    def sum_cz(self, array):
        mine = jnp.swapaxes(self.sum_halves(array, "core", 1), 0, 1)
        return lax.psum_scatter(mine.reshape(-1, array.shape[-1]), "z", scatter_dimension=0, tiled=True)

    def sum_all(self, array):
        array = self.sum_halves(array, "core", 1)
        array = self.sum_halves(array, "x", 0)
        return self.sum_halves(self.sum_z(array, 0).astype(BF16), "y", 0).astype(F32)

    def sum_all_small(self, array):
        array = self.sum_halves(array, "core", 1)
        sent = array.reshape((-1,) + array.shape[3:])
        got = lax.all_to_all(sent, ("x", "z", "y"), 0, 0, tiled=True)
        return jnp.sum(got.astype(F32), axis=0)

    def exchange(self, array):
        count = self.size["x"] * self.size["y"]
        flat = array.reshape((count,) + array.shape[2:])
        return lax.all_to_all(flat, PLANE, 0, 0, tiled=True).reshape(array.shape)

    def gather_plane(self, rows):
        if not self.pairs_only:
            return lax.all_gather(rows, PLANE, axis=0, tiled=True)
        half = rows.shape[0] // 2
        upper, lower = lax.optimization_barrier((rows[:half], rows[half:]))
        near = lax.optimization_barrier((self.swap(upper, "x"), self.swap(lower, "y")))
        upper = jnp.concatenate([upper, near[0]])
        lower = jnp.concatenate([lower, near[1]])
        upper, lower = lax.optimization_barrier((upper, lower))
        far = lax.optimization_barrier((self.swap(upper, "y"), self.swap(lower, "x")))
        return jnp.concatenate([upper, far[0], lower, far[1]])

    def sum_plane(self, rows):
        if not self.pairs_only:
            return lax.psum_scatter(rows, PLANE, scatter_dimension=0, tiled=True).astype(F32)
        part = rows.shape[0] // 8
        at = [rows[k * part : (k + 1) * part] for k in range(8)]
        up, low = lax.optimization_barrier((self.swap(rows[2 * part : 4 * part], "y"), self.swap(rows[6 * part :], "x")))
        up_far = (at[1].astype(F32) + up[part:].astype(F32)).astype(BF16)
        low_far = (at[5].astype(F32) + low[part:].astype(F32)).astype(BF16)
        up_far, low_far = lax.optimization_barrier((up_far, low_far))
        up_far, low_far = lax.optimization_barrier((self.swap(up_far, "x"), self.swap(low_far, "y")))
        return jnp.concatenate(
            [
                at[0].astype(F32) + up[:part].astype(F32) + up_far.astype(F32),
                at[4].astype(F32) + low[:part].astype(F32) + low_far.astype(F32),
            ]
        )

    def window_bases(self, length):
        z, y, wide = self.index("z"), self.index("y"), self.size["y"]
        span = wide * length
        reach = -(-(DOC_LIMIT - 1) // span)
        base = z * span + y * length
        if wide == 2 and reach == 2:
            cross = jnp.where(y == 0, z * span - length, z * span)
            return [base, base - span, base - 2 * span, cross, cross - span]
        return [(z - k) * span + j * length for k in range(reach + 1) for j in range(wide)]

    def window(self, array, length):
        wide = self.size["y"]
        reach = -(-(DOC_LIMIT - 1) // (wide * length))
        if wide == 2 and reach == 2:
            first = self.index("y") == 0
            one = self.shift(array, 1)
            two = self.shift(one, 1)
            near = self.swap(jnp.where(first, array, one), "y")
            far = self.swap(jnp.where(first, one, two), "y")
            return [array, one, two, near, far]
        along = [lax.all_gather(array, "y", axis=0)]
        for _ in range(reach):
            along.append(self.shift(along[-1], 1))
        return [level[j] for level in along for j in range(wide)]

    def window_kinds(self, length):
        if self.size["y"] == 2 and 2 * length * 2 >= DOC_LIMIT - 1 > 2 * length:
            return [F32, F32, F32, BF16, BF16]
        return [F32] * len(self.window_bases(length))

    def window_back(self, terms, length):
        wide = self.size["y"]
        span = wide * length
        reach = -(-(DOC_LIMIT - 1) // span)
        y = self.index("y")

        def send(array, axis, step):
            low = array.astype(BF16)
            moved = self.swap(low, "y") if axis == "y" else self.shift(low, step)
            return moved.astype(F32)

        if wide == 2 and reach == 2:
            first = y == 0
            own, one, two, near, far = terms
            far = send(far, "y", 0)
            near = send(near, "y", 0)
            two = two + jnp.where(first, 0.0, far)
            one = one + jnp.where(first, far, near)
            own = own + jnp.where(first, near, 0.0)
            one = one + send(two, "z", -1)
            return own + send(one, "z", -1)
        total = None
        for k in range(reach, -1, -1):
            level = jnp.stack(terms[k * wide : (k + 1) * wide])
            total = level if total is None else level + send(total, "z", -1)
        return lax.psum_scatter(total.astype(BF16), "y", scatter_dimension=0, tiled=False).astype(F32)


def on_device(
    links,
    tokens,
    segment_ids,
    w_query,
    w_key,
    w_value,
    w_out,
    w_gate,
    w_up,
    w_down,
    g_in,
    g_post_attn,
    g_pre_ffn,
    g_post_ffn,
    g_query,
    g_key,
    cotangent,
):
    rows, length, width = tokens.shape
    count = rows * length
    size = links.size
    sx, sc, sz, sy = (size[axis] for axis in AXES)
    parts = sx * sc * sz * sy
    shard = w_gate.shape[0]
    hidden_shard = w_down.shape[0]
    chunk = -(-hidden_shard // 16) * 16
    units = sc * sz * chunk
    head_shard = g_query.shape[0]
    tokens_flat = tokens.reshape(count, width)
    cot_flat = cotangent.reshape(count, width)

    def columns(weight):
        split = weight.astype(BF16).reshape(shard, sx, sc, sz, sy, hidden_shard)
        split = jnp.pad(split, ((0, 0),) * 5 + ((0, chunk - hidden_shard),))
        return jnp.transpose(split, (1, 4, 0, 2, 3, 5)).reshape(sx, sy, shard, units)

    pair = jnp.stack([columns(w_gate), columns(w_up)], axis=2)
    pair = jnp.transpose(links.exchange(pair), (2, 0, 1, 3, 4)).reshape(2 * sx, sy * shard, units)
    full_pair = links.gather_cz(pair, 1).reshape(2, width, units)
    full_down = links.gather_cz(jnp.pad(w_down.astype(BF16), ((0, chunk - hidden_shard), (0, 0))), 0)

    lanes = 2 * HEAD + SMALL
    seg_row = jnp.pad(segment_ids.astype(BF16), ((0, 0), (0, lanes - length)))
    gain_columns = jnp.stack([g_in, g_post_attn, g_pre_ffn, g_post_ffn], axis=1)
    head_columns = jnp.pad(jnp.stack([g_query, g_key], axis=1), ((0, shard - head_shard), (0, 0)))
    kv_shard = jnp.concatenate(
        [gain_columns, head_columns, jnp.zeros((shard, SMALL - 6), F32), w_key, w_value], axis=1
    ).astype(BF16)
    first, seg_all = links.gather_all(
        jnp.concatenate([kv_shard, seg_row]), ((0, shard, lanes), (shard, rows, length))
    )
    full_kv = first[:, SMALL:]
    small = jnp.transpose(first[:, :SMALL]).astype(F32)
    gains = small[:8]
    heads = jnp.pad(small[4:6].reshape(2, parts, shard)[..., :head_shard].reshape(2, HEAD), ((0, 6), (0, 0)))
    seg_all = seg_all.reshape(sx, sc, sz, sy, rows, length)
    seg_all = lax.dynamic_slice(
        seg_all, (links.index("x"), links.index("core"), 0, 0, 0, 0), (1, 1, sz, sy, rows, length)
    )
    seg_flat = jnp.transpose(seg_all[0, 0], (2, 0, 1, 3)).reshape(rows, -1).astype(jnp.int32)
    bases = links.window_bases(length)
    seg_window = jnp.concatenate(
        [lax.dynamic_slice_in_dim(seg_flat, jnp.maximum(base, 0), length, 1) for base in bases], axis=1
    )
    step = jnp.arange(length, dtype=jnp.int32)
    pos_window = jnp.concatenate([base + step for base in bases])
    pos_own = links.index("z") * sy * length + links.index("y") * length + step
    seg_window = jnp.where((pos_window >= 0)[None], seg_window, -1)
    allowed = (segment_ids[:, :, None] == seg_window[:, None, :]) & (pos_window[None, None, :] <= pos_own[None, :, None])
    positions = jnp.sum(allowed.astype(jnp.int32), axis=2) - 1
    cosine, sine = rope_tables(positions.reshape(count))
    masks = (segment_ids.reshape(count, 1), pos_own[:, None], seg_window[:, None, :], pos_window[None])

    wide = max(width, HEADS * HEAD)
    q_shard = jnp.pad(w_query.astype(BF16), ((0, 0), (0, wide - HEADS * HEAD)))
    o_shard = jnp.pad(w_out.astype(BF16), ((0, 0), (0, wide - width)))
    out_shard = w_out.shape[0]
    full_out, full_query = links.gather_all(
        jnp.concatenate([o_shard, q_shard]), ((0, out_shard, width), (out_shard, shard, HEADS * HEAD))
    )

    h_in, k_proj, kv_low = kv_step(rows, length, tokens_flat, full_kv, gains, heads, cosine, sine)
    kv = links.window(kv_low, length)
    q_proj, query, mixed, attn, resid, h_ffn = attend(
        rows, length, h_in, tokens_flat, full_query, full_out, gains, heads, cosine, sine, masks, kv
    )
    h_all = links.gather_plane(h_ffn)
    hidden, turn, act, ffn_terms = ffn_forward(h_all, full_pair, full_down)
    ffn = links.sum_plane(ffn_terms)
    output, d_ffn, sums_ffn = middle(rows, length, ffn, resid, cot_flat, gains)

    d_all = links.gather_plane(d_ffn)
    d_pair, d_terms = ffn_backward(d_all, turn, act, full_pair, full_down)
    d_hffn = links.sum_plane(d_terms)
    grad_down = weight_grads(hidden, d_all[None], units // 7 if units % 7 == 0 else units)
    grad_down = links.sum_cz(grad_down.reshape(1, sc, sz, chunk, width))[:hidden_shard].astype(F32)
    grad_pair = weight_grads(h_all, d_pair, 384)
    sums = jnp.stack([links.sum_cz(grad_pair[k].reshape(sx, sc, sz, sy * shard, units)) for k in range(2)])
    sums = jnp.transpose(sums.reshape(2, sx, sy, shard, units), (1, 2, 0, 3, 4))
    got = links.exchange(sums).reshape(sx, sy, 2, shard, sc, sz, chunk)[..., :hidden_shard]
    got = jnp.transpose(got, (2, 3, 0, 4, 5, 1, 6)).reshape(2, shard, parts * hidden_shard).astype(F32)

    d_res, d_attn, d_qproj, sums_attn, heads_attn, *terms = attend_back(
        rows, length, d_hffn, cot_flat, resid, attn, q_proj, query, full_out, gains, heads, cosine, sine, masks, kv,
        links.window_kinds(length),
    )
    d_kv = links.window_back(terms, length)
    grad_out = weight_grads(mixed, d_attn[None], 512)[0]
    grad_query = weight_grads(h_in, d_qproj[None], 384)[0]
    wide_q = jnp.pad(grad_query, ((0, 0), (0, wide - HEADS * HEAD))).reshape(sx, sc, sz, sy, shard, wide)
    wide_o = jnp.pad(grad_out, ((0, 0), (0, wide - width))).reshape(sx, sc, sz, sy, out_shard, wide)
    second_sum = links.sum_all(jnp.concatenate([wide_o, wide_q], axis=4))

    d_kvproj, grad_tokens, sums_in, heads_in = finish(
        rows, length, d_kv, k_proj, d_qproj, tokens_flat, d_res, full_query, full_kv, gains, heads, cosine, sine
    )
    grad_kv = weight_grads(h_in, d_kvproj[None], 384)[0]
    gain_terms = (sums_ffn + sums_attn + sums_in)[:4]
    head_terms = (heads_attn + heads_in)[:2].reshape(2, parts, head_shard)
    head_terms = jnp.pad(head_terms, ((0, 0), (0, 0), (0, shard - head_shard))).reshape(2, width)
    small_terms = jnp.pad(jnp.concatenate([gain_terms, head_terms]), ((0, SMALL - 6), (0, 0)))
    first_grad = jnp.concatenate([jnp.transpose(small_terms).astype(BF16), grad_kv], axis=1)
    first_sum = links.sum_all_small(first_grad.reshape(sx, sc, sz, sy, shard, lanes))
    return (
        output.reshape(tokens.shape),
        grad_tokens.reshape(tokens.shape),
        second_sum[out_shard:, : HEADS * HEAD],
        first_sum[:, SMALL : SMALL + HEAD],
        first_sum[:, SMALL + HEAD :],
        second_sum[:out_shard, :width],
        got[0],
        got[1],
        grad_down,
        *(first_sum[:, k] for k in range(4)),
        *(first_sum[:head_shard, 4 + k] for k in range(2)),
    )


def solution(mesh):
    plane = mesh.shape["dp"] // 2
    by_chip = Mesh(mesh.devices.reshape(plane, 2, -1, plane), AXES)
    links = Links(by_chip)
    placed = P(("x", "core"), ("z", "y"), None)
    matrix = P(AXES, None)
    vector = P(AXES)
    in_specs = (placed, P(("x", "core"), ("z", "y"))) + (matrix,) * 7 + (vector,) * 6 + (placed,)
    out_specs = (placed, placed) + (matrix,) * 7 + (vector,) * 6

    def step(*arguments):
        return on_device(links, *arguments)

    return jax.shard_map(step, mesh=by_chip, in_specs=in_specs, out_specs=out_specs, check_vma=False)
```

```python
import functools
import math

import jax
import jax.numpy as jnp
from jax import lax
from jax.experimental import pallas as pl
from jax.experimental.pallas import tpu as pltpu
from jax.sharding import Mesh
from jax.sharding import PartitionSpec as P

HEADS = 4
HEAD = 256
HALF = HEAD // 2
DOC_LIMIT = 512
EPSILON = 1e-06
ROPE_BASE = 1000000.0
NEG_FILL = -1e30
SCORE_SCALE = HEAD ** (-0.5)
SLOPE = math.sqrt(2.0 / math.pi)
F32 = jnp.float32
BF16 = jnp.bfloat16
PLANE = ("x", "y")
AXES = ("x", "core", "z", "y")
SWAP = [(0, 1), (1, 0)]
IN, POST_ATTN, PRE_FFN, POST_FFN = range(4)
SMALL = 128
ROOM = 58 << 20


def dot(left, right, dims):
    return lax.dot_general(left, right, (dims, ((), ())), preferred_element_type=F32)


def mm(left, right):
    return dot(left, right, ((1,), (0,)))


def mm_t(left, right):
    return dot(left, right, ((1,), (1,)))


def t_mm(left, right):
    return dot(left, right, ((0,), (0,)))


def inv_rms(values):
    return lax.rsqrt(jnp.mean(values * values, axis=-1, keepdims=True) + EPSILON)


def rms_back(values, gain_vec, d_norm):
    scale = inv_rms(values)
    unit = values * scale
    weighted = d_norm * gain_vec
    d_values = scale * (weighted - unit * jnp.mean(weighted * unit, axis=-1, keepdims=True))
    return d_values, d_norm * unit


def rope_tables(positions):
    inverse = ROPE_BASE ** (-(jnp.arange(HALF, dtype=F32) * 2.0 / HEAD))
    angles = positions.astype(F32)[..., None] * inverse
    return jnp.cos(angles), jnp.sin(angles)


def rotate(values, cosine, sine):
    first, second = values[:, :HALF], values[:, HALF:]
    return jnp.concatenate([first * cosine - second * sine, second * cosine + first * sine], axis=-1)


def column_sum(terms):
    return jnp.sum(terms, axis=0, keepdims=True)


def call(body, grid, in_specs, out_specs, out_shape, flops, scratch=()):
    moved = sum(math.prod(one.shape) * one.dtype.itemsize for one in jax.tree.leaves(out_shape))
    return pl.pallas_call(
        body,
        grid=grid,
        in_specs=in_specs,
        out_specs=out_specs,
        out_shape=out_shape,
        scratch_shapes=list(scratch),
        compiler_params=pltpu.CompilerParams(vmem_limit_bytes=ROOM),
        cost_estimate=pl.CostEstimate(flops=flops, bytes_accessed=2 * moved, transcendentals=0),
    )


def shaped(*shape, dtype=F32):
    return jax.ShapeDtypeStruct(shape, dtype)


def whole(*shape):
    return pl.BlockSpec(shape, lambda i: (0,) * len(shape))


def rows_of(tile, width):
    return pl.BlockSpec((tile, width), lambda i: (i, 0))


def row_block(*shape):
    return pl.BlockSpec((1,) + shape, lambda i: (i,) + (0,) * len(shape))


def kv_body(tok_ref, wkv_ref, gains_ref, head_ref, cos_ref, sin_ref, h_ref, kproj_ref, kv_ref):
    tokens = tok_ref[...].astype(F32)
    h = (tokens * inv_rms(tokens) * gains_ref[IN : IN + 1]).astype(BF16)
    h_ref[...] = h
    proj = mm(h, wkv_ref[...])
    k_proj = proj[:, :HEAD]
    kproj_ref[...] = k_proj
    key = rotate(k_proj * inv_rms(k_proj) * head_ref[1:2], cos_ref[...], sin_ref[...])
    kv_ref[0, :, :HEAD] = key.astype(BF16)
    kv_ref[0, :, HEAD:] = proj[:, HEAD:].astype(BF16)


def kv_step(rows, length, tokens, wkv, gains, heads, cosine, sine):
    count, width = tokens.shape
    return call(
        kv_body,
        (rows,),
        [rows_of(length, width), whole(*wkv.shape), whole(*gains.shape), whole(*heads.shape)]
        + [whole(length, HALF)] * 2,
        [rows_of(length, width), rows_of(length, HEAD), row_block(length, 2 * HEAD)],
        [shaped(count, width, dtype=BF16), shaped(count, HEAD), shaped(rows, length, 2 * HEAD, dtype=BF16)],
        2 * count * width * 2 * HEAD,
    )(tokens, wkv, gains, heads, cosine, sine)


def by_head(array):
    return jnp.concatenate([array[:, h * HEAD : (h + 1) * HEAD] for h in range(HEADS)], axis=0)


def by_lane(array):
    part = array.shape[0] // HEADS
    return jnp.concatenate([array[h * part : (h + 1) * part] for h in range(HEADS)], axis=1)


def probs_of(links, query, keys, own_ref, seg_ref):
    length = own_ref.shape[0]
    bases = links.window_bases(length)
    here = links.position(length)
    step = lax.broadcasted_iota(jnp.int32, (1, length), 1)
    segs, later = [], []
    for base in bases:
        row = seg_ref[0, pl.ds(jnp.maximum(base, 0) // length, 1), :]
        segs.append(jnp.where(base >= 0, row, -1.0))
        later.append(base - here + step)
    own_step = lax.broadcasted_iota(jnp.int32, (length, 1), 0)
    allowed = (own_ref[...] == jnp.concatenate(segs, axis=1)) & (jnp.concatenate(later, axis=1) <= own_step)
    allowed = jnp.concatenate([allowed.astype(F32)] * HEADS, axis=0) > 0.5
    scores = jnp.where(allowed, mm_t(query, keys) * SCORE_SCALE, NEG_FILL)
    powers = jnp.exp(scores - jnp.max(scores, axis=-1, keepdims=True))
    return powers / jnp.sum(powers, axis=-1, keepdims=True)


def attend_body(links, blocks, *refs):
    (h_ref, tok_ref, wq_ref, wo_ref, gains_ref, head_ref, cos_ref, sin_ref) = refs[:8]
    masks, kv_refs = refs[8:10], refs[10 : 10 + blocks]
    qproj_ref, query_ref, mixed_ref, attn_ref, resid_ref, hffn_ref = refs[10 + blocks :]
    proj = mm(h_ref[...], wq_ref[...])
    qproj_ref[...] = proj
    cosine, sine = cos_ref[...], sin_ref[...]
    query = []
    for h in range(HEADS):
        one = proj[:, h * HEAD : (h + 1) * HEAD]
        query.append(rotate(one * inv_rms(one) * head_ref[0:1], cosine, sine).astype(BF16))
    query_ref[...] = jnp.concatenate(query, axis=1)
    keys = jnp.concatenate([one[0, :, :HEAD] for one in kv_refs], axis=0)
    values = jnp.concatenate([one[0, :, HEAD:] for one in kv_refs], axis=0)
    probs = probs_of(links, jnp.concatenate(query, axis=0), keys, *masks).astype(BF16)
    mixed = by_lane(mm(probs, values).astype(BF16))
    mixed_ref[...] = mixed
    attn = mm(mixed, wo_ref[...])
    attn_ref[...] = attn
    resid = tok_ref[...].astype(F32) + attn * inv_rms(attn) * gains_ref[POST_ATTN : POST_ATTN + 1]
    resid_ref[...] = resid
    hffn_ref[...] = (resid * inv_rms(resid) * gains_ref[PRE_FFN : PRE_FFN + 1]).astype(BF16)


def mask_specs(masks):
    own, segs = masks
    return [rows_of(own.shape[0] // segs.shape[0], 1), row_block(*segs.shape[1:])]


def attend(links, rows, length, h, tokens, wq, wo, gains, heads, cosine, sine, masks, kv):
    count, width = tokens.shape
    wide = HEADS * HEAD
    window = len(kv) * length
    return call(
        functools.partial(attend_body, links, len(kv)),
        (rows,),
        [rows_of(length, width)] * 2
        + [whole(*one.shape) for one in (wq, wo, gains, heads)]
        + [whole(length, HALF)] * 2
        + mask_specs(masks)
        + [row_block(length, 2 * HEAD)] * len(kv),
        [rows_of(length, wide)] * 3 + [rows_of(length, width)] * 3,
        [
            shaped(count, wide),
            shaped(count, wide, dtype=BF16),
            shaped(count, wide, dtype=BF16),
            shaped(count, width),
            shaped(count, width),
            shaped(count, width, dtype=BF16),
        ],
        4 * count * wide * (width + window),
    )(h, tokens, wq, wo, gains, heads, cosine, sine, *masks, *kv)


def attend_back_body(links, blocks, *refs):
    (dh_ref, cot_ref, resid_ref, attn_ref, qproj_ref, query_ref, wo_ref, gains_ref, head_ref, cos_ref, sin_ref) = refs[:11]
    masks, kv_refs = refs[11:13], refs[13 : 13 + blocks]
    dres_ref, dattn_ref, dq_ref, sums_ref, head_sums_ref = refs[13 + blocks : 18 + blocks]
    term_refs = refs[18 + blocks :]
    d_norm, pre_terms = rms_back(resid_ref[...], gains_ref[PRE_FFN : PRE_FFN + 1], dh_ref[...])
    d_res = cot_ref[...].astype(F32) + d_norm
    dres_ref[...] = d_res
    d_attn, post_terms = rms_back(attn_ref[...], gains_ref[POST_ATTN : POST_ATTN + 1], d_res)
    d_attn = d_attn.astype(BF16)
    dattn_ref[...] = d_attn
    d_mixed = by_head(mm_t(d_attn, wo_ref[...]).astype(BF16))
    query = by_head(query_ref[...])
    keys = jnp.concatenate([one[0, :, :HEAD] for one in kv_refs], axis=0)
    values = jnp.concatenate([one[0, :, HEAD:] for one in kv_refs], axis=0)
    probs = probs_of(links, query, keys, *masks)
    d_probs = mm_t(d_mixed, values)
    d_scores = (probs * (d_probs - jnp.sum(d_probs * probs, axis=-1, keepdims=True))).astype(BF16)
    key_terms = t_mm(d_scores, query) * SCORE_SCALE
    value_terms = t_mm(probs.astype(BF16), d_mixed)
    length = query_ref.shape[0]
    for k, ref in enumerate(term_refs):
        at = slice(k * length, (k + 1) * length)
        ref[0, :, :HEAD] = key_terms[at].astype(ref.dtype)
        ref[0, :, HEAD:] = value_terms[at].astype(ref.dtype)
    d_query = mm(d_scores, keys) * SCORE_SCALE
    cosine, sine = cos_ref[...], -sin_ref[...]
    head_sum = jnp.zeros((1, HEAD), F32)
    for h in range(HEADS):
        turned = rotate(d_query[h * length : (h + 1) * length], cosine, sine)
        lanes = slice(h * HEAD, (h + 1) * HEAD)
        d_proj, terms = rms_back(qproj_ref[:, lanes], head_ref[0:1], turned)
        dq_ref[:, lanes] = d_proj.astype(BF16)
        head_sum += column_sum(terms)

    @pl.when(pl.program_id(0) == 0)
    def _():
        sums_ref[...] = jnp.zeros_like(sums_ref)
        head_sums_ref[...] = jnp.zeros_like(head_sums_ref)

    sums_ref[POST_ATTN : POST_ATTN + 1] += column_sum(post_terms)
    sums_ref[PRE_FFN : PRE_FFN + 1] += column_sum(pre_terms)
    head_sums_ref[0:1] += head_sum


def attend_back(links, rows, length, dh, cot, resid, attn, qproj, query, wo, gains, heads, cosine, sine, masks, kv, kinds):
    count, width = dh.shape
    wide = HEADS * HEAD
    window = len(kv) * length
    return call(
        functools.partial(attend_back_body, links, len(kv)),
        (rows,),
        [rows_of(length, width)] * 4
        + [rows_of(length, wide)] * 2
        + [whole(*one.shape) for one in (wo, gains, heads)]
        + [whole(length, HALF)] * 2
        + mask_specs(masks)
        + [row_block(length, 2 * HEAD)] * len(kv),
        [rows_of(length, width)] * 2
        + [rows_of(length, wide), whole(8, width), whole(8, HEAD)]
        + [row_block(length, 2 * HEAD)] * len(kv),
        [
            shaped(count, width),
            shaped(count, width, dtype=BF16),
            shaped(count, wide, dtype=BF16),
            shaped(8, width),
            shaped(8, HEAD),
        ]
        + [shaped(rows, length, 2 * HEAD, dtype=kind) for kind in kinds],
        2 * count * wide * (width + 5 * window),
    )(dh, cot, resid, attn, qproj, query, wo, gains, heads, cosine, sine, *masks, *kv)


def finish_body(dkv_ref, kproj_ref, dq_ref, tok_ref, dres_ref, wq_ref, wkv_ref, gains_ref, head_ref, cos_ref, sin_ref,
                dkvp_ref, grad_ref, sums_ref, head_sums_ref):
    d_kv = dkv_ref[0]
    turned = rotate(d_kv[:, :HEAD], cos_ref[...], -sin_ref[...])
    d_key, key_terms = rms_back(kproj_ref[...], head_ref[1:2], turned)
    d_proj = jnp.concatenate([d_key.astype(BF16), d_kv[:, HEAD:].astype(BF16)], axis=1)
    dkvp_ref[...] = d_proj
    d_hin = mm_t(dq_ref[...], wq_ref[...]) + mm_t(d_proj, wkv_ref[...])
    d_tokens, in_terms = rms_back(tok_ref[...].astype(F32), gains_ref[IN : IN + 1], d_hin)
    grad_ref[...] = (dres_ref[...] + d_tokens).astype(BF16)

    @pl.when(pl.program_id(0) == 0)
    def _():
        sums_ref[...] = jnp.zeros_like(sums_ref)
        head_sums_ref[...] = jnp.zeros_like(head_sums_ref)

    sums_ref[IN : IN + 1] += column_sum(in_terms)
    head_sums_ref[1:2] += column_sum(key_terms)


def finish(rows, length, dkv, kproj, dq, tokens, dres, wq, wkv, gains, heads, cosine, sine):
    count, width = tokens.shape
    wide = HEADS * HEAD
    return call(
        finish_body,
        (rows,),
        [row_block(length, 2 * HEAD), rows_of(length, HEAD), rows_of(length, wide)]
        + [rows_of(length, width)] * 2
        + [whole(*one.shape) for one in (wq, wkv, gains, heads)]
        + [whole(length, HALF)] * 2,
        [rows_of(length, 2 * HEAD), rows_of(length, width), whole(8, width), whole(8, HEAD)],
        [shaped(count, 2 * HEAD, dtype=BF16), shaped(count, width, dtype=BF16), shaped(8, width), shaped(8, HEAD)],
        2 * count * width * (wide + 2 * HEAD),
    )(dkv, kproj, dq, tokens, dres, wq, wkv, gains, heads, cosine, sine)


def pieces_of(total, step):
    return [(k, min(step, total - k)) for k in range(0, total, step)]


def up_body(step, h_ref, pair_ref, down_ref, hidden_ref, turn_ref, act_ref, out_ref):
    h = h_ref[...]
    for at, wide in pieces_of(hidden_ref.shape[1], step):
        cols = pl.ds(at, wide)
        gate = mm(h, pair_ref[0, :, cols])
        up = mm(h, pair_ref[1, :, cols])
        square = gate * gate
        bent = jnp.tanh(gate * (SLOPE + SLOPE * 0.044715 * square))
        half = 0.5 + 0.5 * bent
        act = gate * half
        d_act = half + 0.5 * gate * (1.0 - bent * bent) * (SLOPE + 3 * SLOPE * 0.044715 * square)
        hidden_ref[:, cols] = (act * up).astype(BF16)
        turn_ref[:, cols] = (up * d_act).astype(BF16)
        act_ref[:, cols] = act.astype(BF16)
    out_ref[...] = mm(hidden_ref[...], down_ref[...]).astype(BF16)


def ffn_forward(h, pair, down, tile=256, step=256):
    count, width = h.shape
    units = pair.shape[2]
    return call(
        functools.partial(up_body, step),
        (count // tile,),
        [rows_of(tile, width), whole(2, width, units), whole(units, width)],
        [rows_of(tile, units)] * 3 + [rows_of(tile, width)],
        [shaped(count, units, dtype=BF16)] * 3 + [shaped(count, width, dtype=BF16)],
        6 * count * width * units,
    )(h, pair, down)


def down_body(step, d_ref, turn_ref, act_ref, pair_ref, down_ref, pair_out, out_ref):
    d = d_ref[...]
    for at, wide in pieces_of(turn_ref.shape[1], step):
        cols = pl.ds(at, wide)
        d_hidden = mm_t(d, down_ref[cols, :])
        pair_out[0, :, cols] = (d_hidden * turn_ref[:, cols].astype(F32)).astype(BF16)
        pair_out[1, :, cols] = (d_hidden * act_ref[:, cols].astype(F32)).astype(BF16)
    out_ref[...] = (mm_t(pair_out[0], pair_ref[0]) + mm_t(pair_out[1], pair_ref[1])).astype(BF16)


def ffn_backward(d, turn, act, pair, down, tile=256, step=256):
    count, width = d.shape
    units = pair.shape[2]
    return call(
        functools.partial(down_body, step),
        (count // tile,),
        [rows_of(tile, width), rows_of(tile, units), rows_of(tile, units), whole(2, width, units), whole(units, width)],
        [pl.BlockSpec((2, tile, units), lambda i: (0, i, 0)), rows_of(tile, width)],
        [shaped(2, count, units, dtype=BF16), shaped(count, width, dtype=BF16)],
        6 * count * width * units,
    )(d, turn, act, pair, down)


def put(kept_ref, sent_ref, core, index, value):
    @pl.when(lax.axis_index("core") == core)
    def _():
        kept_ref[index] = value

    @pl.when(lax.axis_index("core") != core)
    def _():
        sent_ref[index] = value


def grads_body(places, sets, *refs):
    kept_ref, sent_ref = refs[2 * sets :]
    total = None
    for left_ref, right_ref in zip(refs[:sets], refs[sets : 2 * sets], strict=True):
        term = t_mm(left_ref[...], right_ref[0])
        total = term if total is None else total + term
    total = total.astype(BF16)
    tile = total.shape[0]
    for k in range(sum(count for _, _, _, count in places) // tile):

        @pl.when(pl.program_id(0) == k)
        def _(k=k):
            for core, at, row, count in places:
                begin, end = max(row, k * tile), min(row + count, (k + 1) * tile)
                if begin < end:
                    to = at + begin - row
                    index = (slice(to, to + end - begin), slice(None))
                    put(kept_ref, sent_ref, core, index, total[begin - k * tile : end - k * tile])


def weight_grads(lefts, rights, which, places):
    rows, cols = lefts[0].shape[1], rights[0].shape[2]
    count = sum(one.shape[0] for one in lefts)
    tile = 384 if rows % 384 == 0 else 256
    return call(
        functools.partial(grads_body, places, len(lefts)),
        (rows // tile,),
        [pl.BlockSpec((one.shape[0], tile), lambda i: (0, i)) for one in lefts]
        + [pl.BlockSpec((1,) + one.shape[1:], lambda i: (which, 0, 0)) for one in rights],
        [whole(rows // 2, cols)] * 2,
        [shaped(rows // 2, cols, dtype=BF16)] * 2,
        2 * count * rows * cols,
    )(*lefts, *rights)


def outer_body(order, shards, mixed_ref, dattn_ref, h_ref, dq_ref, kept_ref, sent_ref):
    lanes = kept_ref.shape[2]
    at = 0
    for rows, left, right in ((shards[0], mixed_ref, dattn_ref), (shards[1], h_ref, dq_ref)):
        total = t_mm(left[...], right[...]).astype(BF16)
        wide = total.shape[1]
        for core, place, number in order:
            index = (place, slice(at, at + rows), slice(0, wide))
            put(kept_ref, sent_ref, core, index, total[number * rows : (number + 1) * rows])
        if wide < lanes:
            empty = jnp.zeros((kept_ref.shape[0], rows, lanes - wide), BF16)
            kept_ref[:, at : at + rows, wide:] = empty
            sent_ref[:, at : at + rows, wide:] = empty
        at += rows


def outer_grads(order, shards, mixed, d_attn, h, d_q):
    count = mixed.shape[0]
    shape = (len(order) // 2, sum(shards), max(d_attn.shape[1], d_q.shape[1]))
    return call(
        functools.partial(outer_body, order, shards),
        (1,),
        [whole(*one.shape) for one in (mixed, d_attn, h, d_q)],
        [whole(*shape)] * 2,
        [shaped(*shape, dtype=BF16)] * 2,
        2 * count * (mixed.shape[1] * d_attn.shape[1] + h.shape[1] * d_q.shape[1]),
    )(mixed, d_attn, h, d_q)


def first_body(order, shard, h_ref, dkv_ref, small_ref, kept_ref, sent_ref):
    small = small_ref[...].T.astype(BF16)
    total = t_mm(h_ref[...], dkv_ref[...]).astype(BF16)
    for core, place, number in order:
        rows = slice(number * shard, (number + 1) * shard)
        put(kept_ref, sent_ref, core, (place, slice(None), slice(0, SMALL)), small[rows])
        put(kept_ref, sent_ref, core, (place, slice(None), slice(SMALL, None)), total[rows])


def first_grads(order, shard, h, d_kv, small):
    count, rows = h.shape
    shape = (len(order) // 2, shard, d_kv.shape[1] + SMALL)
    return call(
        functools.partial(first_body, order, shard),
        (1,),
        [whole(*one.shape) for one in (h, d_kv, small)],
        [whole(*shape)] * 2,
        [shaped(*shape, dtype=BF16)] * 2,
        2 * count * rows * d_kv.shape[1],
    )(h, d_kv, small)


def middle_body(ffn_ref, resid_ref, cot_ref, gains_ref, out_ref, dffn_ref, sums_ref):
    ffn = ffn_ref[...]
    gain = gains_ref[POST_FFN : POST_FFN + 1]
    out_ref[...] = (resid_ref[...] + ffn * inv_rms(ffn) * gain).astype(BF16)
    d_ffn, terms = rms_back(ffn, gain, cot_ref[...].astype(F32))
    dffn_ref[...] = d_ffn.astype(BF16)

    @pl.when(pl.program_id(0) == 0)
    def _():
        sums_ref[...] = jnp.zeros_like(sums_ref)

    sums_ref[POST_FFN : POST_FFN + 1] += column_sum(terms)


def middle(rows, length, ffn, resid, cot, gains):
    count, width = ffn.shape
    return call(
        middle_body,
        (rows,),
        [rows_of(length, width)] * 3 + [whole(*gains.shape)],
        [rows_of(length, width)] * 2 + [whole(8, width)],
        [shaped(count, width, dtype=BF16), shaped(count, width, dtype=BF16), shaped(8, width)],
        20 * count * width,
    )(ffn, resid, cot, gains)


def place_body(links, shard, parts, own_ref, other_ref, *refs):
    outs, scratch = refs[:-1], refs[-1]
    depth = links.size["z"]
    at_x, at_c, at_z, at_y = (links.index(axis) for axis in AXES)
    number = 0
    for x in range(2):
        for core in range(2):
            for z in range(depth):
                for y in range(2):
                    slot = jnp.abs(at_x - x) + 2 * jnp.abs(at_y - y)
                    slot = slot * depth + jnp.remainder(at_z - z + depth, depth)
                    mine = own_ref[slot].astype(F32)
                    theirs = other_ref[slot].astype(F32)
                    piece = jnp.where(at_c == core, mine, theirs)
                    scratch[number] = piece
                    number += 1
    for part, out in zip(parts, outs, strict=True):
        for k in range(number):
            if len(part) == 4:
                first, count, at, lanes = part
                out[k * count : (k + 1) * count, :] = scratch[k, first : first + count, at : at + lanes].astype(out.dtype)
                continue
            if len(part) == 3:
                first, count, lanes = part
                if k < 2 * depth:
                    ids = scratch[(at_x * 2 + at_c) * 2 * depth + k]
                    for row in range(count):
                        out[row, k : k + 1, :] = ids[first + row : first + row + 1, :lanes]
                continue
            row, at, lanes, vectors = part[:4]
            for v in range(vectors):
                begin = at + v * lanes
                out[v : v + 1, k * lanes : (k + 1) * lanes] = scratch[k, row : row + 1, begin : begin + lanes]


def placed(links, own, other, parts):
    slots, rows, lanes = own.shape
    number = 2 * slots
    return pl.pallas_call(
        functools.partial(place_body, links, rows, parts),
        out_shape=[
            shaped(number * part[1], part[3], dtype=BF16)
            if len(part) == 4
            else shaped(part[1], slots // 2, part[2])
            if len(part) == 3
            else shaped(8, number * part[2])
            for part in parts
        ],
        scratch_shapes=[pltpu.VMEM((number, rows, lanes), F32)],
        compiler_params=pltpu.CompilerParams(vmem_limit_bytes=ROOM),
    )(own, other)


class Links:
    def __init__(self, mesh):
        self.size = dict(mesh.shape)
        self.pairs_only = self.size["x"] == 2 and self.size["y"] == 2

    def index(self, axis):
        return lax.axis_index(axis)

    def swap(self, array, axis):
        return lax.ppermute(array, axis, SWAP)

    def shift(self, array, step):
        depth = self.size["z"]
        pairs = [(i, i + step) for i in range(depth) if 0 <= i + step < depth]
        return lax.ppermute(array, "z", pairs)

    def turn(self, array, step):
        depth = self.size["z"]
        return lax.ppermute(array, "z", [(i, (i + step) % depth) for i in range(depth)])

    def ordered(self, own, other, axis):
        first = self.index(axis) == 0
        return jnp.where(first, jnp.stack([own, other]), jnp.stack([other, own]))

    def along_z(self, array):
        return jnp.stack([array] + [self.turn(array, k) for k in range(1, self.size["z"])])

    def across_plane(self, along):
        if not self.pairs_only:
            return along
        across = lax.ppermute(along, PLANE, [(k, 3 - k) for k in range(4)])
        return jnp.concatenate([along, self.swap(along, "x"), self.swap(along, "y"), across])

    def placed(self, array, own, parts, other=None):
        if self.pairs_only:
            other = self.swap(own, "core") if other is None else other
            return placed(self, own, other, parts)
        full = lax.all_gather(array, AXES, axis=0)
        cuts = []
        for part in parts:
            if len(part) == 4:
                r, n, c, w = part
                cuts.append(full[:, r : r + n, c : c + w].reshape(-1, w))
            elif len(part) == 3:
                r, n, w = part
                blocks = self.size["z"] * self.size["y"]
                at = (self.index("x") * 2 + self.index("core")) * blocks
                ids = lax.dynamic_slice_in_dim(full[:, r : r + n, :w], at, blocks)
                cuts.append(jnp.swapaxes(ids, 0, 1).astype(F32))
            else:
                r, c, w, n = part[:4]
                rows = jnp.swapaxes(full[:, r, c : c + n * w].reshape(-1, n, w), 0, 1).reshape(n, -1)
                cuts.append(jnp.pad(rows.astype(F32), ((0, 8 - n), (0, 0))))
        return cuts

    def order(self, axes):
        found = []
        counts = [self.size[axis] for axis in AXES]
        for number in range(math.prod(counts)):
            at, rest = {}, number
            for axis, many in zip(AXES[::-1], counts[::-1], strict=True):
                at[axis], rest = rest % many, rest // many
            place = 0
            for axis in axes:
                place = place * self.size[axis] + at[axis]
            found.append((at["core"], place, number))
        return found

    def gather_cz(self, array, dim):
        return lax.all_gather(array, ("core", "z"), axis=dim, tiled=True)

    def sum_halves(self, array, axis, dim):
        if self.size[axis] == 2:
            at = self.index(axis)
            sent = self.swap(lax.dynamic_index_in_dim(array, 1 - at, dim, False), axis)
            kept = lax.dynamic_index_in_dim(array, at, dim, False)
            return (kept.astype(F32) + sent.astype(F32)).astype(array.dtype)
        return lax.psum_scatter(array, axis, scatter_dimension=dim, tiled=False)

    def sum_cores(self, kept, sent):
        return (kept.astype(F32) + self.swap(sent, "core").astype(F32)).astype(kept.dtype)

    def sum_z(self, array, dim):
        depth = self.size["z"]
        z = self.index("z")

        def block(k):
            return lax.dynamic_index_in_dim(array, jnp.remainder(z + k, depth), dim, False)

        total = block(0).astype(F32)
        for k in range(1, depth):
            total = total + self.turn(block(k), k).astype(F32)
        return total

    def sum_z_low(self, array):
        return lax.psum_scatter(array, "z", scatter_dimension=0, tiled=True)

    def planes(self, array):
        sx, sy, sz = (self.size[axis] for axis in "xyz")
        return self.sum_halves(array.reshape((sx, sy, sz) + array.shape[1:]), "x", 0)

    def sum_all_small(self, array):
        got = lax.all_to_all(array, ("x", "z", "y"), 0, 0, tiled=True)
        return jnp.sum(got.astype(F32), axis=0)

    def exchange(self, array):
        count = self.size["x"] * self.size["y"]
        flat = array.reshape((count,) + array.shape[2:])
        return lax.all_to_all(flat, PLANE, 0, 0, tiled=True).reshape(array.shape)

    def over_plane(self, rows, first, then=None):
        if not self.pairs_only:
            return [first(lax.all_gather(rows, PLANE, axis=0, tiled=True))]
        half = rows.shape[0] // 2
        upper, lower = lax.optimization_barrier((rows[:half], rows[half:]))
        near = lax.optimization_barrier((self.swap(upper, "x"), self.swap(lower, "y")))
        near = jnp.concatenate([upper, near[0], lower, near[1]])
        upper, lower, near = lax.optimization_barrier((near[: 2 * half], near[2 * half :], near))
        upper, lower, done = lax.optimization_barrier((self.swap(upper, "y"), self.swap(lower, "x"), first(near)))
        return [done, first(jnp.concatenate([upper, lower]))]

    def sum_plane(self, parts, beside=(None, None)):
        works = [work or (lambda *given: ()) for work in beside]
        if not self.pairs_only:
            total = lax.psum_scatter(parts[0], PLANE, scatter_dimension=0, tiled=True).astype(F32)
            return total, works[1](*works[0]())
        near, far = parts
        half = far.shape[0] // 2
        quarter = half // 2
        upper, lower = lax.optimization_barrier((far[:half], far[half:]))
        upper, lower, extra = lax.optimization_barrier((self.swap(upper, "y"), self.swap(lower, "x"), works[0]()))
        at = [near[k * quarter : (k + 1) * quarter].astype(F32) for k in range(4)]
        own = (at[0] + upper[:quarter].astype(F32), at[2] + lower[:quarter].astype(F32))
        upper = (at[1] + upper[quarter:].astype(F32)).astype(BF16)
        lower = (at[3] + lower[quarter:].astype(F32)).astype(BF16)
        upper, lower = lax.optimization_barrier((upper, lower))
        upper, lower, extra = lax.optimization_barrier((self.swap(upper, "x"), self.swap(lower, "y"), works[1](*extra)))
        return jnp.concatenate([own[0] + upper.astype(F32), own[1] + lower.astype(F32)]), extra

    def position(self, length):
        return (self.index("z") * self.size["y"] + self.index("y")) * length

    def window_bases(self, length):
        z, y, wide = self.index("z"), self.index("y"), self.size["y"]
        span = wide * length
        reach = -(-(DOC_LIMIT - 1) // span)
        base = self.position(length)
        if wide == 2 and reach == 2:
            cross = jnp.where(y == 0, z * span - length, z * span)
            return [base, base - span, base - 2 * span, cross, cross - span]
        return [(z - k) * span + j * length for k in range(reach + 1) for j in range(wide)]

    def window(self, array, length, beside):
        wide = self.size["y"]
        reach = -(-(DOC_LIMIT - 1) // (wide * length))
        if wide == 2 and reach == 2:
            first = self.index("y") == 0
            one, extra = lax.optimization_barrier((self.shift(array, 1), beside[0]()))
            near = self.swap(jnp.where(first, array, one), "y")
            two, near, extra = lax.optimization_barrier((self.shift(one, 1), near, beside[1](extra)))
            far = self.swap(jnp.where(first, one, two), "y")
            return [array, one, two, near, far], extra
        along = [lax.all_gather(array, "y", axis=0)]
        for _ in range(reach):
            along.append(self.shift(along[-1], 1))
        return [level[j] for level in along for j in range(wide)], beside[1](beside[0]())

    def window_kinds(self, length):
        if self.size["y"] == 2 and 2 * length * 2 >= DOC_LIMIT - 1 > 2 * length:
            return [F32, F32, F32, BF16, BF16]
        return [F32] * len(self.window_bases(length))

    def window_back(self, terms, length, beside=()):
        wide = self.size["y"]
        span = wide * length
        reach = -(-(DOC_LIMIT - 1) // span)
        results = []

        def follow(*arrays):
            if len(results) < len(beside):
                results.append(beside[len(results)](*(results[-1] if results else ())))
                *arrays, results[-1] = lax.optimization_barrier((*arrays, results[-1]))
            return arrays

        if wide == 2 and reach == 2:
            first = self.index("y") == 0
            own, one, two, near, far = terms
            (far,) = follow(self.swap(far, "y"))
            two = (two + jnp.where(first, 0.0, far.astype(F32))).astype(BF16)
            two, near = follow(self.shift(two, -1), self.swap(near, "y"))
            near = near.astype(F32)
            one = (one + jnp.where(first, far.astype(F32), near) + two.astype(F32)).astype(BF16)
            own = own + jnp.where(first, near, 0.0)
            (own,) = follow(own + self.shift(one, -1).astype(F32))
            return own, results
        total = None
        for k in range(reach, -1, -1):
            level = jnp.stack(terms[k * wide : (k + 1) * wide])
            total = level if total is None else level + self.shift(total.astype(BF16), -1).astype(F32)
        total = lax.psum_scatter(total.astype(BF16), "y", scatter_dimension=0, tiled=False).astype(F32)
        for _ in beside:
            (total,) = follow(total)
        return total, results


def on_device(
    links,
    tokens,
    segment_ids,
    w_query,
    w_key,
    w_value,
    w_out,
    w_gate,
    w_up,
    w_down,
    g_in,
    g_post_attn,
    g_pre_ffn,
    g_post_ffn,
    g_query,
    g_key,
    cotangent,
):
    rows, length, width = tokens.shape
    count = rows * length
    size = links.size
    sx, sc, sz, sy = (size[axis] for axis in AXES)
    parts = sx * sc * sz * sy
    shard = w_gate.shape[0]
    hidden_shard = w_down.shape[0]
    chunk = -(-hidden_shard // 16) * 16
    units = sc * sz * chunk
    head_shard = g_query.shape[0]
    tokens_flat = tokens.reshape(count, width)
    cot_flat = cotangent.reshape(count, width)

    step = jnp.arange(length, dtype=jnp.int32)
    pos_own = links.position(length) + step
    cosine, sine = rope_tables(pos_own)

    lanes = 2 * HEAD + SMALL
    vectors = jnp.concatenate([g_in, g_post_attn, g_pre_ffn, g_post_ffn, g_query, g_key])
    vectors = lax.optimization_barrier(jnp.pad(vectors, (0, 2 * HEAD - vectors.shape[0])))[None]
    seg_rows = jnp.pad(segment_ids.astype(F32), ((0, 0), (0, 2 * HEAD - length)))
    kv_shard = jnp.concatenate([jnp.concatenate([w_key, w_value], axis=1), seg_rows, vectors]).astype(BF16)
    own_ids = segment_ids.astype(F32).reshape(count, 1)
    kv_shard, own_ids, w_gate, w_up, w_down, w_query, w_out = lax.optimization_barrier(
        (kv_shard, own_ids, w_gate, w_up, w_down, w_query, w_out)
    )
    kv_along = links.along_z(kv_shard)
    full_down = links.gather_cz(jnp.pad(w_down.astype(BF16), ((0, chunk - hidden_shard), (0, 0))), 0)

    def columns(weight):
        split = weight.astype(BF16).reshape(shard, sx, sc, sz, sy, hidden_shard)
        split = jnp.pad(split, ((0, 0),) * 5 + ((0, chunk - hidden_shard),))
        return jnp.transpose(split, (1, 4, 0, 2, 3, 5)).reshape(sx, sy, shard, units)

    pair = jnp.stack([columns(w_gate), columns(w_up)], axis=2)
    wide = max(width, HEADS * HEAD)
    q_shard = jnp.pad(w_query.astype(BF16), ((0, 0), (0, wide - HEADS * HEAD)))
    o_shard = jnp.pad(w_out.astype(BF16), ((0, 0), (0, wide - width)))
    out_shard = w_out.shape[0]
    qo_shard = jnp.concatenate([o_shard, q_shard])
    pair, qo_shard, kv_along = lax.optimization_barrier((pair, qo_shard, kv_along))
    pair = jnp.transpose(links.exchange(pair), (2, 0, 1, 3, 4)).reshape(2 * sx, sy * shard, units)
    kv_own, pair, qo_shard = lax.optimization_barrier((links.across_plane(kv_along), pair, qo_shard))
    full_kv, gains, heads, seg_all = links.placed(
        kv_shard,
        kv_own,
        (
            (0, shard, 0, 2 * HEAD),
            (shard + rows, 0, shard, 4, True),
            (shard + rows, 4 * shard, head_shard, 2, True),
            (shard, rows, length),
        ),
    )
    h_in, k_proj, kv_low = kv_step(rows, length, tokens_flat, full_kv, gains, heads, cosine, sine)
    kv_low, qo_along = lax.optimization_barrier((kv_low, links.along_z(qo_shard)))
    kv, qo = links.window(
        kv_low,
        length,
        (
            lambda: (links.across_plane(qo_along),),
            lambda qo: (qo[0], links.swap(qo[0], "core") if links.pairs_only else qo[0]),
        ),
    )
    masks = (own_ids, seg_all)
    full_pair = links.gather_cz(pair, 1).reshape(2, width, units)
    full_out, full_query = links.placed(
        qo_shard, qo[0], ((0, out_shard, 0, width), (out_shard, shard, 0, HEADS * HEAD)), qo[1]
    )

    q_proj, query, mixed, attn, resid, h_ffn = attend(
        links, rows, length, h_in, tokens_flat, full_query, full_out, gains, heads, cosine, sine, masks, kv
    )
    parts_up = links.over_plane(h_ffn, lambda part: (part, *ffn_forward(part, full_pair, full_down)))
    h_parts, hidden, turn, act, ffn_terms = zip(*parts_up, strict=True)
    ffn, _ = links.sum_plane(ffn_terms)
    output, d_ffn, sums_ffn = middle(rows, length, ffn, resid, cot_flat, gains)

    pending = list(zip(turn, act, strict=True))

    def back(part):
        return (part, *ffn_backward(part, *pending.pop(0), full_pair, full_down))

    d_parts, d_pairs, d_terms = zip(*links.over_plane(d_ffn, back), strict=True)
    block = sy * shard
    places = sorted(
        (c, (z * sx + x) * block, ((x * sc + c) * sz + z) * block, block)
        for x in range(sx)
        for c in range(sc)
        for z in range(sz)
    )
    half = units // 2
    down_places = [(c, 0, c * half, half) for c in range(sc)]

    def gate_up():
        grad_gate = weight_grads(h_parts, d_pairs, 0, places)
        return (links.sum_cores(*grad_gate), *weight_grads(h_parts, d_pairs, 1, places))

    def up_down(half_gate, *grad_up):
        grad_down = weight_grads(hidden, [part[None] for part in d_parts], 0, down_places)
        return (half_gate, links.sum_cores(*grad_up), *grad_down)

    d_hffn, (half_gate, half_up, *grad_down) = links.sum_plane(d_terms, (gate_up, up_down))

    def owned(sums):
        return links.exchange(sums.reshape(sx, sy, shard, units))

    def unpacked(got):
        got = got.reshape(sx, sy, shard, sc, sz, chunk)[..., :hidden_shard]
        return jnp.transpose(got, (2, 0, 3, 4, 1, 5)).reshape(shard, parts * hidden_shard).astype(F32)

    d_res, d_attn, d_qproj, sums_attn, heads_attn, *terms = attend_back(
        links, rows, length, d_hffn, cot_flat, resid, attn, q_proj, query, full_out, gains, heads, cosine, sine, masks, kv,
        links.window_kinds(length),
    )
    d_kv, beside = links.window_back(
        terms,
        length,
        (
            lambda: (
                links.sum_cores(*outer_grads(links.order("xyz"), (out_shard, shard), mixed, d_attn, h_in, d_qproj)),
                links.sum_cores(*grad_down),
                links.sum_z_low(half_gate),
            ),
            lambda second, low, gate: (second, low, owned(gate)),
            lambda second, low, gate: (links.planes(second), low, unpacked(gate), links.sum_z_low(half_up)),
        ),
    )
    second, low, grad_gate, up = beside[2]

    d_kvproj, grad_tokens, sums_in, heads_in = finish(
        rows, length, d_kv, k_proj, d_qproj, tokens_flat, d_res, full_query, full_kv, gains, heads, cosine, sine
    )
    gain_terms = (sums_ffn + sums_attn + sums_in)[:4]
    head_terms = (heads_attn + heads_in)[:2].reshape(2, parts, head_shard)
    head_terms = jnp.pad(head_terms, ((0, 0), (0, 0), (0, shard - head_shard))).reshape(2, width)
    small_terms = jnp.pad(jnp.concatenate([gain_terms, head_terms]), ((0, SMALL - 6), (0, 0)))
    first_grad = first_grads(links.order("xzy"), shard, h_in, d_kvproj, small_terms)
    first_core, second, got_up = lax.optimization_barrier(
        (links.sum_cores(*first_grad), links.sum_halves(second, "y", 0), owned(up))
    )
    first_sum = links.sum_all_small(first_core)
    second_sum = links.sum_z(second, 0)
    grad_up = unpacked(got_up)
    grad_down = links.sum_z_low(low)[:hidden_shard].astype(F32)
    return (
        output.reshape(tokens.shape),
        grad_tokens.reshape(tokens.shape),
        second_sum[out_shard:, : HEADS * HEAD],
        first_sum[:, SMALL : SMALL + HEAD],
        first_sum[:, SMALL + HEAD :],
        second_sum[:out_shard, :width],
        grad_gate,
        grad_up,
        grad_down,
        *(first_sum[:, k] for k in range(4)),
        *(first_sum[:head_shard, 4 + k] for k in range(2)),
    )


def solution(mesh):
    plane = mesh.shape["dp"] // 2
    by_chip = Mesh(mesh.devices.reshape(plane, 2, -1, plane), AXES)
    links = Links(by_chip)
    placed = P(("x", "core"), ("z", "y"), None)
    matrix = P(AXES, None)
    vector = P(AXES)
    in_specs = (placed, P(("x", "core"), ("z", "y"))) + (matrix,) * 7 + (vector,) * 6 + (placed,)
    out_specs = (placed, placed) + (matrix,) * 7 + (vector,) * 6

    def step(*arguments):
        return on_device(links, *arguments)

    return jax.shard_map(step, mesh=by_chip, in_specs=in_specs, out_specs=out_specs, check_vma=False)
```

```python
import functools
import math

import jax
import jax.numpy as jnp
from jax import lax
from jax.experimental import pallas as pl
from jax.experimental.pallas import tpu as pltpu
from jax.sharding import Mesh
from jax.sharding import PartitionSpec as P

HEADS = 4
HEAD = 256
HALF = HEAD // 2
DOC_LIMIT = 512
EPSILON = 1e-06
ROPE_BASE = 1000000.0
NEG_FILL = -1e30
SCORE_SCALE = HEAD ** (-0.5)
SLOPE = math.sqrt(2.0 / math.pi)
F32 = jnp.float32
BF16 = jnp.bfloat16
PLANE = ("x", "y")
AXES = ("x", "core", "z", "y")
SWAP = [(0, 1), (1, 0)]
IN, POST_ATTN, PRE_FFN, POST_FFN = range(4)
SMALL = 128
ROOM = 58 << 20


def dot(left, right, dims):
    return lax.dot_general(left, right, (dims, ((), ())), preferred_element_type=F32)


def mm(left, right):
    return dot(left, right, ((1,), (0,)))


def mm_t(left, right):
    return dot(left, right, ((1,), (1,)))


def t_mm(left, right):
    return dot(left, right, ((0,), (0,)))


def inv_rms(values):
    return lax.rsqrt(jnp.mean(values * values, axis=-1, keepdims=True) + EPSILON)


def rms_back(values, gain_vec, d_norm):
    scale = inv_rms(values)
    unit = values * scale
    weighted = d_norm * gain_vec
    d_values = scale * (weighted - unit * jnp.mean(weighted * unit, axis=-1, keepdims=True))
    return d_values, d_norm * unit


def rope_tables(positions):
    inverse = ROPE_BASE ** (-(jnp.arange(HALF, dtype=F32) * 2.0 / HEAD))
    angles = positions.astype(F32)[..., None] * inverse
    return jnp.cos(angles), jnp.sin(angles)


def rotate(values, cosine, sine):
    first, second = values[:, :HALF], values[:, HALF:]
    return jnp.concatenate([first * cosine - second * sine, second * cosine + first * sine], axis=-1)


def column_sum(terms):
    return jnp.sum(terms, axis=0, keepdims=True)


def call(body, grid, in_specs, out_specs, out_shape, flops, scratch=()):
    moved = sum(math.prod(one.shape) * one.dtype.itemsize for one in jax.tree.leaves(out_shape))
    return pl.pallas_call(
        body,
        grid=grid,
        in_specs=in_specs,
        out_specs=out_specs,
        out_shape=out_shape,
        scratch_shapes=list(scratch),
        compiler_params=pltpu.CompilerParams(vmem_limit_bytes=ROOM),
        cost_estimate=pl.CostEstimate(flops=flops, bytes_accessed=2 * moved, transcendentals=0),
    )


def shaped(*shape, dtype=F32):
    return jax.ShapeDtypeStruct(shape, dtype)


def whole(*shape):
    return pl.BlockSpec(shape, lambda i: (0,) * len(shape))


def rows_of(tile, width):
    return pl.BlockSpec((tile, width), lambda i: (i, 0))


def row_block(*shape):
    return pl.BlockSpec((1,) + shape, lambda i: (i,) + (0,) * len(shape))


def kv_body(tok_ref, wkv_ref, gains_ref, head_ref, cos_ref, sin_ref, h_ref, kproj_ref, kv_ref):
    tokens = tok_ref[...].astype(F32)
    h = (tokens * inv_rms(tokens) * gains_ref[IN : IN + 1]).astype(BF16)
    h_ref[...] = h
    proj = mm(h, wkv_ref[...])
    k_proj = proj[:, :HEAD]
    kproj_ref[...] = k_proj
    key = rotate(k_proj * inv_rms(k_proj) * head_ref[1:2], cos_ref[...], sin_ref[...])
    kv_ref[0, :, :HEAD] = key.astype(BF16)
    kv_ref[0, :, HEAD:] = proj[:, HEAD:].astype(BF16)


def kv_step(rows, length, tokens, wkv, gains, heads, cosine, sine):
    count, width = tokens.shape
    return call(
        kv_body,
        (rows,),
        [rows_of(length, width), whole(*wkv.shape), whole(*gains.shape), whole(*heads.shape)]
        + [whole(length, HALF)] * 2,
        [rows_of(length, width), rows_of(length, HEAD), row_block(length, 2 * HEAD)],
        [shaped(count, width, dtype=BF16), shaped(count, HEAD), shaped(rows, length, 2 * HEAD, dtype=BF16)],
        2 * count * width * 2 * HEAD,
    )(tokens, wkv, gains, heads, cosine, sine)


def by_head(array):
    return jnp.concatenate([array[:, h * HEAD : (h + 1) * HEAD] for h in range(HEADS)], axis=0)


def by_lane(array):
    part = array.shape[0] // HEADS
    return jnp.concatenate([array[h * part : (h + 1) * part] for h in range(HEADS)], axis=1)


def probs_of(links, query, keys, own_ref, seg_ref):
    length = own_ref.shape[0]
    bases = links.window_bases(length)
    here = links.position(length)
    step = lax.broadcasted_iota(jnp.int32, (1, length), 1)
    segs, later = [], []
    for base in bases:
        row = seg_ref[0, pl.ds(jnp.maximum(base, 0) // length, 1), :]
        segs.append(jnp.where(base >= 0, row, -1.0))
        later.append(base - here + step)
    own_step = lax.broadcasted_iota(jnp.int32, (length, 1), 0)
    allowed = (own_ref[...] == jnp.concatenate(segs, axis=1)) & (jnp.concatenate(later, axis=1) <= own_step)
    allowed = jnp.concatenate([allowed.astype(F32)] * HEADS, axis=0) > 0.5
    scores = jnp.where(allowed, mm_t(query, keys) * SCORE_SCALE, NEG_FILL)
    powers = jnp.exp(scores - jnp.max(scores, axis=-1, keepdims=True))
    return powers / jnp.sum(powers, axis=-1, keepdims=True)


def attend_body(links, blocks, *refs):
    (h_ref, tok_ref, wq_ref, wo_ref, gains_ref, head_ref, cos_ref, sin_ref) = refs[:8]
    masks, kv_refs = refs[8:10], refs[10 : 10 + blocks]
    qproj_ref, query_ref, mixed_ref, attn_ref, resid_ref, hffn_ref = refs[10 + blocks :]
    proj = mm(h_ref[...], wq_ref[...])
    qproj_ref[...] = proj
    cosine, sine = cos_ref[...], sin_ref[...]
    query = []
    for h in range(HEADS):
        one = proj[:, h * HEAD : (h + 1) * HEAD]
        query.append(rotate(one * inv_rms(one) * head_ref[0:1], cosine, sine).astype(BF16))
    query_ref[...] = jnp.concatenate(query, axis=1)
    keys = jnp.concatenate([one[0, :, :HEAD] for one in kv_refs], axis=0)
    values = jnp.concatenate([one[0, :, HEAD:] for one in kv_refs], axis=0)
    probs = probs_of(links, jnp.concatenate(query, axis=0), keys, *masks).astype(BF16)
    mixed = by_lane(mm(probs, values).astype(BF16))
    mixed_ref[...] = mixed
    attn = mm(mixed, wo_ref[...])
    attn_ref[...] = attn
    resid = tok_ref[...].astype(F32) + attn * inv_rms(attn) * gains_ref[POST_ATTN : POST_ATTN + 1]
    resid_ref[...] = resid
    hffn_ref[...] = (resid * inv_rms(resid) * gains_ref[PRE_FFN : PRE_FFN + 1]).astype(BF16)


def mask_specs(masks):
    own, segs = masks
    return [rows_of(own.shape[0] // segs.shape[0], 1), row_block(*segs.shape[1:])]


def attend(links, rows, length, h, tokens, wq, wo, gains, heads, cosine, sine, masks, kv):
    count, width = tokens.shape
    wide = HEADS * HEAD
    window = len(kv) * length
    return call(
        functools.partial(attend_body, links, len(kv)),
        (rows,),
        [rows_of(length, width)] * 2
        + [whole(*one.shape) for one in (wq, wo, gains, heads)]
        + [whole(length, HALF)] * 2
        + mask_specs(masks)
        + [row_block(length, 2 * HEAD)] * len(kv),
        [rows_of(length, wide)] * 3 + [rows_of(length, width)] * 3,
        [
            shaped(count, wide),
            shaped(count, wide, dtype=BF16),
            shaped(count, wide, dtype=BF16),
            shaped(count, width),
            shaped(count, width),
            shaped(count, width, dtype=BF16),
        ],
        4 * count * wide * (width + window),
    )(h, tokens, wq, wo, gains, heads, cosine, sine, *masks, *kv)


def attend_back_body(links, blocks, *refs):
    (dh_ref, cot_ref, resid_ref, attn_ref, qproj_ref, query_ref, wo_ref, gains_ref, head_ref, cos_ref, sin_ref) = refs[:11]
    masks, kv_refs = refs[11:13], refs[13 : 13 + blocks]
    dres_ref, dattn_ref, dq_ref, sums_ref, head_sums_ref = refs[13 + blocks : 18 + blocks]
    term_refs = refs[18 + blocks :]
    d_norm, pre_terms = rms_back(resid_ref[...], gains_ref[PRE_FFN : PRE_FFN + 1], dh_ref[...])
    d_res = cot_ref[...].astype(F32) + d_norm
    dres_ref[...] = d_res
    d_attn, post_terms = rms_back(attn_ref[...], gains_ref[POST_ATTN : POST_ATTN + 1], d_res)
    d_attn = d_attn.astype(BF16)
    dattn_ref[...] = d_attn
    d_mixed = by_head(mm_t(d_attn, wo_ref[...]).astype(BF16))
    query = by_head(query_ref[...])
    keys = jnp.concatenate([one[0, :, :HEAD] for one in kv_refs], axis=0)
    values = jnp.concatenate([one[0, :, HEAD:] for one in kv_refs], axis=0)
    probs = probs_of(links, query, keys, *masks)
    d_probs = mm_t(d_mixed, values)
    d_scores = (probs * (d_probs - jnp.sum(d_probs * probs, axis=-1, keepdims=True))).astype(BF16)
    key_terms = t_mm(d_scores, query) * SCORE_SCALE
    value_terms = t_mm(probs.astype(BF16), d_mixed)
    length = query_ref.shape[0]
    for k, ref in enumerate(term_refs):
        at = slice(k * length, (k + 1) * length)
        ref[0, :, :HEAD] = key_terms[at].astype(ref.dtype)
        ref[0, :, HEAD:] = value_terms[at].astype(ref.dtype)
    d_query = mm(d_scores, keys) * SCORE_SCALE
    cosine, sine = cos_ref[...], -sin_ref[...]
    head_sum = jnp.zeros((1, HEAD), F32)
    for h in range(HEADS):
        turned = rotate(d_query[h * length : (h + 1) * length], cosine, sine)
        lanes = slice(h * HEAD, (h + 1) * HEAD)
        d_proj, terms = rms_back(qproj_ref[:, lanes], head_ref[0:1], turned)
        dq_ref[:, lanes] = d_proj.astype(BF16)
        head_sum += column_sum(terms)

    @pl.when(pl.program_id(0) == 0)
    def _():
        sums_ref[...] = jnp.zeros_like(sums_ref)
        head_sums_ref[...] = jnp.zeros_like(head_sums_ref)

    sums_ref[POST_ATTN : POST_ATTN + 1] += column_sum(post_terms)
    sums_ref[PRE_FFN : PRE_FFN + 1] += column_sum(pre_terms)
    head_sums_ref[0:1] += head_sum


def attend_back(links, rows, length, dh, cot, resid, attn, qproj, query, wo, gains, heads, cosine, sine, masks, kv, kinds):
    count, width = dh.shape
    wide = HEADS * HEAD
    window = len(kv) * length
    return call(
        functools.partial(attend_back_body, links, len(kv)),
        (rows,),
        [rows_of(length, width)] * 4
        + [rows_of(length, wide)] * 2
        + [whole(*one.shape) for one in (wo, gains, heads)]
        + [whole(length, HALF)] * 2
        + mask_specs(masks)
        + [row_block(length, 2 * HEAD)] * len(kv),
        [rows_of(length, width)] * 2
        + [rows_of(length, wide), whole(8, width), whole(8, HEAD)]
        + [row_block(length, 2 * HEAD)] * len(kv),
        [
            shaped(count, width),
            shaped(count, width, dtype=BF16),
            shaped(count, wide, dtype=BF16),
            shaped(8, width),
            shaped(8, HEAD),
        ]
        + [shaped(rows, length, 2 * HEAD, dtype=kind) for kind in kinds],
        2 * count * wide * (width + 5 * window),
    )(dh, cot, resid, attn, qproj, query, wo, gains, heads, cosine, sine, *masks, *kv)


def finish_body(dkv_ref, kproj_ref, dq_ref, tok_ref, dres_ref, wq_ref, wkv_ref, gains_ref, head_ref, cos_ref, sin_ref,
                dkvp_ref, grad_ref, sums_ref, head_sums_ref):
    d_kv = dkv_ref[0]
    turned = rotate(d_kv[:, :HEAD], cos_ref[...], -sin_ref[...])
    d_key, key_terms = rms_back(kproj_ref[...], head_ref[1:2], turned)
    d_proj = jnp.concatenate([d_key.astype(BF16), d_kv[:, HEAD:].astype(BF16)], axis=1)
    dkvp_ref[...] = d_proj
    d_hin = mm_t(dq_ref[...], wq_ref[...]) + mm_t(d_proj, wkv_ref[...])
    d_tokens, in_terms = rms_back(tok_ref[...].astype(F32), gains_ref[IN : IN + 1], d_hin)
    grad_ref[...] = (dres_ref[...] + d_tokens).astype(BF16)

    @pl.when(pl.program_id(0) == 0)
    def _():
        sums_ref[...] = jnp.zeros_like(sums_ref)
        head_sums_ref[...] = jnp.zeros_like(head_sums_ref)

    sums_ref[IN : IN + 1] += column_sum(in_terms)
    head_sums_ref[1:2] += column_sum(key_terms)


def finish(rows, length, dkv, kproj, dq, tokens, dres, wq, wkv, gains, heads, cosine, sine):
    count, width = tokens.shape
    wide = HEADS * HEAD
    return call(
        finish_body,
        (rows,),
        [row_block(length, 2 * HEAD), rows_of(length, HEAD), rows_of(length, wide)]
        + [rows_of(length, width)] * 2
        + [whole(*one.shape) for one in (wq, wkv, gains, heads)]
        + [whole(length, HALF)] * 2,
        [rows_of(length, 2 * HEAD), rows_of(length, width), whole(8, width), whole(8, HEAD)],
        [shaped(count, 2 * HEAD, dtype=BF16), shaped(count, width, dtype=BF16), shaped(8, width), shaped(8, HEAD)],
        2 * count * width * (wide + 2 * HEAD),
    )(dkv, kproj, dq, tokens, dres, wq, wkv, gains, heads, cosine, sine)


def pieces_of(total, step):
    return [(k, min(step, total - k)) for k in range(0, total, step)]


def up_body(step, h_ref, pair_ref, down_ref, hidden_ref, turn_ref, act_ref, out_ref):
    h = h_ref[...]
    for at, wide in pieces_of(hidden_ref.shape[1], step):
        cols = pl.ds(at, wide)
        gate = mm(h, pair_ref[0, :, cols])
        up = mm(h, pair_ref[1, :, cols])
        square = gate * gate
        bent = jnp.tanh(gate * (SLOPE + SLOPE * 0.044715 * square))
        half = 0.5 + 0.5 * bent
        act = gate * half
        d_act = half + 0.5 * gate * (1.0 - bent * bent) * (SLOPE + 3 * SLOPE * 0.044715 * square)
        hidden_ref[:, cols] = (act * up).astype(BF16)
        turn_ref[:, cols] = (up * d_act).astype(BF16)
        act_ref[:, cols] = act.astype(BF16)
    out_ref[...] = mm(hidden_ref[...], down_ref[...]).astype(BF16)


def ffn_forward(h, pair, down, tile=256, step=256):
    count, width = h.shape
    units = pair.shape[2]
    return call(
        functools.partial(up_body, step),
        (count // tile,),
        [rows_of(tile, width), whole(2, width, units), whole(units, width)],
        [rows_of(tile, units)] * 3 + [rows_of(tile, width)],
        [shaped(count, units, dtype=BF16)] * 3 + [shaped(count, width, dtype=BF16)],
        6 * count * width * units,
    )(h, pair, down)


def down_body(step, d_ref, turn_ref, act_ref, pair_ref, down_ref, pair_out, out_ref):
    d = d_ref[...]
    for at, wide in pieces_of(turn_ref.shape[1], step):
        cols = pl.ds(at, wide)
        d_hidden = mm_t(d, down_ref[cols, :])
        pair_out[0, :, cols] = (d_hidden * turn_ref[:, cols].astype(F32)).astype(BF16)
        pair_out[1, :, cols] = (d_hidden * act_ref[:, cols].astype(F32)).astype(BF16)
    out_ref[...] = (mm_t(pair_out[0], pair_ref[0]) + mm_t(pair_out[1], pair_ref[1])).astype(BF16)


def ffn_backward(d, turn, act, pair, down, tile=256, step=256):
    count, width = d.shape
    units = pair.shape[2]
    return call(
        functools.partial(down_body, step),
        (count // tile,),
        [rows_of(tile, width), rows_of(tile, units), rows_of(tile, units), whole(2, width, units), whole(units, width)],
        [pl.BlockSpec((2, tile, units), lambda i: (0, i, 0)), rows_of(tile, width)],
        [shaped(2, count, units, dtype=BF16), shaped(count, width, dtype=BF16)],
        6 * count * width * units,
    )(d, turn, act, pair, down)


def put(kept_ref, sent_ref, core, index, value):
    @pl.when(lax.axis_index("core") == core)
    def _():
        kept_ref[index] = value

    @pl.when(lax.axis_index("core") != core)
    def _():
        sent_ref[index] = value


def grads_body(places, sets, *refs):
    kept_ref, sent_ref = refs[2 * sets :]
    total = None
    for left_ref, right_ref in zip(refs[:sets], refs[sets : 2 * sets], strict=True):
        term = t_mm(left_ref[...], right_ref[0])
        total = term if total is None else total + term
    total = total.astype(BF16)
    tile = total.shape[0]
    for which, moves in enumerate(places):
        for k in range(sum(count for _, _, _, count in moves) // tile):

            @pl.when((pl.program_id(0) == which) & (pl.program_id(1) == k))
            def _(k=k, moves=moves):
                for core, at, row, count in moves:
                    begin, end = max(row, k * tile), min(row + count, (k + 1) * tile)
                    if begin < end:
                        to = at + begin - row
                        index = (slice(to, to + end - begin), slice(None))
                        put(kept_ref, sent_ref, core, index, total[begin - k * tile : end - k * tile])


def weight_grads(lefts, rights, places):
    rows, cols = lefts[0].shape[1], rights[0].shape[2]
    count = sum(one.shape[0] for one in lefts)
    tile = 384 if rows % 384 == 0 else 256
    out = len(places) * rows // 2
    return call(
        functools.partial(grads_body, places, len(lefts)),
        (len(places), rows // tile),
        [pl.BlockSpec((one.shape[0], tile), lambda k, i: (0, i)) for one in lefts]
        + [pl.BlockSpec((1,) + one.shape[1:], lambda k, i: (k, 0, 0)) for one in rights],
        [pl.BlockSpec((out, cols), lambda k, i: (0, 0))] * 2,
        [shaped(out, cols, dtype=BF16)] * 2,
        2 * len(places) * count * rows * cols,
    )(*lefts, *rights)


def outer_body(order, shards, mixed_ref, dattn_ref, h_ref, dq_ref, kept_ref, sent_ref):
    lanes = kept_ref.shape[2]
    at = 0
    for rows, left, right in ((shards[0], mixed_ref, dattn_ref), (shards[1], h_ref, dq_ref)):
        total = t_mm(left[...], right[...]).astype(BF16)
        wide = total.shape[1]
        for core, place, number in order:
            index = (place, slice(at, at + rows), slice(0, wide))
            put(kept_ref, sent_ref, core, index, total[number * rows : (number + 1) * rows])
        if wide < lanes:
            empty = jnp.zeros((kept_ref.shape[0], rows, lanes - wide), BF16)
            kept_ref[:, at : at + rows, wide:] = empty
            sent_ref[:, at : at + rows, wide:] = empty
        at += rows


def outer_grads(order, shards, mixed, d_attn, h, d_q):
    count = mixed.shape[0]
    shape = (len(order) // 2, sum(shards), max(d_attn.shape[1], d_q.shape[1]))
    return call(
        functools.partial(outer_body, order, shards),
        (1,),
        [whole(*one.shape) for one in (mixed, d_attn, h, d_q)],
        [whole(*shape)] * 2,
        [shaped(*shape, dtype=BF16)] * 2,
        2 * count * (mixed.shape[1] * d_attn.shape[1] + h.shape[1] * d_q.shape[1]),
    )(mixed, d_attn, h, d_q)


def first_body(order, shard, h_ref, dkv_ref, small_ref, kept_ref, sent_ref):
    small = small_ref[...].T.astype(BF16)
    total = t_mm(h_ref[...], dkv_ref[...]).astype(BF16)
    for core, place, number in order:
        rows = slice(number * shard, (number + 1) * shard)
        put(kept_ref, sent_ref, core, (place, slice(None), slice(0, SMALL)), small[rows])
        put(kept_ref, sent_ref, core, (place, slice(None), slice(SMALL, None)), total[rows])


def first_grads(order, shard, h, d_kv, small):
    count, rows = h.shape
    shape = (len(order) // 2, shard, d_kv.shape[1] + SMALL)
    return call(
        functools.partial(first_body, order, shard),
        (1,),
        [whole(*one.shape) for one in (h, d_kv, small)],
        [whole(*shape)] * 2,
        [shaped(*shape, dtype=BF16)] * 2,
        2 * count * rows * d_kv.shape[1],
    )(h, d_kv, small)


def middle_body(ffn_ref, resid_ref, cot_ref, gains_ref, out_ref, dffn_ref, sums_ref):
    ffn = ffn_ref[...]
    gain = gains_ref[POST_FFN : POST_FFN + 1]
    out_ref[...] = (resid_ref[...] + ffn * inv_rms(ffn) * gain).astype(BF16)
    d_ffn, terms = rms_back(ffn, gain, cot_ref[...].astype(F32))
    dffn_ref[...] = d_ffn.astype(BF16)

    @pl.when(pl.program_id(0) == 0)
    def _():
        sums_ref[...] = jnp.zeros_like(sums_ref)

    sums_ref[POST_FFN : POST_FFN + 1] += column_sum(terms)


def middle(rows, length, ffn, resid, cot, gains):
    count, width = ffn.shape
    return call(
        middle_body,
        (rows,),
        [rows_of(length, width)] * 3 + [whole(*gains.shape)],
        [rows_of(length, width)] * 2 + [whole(8, width)],
        [shaped(count, width, dtype=BF16), shaped(count, width, dtype=BF16), shaped(8, width)],
        20 * count * width,
    )(ffn, resid, cot, gains)


def place_body(links, shard, parts, own_ref, other_ref, *refs):
    outs, scratch = refs[:-1], refs[-1]
    depth = links.size["z"]
    at_x, at_c, at_z, at_y = (links.index(axis) for axis in AXES)
    number = 0
    for x in range(2):
        for core in range(2):
            for z in range(depth):
                for y in range(2):
                    slot = jnp.abs(at_x - x) + 2 * jnp.abs(at_y - y)
                    slot = slot * depth + jnp.remainder(at_z - z + depth, depth)
                    mine = own_ref[slot].astype(F32)
                    theirs = other_ref[slot].astype(F32)
                    piece = jnp.where(at_c == core, mine, theirs)
                    scratch[number] = piece
                    number += 1
    for part, out in zip(parts, outs, strict=True):
        for k in range(number):
            if len(part) == 4:
                first, count, at, lanes = part
                out[k * count : (k + 1) * count, :] = scratch[k, first : first + count, at : at + lanes].astype(out.dtype)
                continue
            if len(part) == 3:
                first, count, lanes = part
                if k < 2 * depth:
                    ids = scratch[(at_x * 2 + at_c) * 2 * depth + k]
                    for row in range(count):
                        out[row, k : k + 1, :] = ids[first + row : first + row + 1, :lanes]
                continue
            row, at, lanes, vectors = part[:4]
            for v in range(vectors):
                begin = at + v * lanes
                out[v : v + 1, k * lanes : (k + 1) * lanes] = scratch[k, row : row + 1, begin : begin + lanes]


def placed(links, own, other, parts):
    slots, rows, lanes = own.shape
    number = 2 * slots
    return pl.pallas_call(
        functools.partial(place_body, links, rows, parts),
        out_shape=[
            shaped(number * part[1], part[3], dtype=BF16)
            if len(part) == 4
            else shaped(part[1], slots // 2, part[2])
            if len(part) == 3
            else shaped(8, number * part[2])
            for part in parts
        ],
        scratch_shapes=[pltpu.VMEM((number, rows, lanes), F32)],
        compiler_params=pltpu.CompilerParams(vmem_limit_bytes=ROOM),
    )(own, other)


class Links:
    def __init__(self, mesh):
        self.size = dict(mesh.shape)
        self.pairs_only = self.size["x"] == 2 and self.size["y"] == 2

    def index(self, axis):
        return lax.axis_index(axis)

    def swap(self, array, axis):
        return lax.ppermute(array, axis, SWAP)

    def shift(self, array, step):
        depth = self.size["z"]
        pairs = [(i, i + step) for i in range(depth) if 0 <= i + step < depth]
        return lax.ppermute(array, "z", pairs)

    def turn(self, array, step):
        depth = self.size["z"]
        return lax.ppermute(array, "z", [(i, (i + step) % depth) for i in range(depth)])

    def ordered(self, own, other, axis):
        first = self.index(axis) == 0
        return jnp.where(first, jnp.stack([own, other]), jnp.stack([other, own]))

    def along_z(self, array):
        return jnp.stack([array] + [self.turn(array, k) for k in range(1, self.size["z"])])

    def across_plane(self, along):
        if not self.pairs_only:
            return along
        across = lax.ppermute(along, PLANE, [(k, 3 - k) for k in range(4)])
        return jnp.concatenate([along, self.swap(along, "x"), self.swap(along, "y"), across])

    def placed(self, array, own, parts, other=None):
        if self.pairs_only:
            other = self.swap(own, "core") if other is None else other
            return placed(self, own, other, parts)
        full = lax.all_gather(array, AXES, axis=0)
        cuts = []
        for part in parts:
            if len(part) == 4:
                r, n, c, w = part
                cuts.append(full[:, r : r + n, c : c + w].reshape(-1, w))
            elif len(part) == 3:
                r, n, w = part
                blocks = self.size["z"] * self.size["y"]
                at = (self.index("x") * 2 + self.index("core")) * blocks
                ids = lax.dynamic_slice_in_dim(full[:, r : r + n, :w], at, blocks)
                cuts.append(jnp.swapaxes(ids, 0, 1).astype(F32))
            else:
                r, c, w, n = part[:4]
                rows = jnp.swapaxes(full[:, r, c : c + n * w].reshape(-1, n, w), 0, 1).reshape(n, -1)
                cuts.append(jnp.pad(rows.astype(F32), ((0, 8 - n), (0, 0))))
        return cuts

    def order(self, axes):
        found = []
        counts = [self.size[axis] for axis in AXES]
        for number in range(math.prod(counts)):
            at, rest = {}, number
            for axis, many in zip(AXES[::-1], counts[::-1], strict=True):
                at[axis], rest = rest % many, rest // many
            place = 0
            for axis in axes:
                place = place * self.size[axis] + at[axis]
            found.append((at["core"], place, number))
        return found

    def gather_cz(self, array, dim):
        return lax.all_gather(array, ("core", "z"), axis=dim, tiled=True)

    def sum_halves(self, array, axis, dim):
        if self.size[axis] == 2:
            at = self.index(axis)
            sent = self.swap(lax.dynamic_index_in_dim(array, 1 - at, dim, False), axis)
            kept = lax.dynamic_index_in_dim(array, at, dim, False)
            return (kept.astype(F32) + sent.astype(F32)).astype(array.dtype)
        return lax.psum_scatter(array, axis, scatter_dimension=dim, tiled=False)

    def sum_cores(self, kept, sent):
        return (kept.astype(F32) + self.swap(sent, "core").astype(F32)).astype(kept.dtype)

    def sum_z(self, array, dim):
        depth = self.size["z"]
        z = self.index("z")

        def block(k):
            return lax.dynamic_index_in_dim(array, jnp.remainder(z + k, depth), dim, False)

        total = block(0).astype(F32)
        for k in range(1, depth):
            total = total + self.turn(block(k), k).astype(F32)
        return total

    def sum_z_low(self, array):
        return lax.psum_scatter(array, "z", scatter_dimension=0, tiled=True)

    def planes(self, array):
        sx, sy, sz = (self.size[axis] for axis in "xyz")
        return self.sum_halves(array.reshape((sx, sy, sz) + array.shape[1:]), "x", 0)

    def sum_all_small(self, array):
        got = lax.all_to_all(array, ("x", "z", "y"), 0, 0, tiled=True)
        return jnp.sum(got.astype(F32), axis=0)

    def exchange(self, array):
        count = self.size["x"] * self.size["y"]
        flat = array.reshape((count,) + array.shape[2:])
        return lax.all_to_all(flat, PLANE, 0, 0, tiled=True).reshape(array.shape)

    def over_plane(self, rows, first, then=None):
        if not self.pairs_only:
            return [first(lax.all_gather(rows, PLANE, axis=0, tiled=True))]
        half = rows.shape[0] // 2
        upper, lower = lax.optimization_barrier((rows[:half], rows[half:]))
        near = lax.optimization_barrier((self.swap(upper, "x"), self.swap(lower, "y")))
        near = jnp.concatenate([upper, near[0], lower, near[1]])
        upper, lower, near = lax.optimization_barrier((near[: 2 * half], near[2 * half :], near))
        upper, lower, done = lax.optimization_barrier((self.swap(upper, "y"), self.swap(lower, "x"), first(near)))
        return [done, first(jnp.concatenate([upper, lower]))]

    def sum_plane(self, parts, held=(), beside=(None, None)):
        works = [work or (lambda *given: ()) for work in beside]
        if not self.pairs_only:
            total = lax.psum_scatter(parts[0], PLANE, scatter_dimension=0, tiled=True).astype(F32)
            return total, works[1](*works[0](*held))
        near, far = parts
        half = far.shape[0] // 2
        quarter = half // 2
        upper, lower, held = lax.optimization_barrier((far[:half], far[half:], tuple(held)))
        upper, lower, extra = lax.optimization_barrier((self.swap(upper, "y"), self.swap(lower, "x"), works[0](*held)))
        at = [near[k * quarter : (k + 1) * quarter].astype(F32) for k in range(4)]
        own = (at[0] + upper[:quarter].astype(F32), at[2] + lower[:quarter].astype(F32))
        upper = (at[1] + upper[quarter:].astype(F32)).astype(BF16)
        lower = (at[3] + lower[quarter:].astype(F32)).astype(BF16)
        upper, lower, extra = lax.optimization_barrier((upper, lower, extra))
        upper, lower, extra = lax.optimization_barrier((self.swap(upper, "x"), self.swap(lower, "y"), works[1](*extra)))
        return jnp.concatenate([own[0] + upper.astype(F32), own[1] + lower.astype(F32)]), extra

    def position(self, length):
        return (self.index("z") * self.size["y"] + self.index("y")) * length

    def window_bases(self, length):
        z, y, wide = self.index("z"), self.index("y"), self.size["y"]
        span = wide * length
        reach = -(-(DOC_LIMIT - 1) // span)
        base = self.position(length)
        if wide == 2 and reach == 2:
            cross = jnp.where(y == 0, z * span - length, z * span)
            return [base, base - span, base - 2 * span, cross, cross - span]
        return [(z - k) * span + j * length for k in range(reach + 1) for j in range(wide)]

    def window(self, array, length, beside):
        wide = self.size["y"]
        reach = -(-(DOC_LIMIT - 1) // (wide * length))
        if wide == 2 and reach == 2:
            first = self.index("y") == 0
            one, two, extra = lax.optimization_barrier((self.shift(array, 1), self.shift(array, 2), beside[0]()))
            near = self.swap(jnp.where(first, array, one), "y")
            far = self.swap(jnp.where(first, one, two), "y")
            near, far, extra = lax.optimization_barrier((near, far, beside[1](extra)))
            return [array, one, two, near, far], extra
        along = [lax.all_gather(array, "y", axis=0)]
        for _ in range(reach):
            along.append(self.shift(along[-1], 1))
        return [level[j] for level in along for j in range(wide)], beside[1](beside[0]())

    def window_kinds(self, length):
        if self.size["y"] == 2 and 2 * length * 2 >= DOC_LIMIT - 1 > 2 * length:
            return [F32, F32, F32, BF16, BF16]
        return [F32] * len(self.window_bases(length))

    def window_back(self, terms, length, beside=()):
        wide = self.size["y"]
        span = wide * length
        reach = -(-(DOC_LIMIT - 1) // span)
        results = []

        def follow(*arrays):
            if len(results) < len(beside):
                results.append(beside[len(results)](*(results[-1] if results else ())))
                *arrays, results[-1] = lax.optimization_barrier((*arrays, results[-1]))
            return arrays

        if wide == 2 and reach == 2:
            first = self.index("y") == 0
            own, one, two, near, far = terms
            far, near = follow(self.swap(far, "y"), self.swap(near, "y"))
            far, near = far.astype(F32), near.astype(F32)
            two = (two + jnp.where(first, 0.0, far)).astype(BF16)
            one = (one + jnp.where(first, far, near)).astype(BF16)
            two, one = follow(self.shift(two, -2), self.shift(one, -1))
            own = own + jnp.where(first, near, 0.0) + one.astype(F32) + two.astype(F32)
            (own,) = follow(own)
            return own, results
        total = None
        for k in range(reach, -1, -1):
            level = jnp.stack(terms[k * wide : (k + 1) * wide])
            total = level if total is None else level + self.shift(total.astype(BF16), -1).astype(F32)
        total = lax.psum_scatter(total.astype(BF16), "y", scatter_dimension=0, tiled=False).astype(F32)
        for _ in beside:
            (total,) = follow(total)
        return total, results


def on_device(
    links,
    tokens,
    segment_ids,
    w_query,
    w_key,
    w_value,
    w_out,
    w_gate,
    w_up,
    w_down,
    g_in,
    g_post_attn,
    g_pre_ffn,
    g_post_ffn,
    g_query,
    g_key,
    cotangent,
):
    rows, length, width = tokens.shape
    count = rows * length
    size = links.size
    sx, sc, sz, sy = (size[axis] for axis in AXES)
    parts = sx * sc * sz * sy
    shard = w_gate.shape[0]
    hidden_shard = w_down.shape[0]
    chunk = -(-hidden_shard // 16) * 16
    units = sc * sz * chunk
    head_shard = g_query.shape[0]
    tokens_flat = tokens.reshape(count, width)
    cot_flat = cotangent.reshape(count, width)

    step = jnp.arange(length, dtype=jnp.int32)
    pos_own = links.position(length) + step
    cosine, sine = rope_tables(pos_own)

    lanes = 2 * HEAD + SMALL
    vectors = jnp.concatenate([g_in, g_post_attn, g_pre_ffn, g_post_ffn, g_query, g_key])
    vectors = lax.optimization_barrier(jnp.pad(vectors, (0, 2 * HEAD - vectors.shape[0])))[None]
    seg_rows = jnp.pad(segment_ids.astype(F32), ((0, 0), (0, 2 * HEAD - length)))
    kv_shard = jnp.concatenate([jnp.concatenate([w_key, w_value], axis=1), seg_rows, vectors]).astype(BF16)
    own_ids = segment_ids.astype(F32).reshape(count, 1)
    kv_shard, own_ids, w_gate, w_up, w_down, w_query, w_out = lax.optimization_barrier(
        (kv_shard, own_ids, w_gate, w_up, w_down, w_query, w_out)
    )
    kv_along = links.along_z(kv_shard)
    full_down = links.gather_cz(jnp.pad(w_down.astype(BF16), ((0, chunk - hidden_shard), (0, 0))), 0)

    def columns(weight):
        split = weight.astype(BF16).reshape(shard, sx, sc, sz, sy, hidden_shard)
        split = jnp.pad(split, ((0, 0),) * 5 + ((0, chunk - hidden_shard),))
        return jnp.transpose(split, (1, 4, 0, 2, 3, 5)).reshape(sx, sy, shard, units)

    pair = jnp.stack([columns(w_gate), columns(w_up)], axis=2)
    wide = max(width, HEADS * HEAD)
    q_shard = jnp.pad(w_query.astype(BF16), ((0, 0), (0, wide - HEADS * HEAD)))
    o_shard = jnp.pad(w_out.astype(BF16), ((0, 0), (0, wide - width)))
    out_shard = w_out.shape[0]
    qo_shard = jnp.concatenate([o_shard, q_shard])
    pair, qo_shard, kv_along = lax.optimization_barrier((pair, qo_shard, kv_along))
    kv_own, pair, qo_shard = lax.optimization_barrier((links.across_plane(kv_along), pair, qo_shard))
    full_kv, gains, heads, seg_all = links.placed(
        kv_shard,
        kv_own,
        (
            (0, shard, 0, 2 * HEAD),
            (shard + rows, 0, shard, 4, True),
            (shard + rows, 4 * shard, head_shard, 2, True),
            (shard, rows, length),
        ),
    )
    h_in, k_proj, kv_low = kv_step(rows, length, tokens_flat, full_kv, gains, heads, cosine, sine)
    kv_low, qo_along, pair = lax.optimization_barrier((kv_low, links.along_z(qo_shard), links.exchange(pair)))
    pair = jnp.transpose(pair, (2, 0, 1, 3, 4)).reshape(2 * sx, sy * shard, units)
    kv, qo = links.window(
        kv_low,
        length,
        (
            lambda: (links.across_plane(qo_along),),
            lambda qo: (qo[0], links.swap(qo[0], "core") if links.pairs_only else qo[0]),
        ),
    )
    masks = (own_ids, seg_all)
    kv[2], pair = lax.optimization_barrier((kv[2], pair))
    full_pair = links.gather_cz(pair, 1).reshape(2, width, units)
    full_out, full_query = links.placed(
        qo_shard, qo[0], ((0, out_shard, 0, width), (out_shard, shard, 0, HEADS * HEAD)), qo[1]
    )

    q_proj, query, mixed, attn, resid, h_ffn = attend(
        links, rows, length, h_in, tokens_flat, full_query, full_out, gains, heads, cosine, sine, masks, kv
    )
    parts_up = links.over_plane(h_ffn, lambda part: (part, *ffn_forward(part, full_pair, full_down)))
    h_parts, hidden, turn, act, ffn_terms = zip(*parts_up, strict=True)
    ffn, _ = links.sum_plane(ffn_terms)
    output, d_ffn, sums_ffn = middle(rows, length, ffn, resid, cot_flat, gains)

    pending = list(zip(turn, act, strict=True))

    def back(part):
        return (part, *ffn_backward(part, *pending.pop(0), full_pair, full_down))

    d_parts, d_pairs, d_terms = zip(*links.over_plane(d_ffn, back), strict=True)
    block = sy * shard
    places = [
        [
            (c, ((z * 2 + k) * sx + x) * block, ((x * sc + c) * sz + z) * block, block)
            for x in range(sx)
            for c in range(sc)
            for z in range(sz)
        ]
        for k in range(2)
    ]
    half = units // 2
    down_places = [(c, 0, c * half, half) for c in range(sc)]

    def pair_down(kept, sent):
        low = weight_grads(hidden, [part[None] for part in d_parts], [down_places])
        return (kept, links.swap(sent, "core"), *low)

    d_hffn, (kept, got, *grad_down) = links.sum_plane(
        d_terms, d_pairs, (lambda *pairs: weight_grads(h_parts, pairs, places), pair_down)
    )
    d_hffn, half_pair = lax.optimization_barrier((d_hffn, (kept.astype(F32) + got.astype(F32)).astype(BF16)))
    grad_pair = links.sum_z_low(half_pair)

    def by_member(sums):
        return jnp.transpose(sums.reshape(2, sx, sy, shard, units), (1, 2, 0, 3, 4))

    def unpacked(got):
        got = got.reshape(sx, sy, 2, shard, sc, sz, chunk)[..., :hidden_shard]
        return jnp.transpose(got, (2, 3, 0, 4, 5, 1, 6)).reshape(2, shard, parts * hidden_shard).astype(F32)

    d_res, d_attn, d_qproj, sums_attn, heads_attn, *terms = attend_back(
        links, rows, length, d_hffn, cot_flat, resid, attn, q_proj, query, full_out, gains, heads, cosine, sine, masks, kv,
        links.window_kinds(length),
    )
    d_kv, beside = links.window_back(
        terms,
        length,
        (
            lambda: (
                links.sum_cores(*outer_grads(links.order("xyz"), (out_shard, shard), mixed, d_attn, h_in, d_qproj)),
                links.sum_cores(*grad_down),
            ),
            lambda second, low: (links.planes(second), low, grad_pair),
        ),
    )
    second, low, grad_pair = beside[1]
    grad_down = links.sum_z_low(low)[:hidden_shard].astype(F32)

    d_kvproj, grad_tokens, sums_in, heads_in = finish(
        rows, length, d_kv, k_proj, d_qproj, tokens_flat, d_res, full_query, full_kv, gains, heads, cosine, sine
    )
    gain_terms = (sums_ffn + sums_attn + sums_in)[:4]
    head_terms = (heads_attn + heads_in)[:2].reshape(2, parts, head_shard)
    head_terms = jnp.pad(head_terms, ((0, 0), (0, 0), (0, shard - head_shard))).reshape(2, width)
    small_terms = jnp.pad(jnp.concatenate([gain_terms, head_terms]), ((0, SMALL - 6), (0, 0)))
    d_kvproj, second, got_pair = lax.optimization_barrier(
        (d_kvproj, links.sum_halves(second, "y", 0), links.exchange(by_member(grad_pair)))
    )
    first_grad = first_grads(links.order("xzy"), shard, h_in, d_kvproj, small_terms)
    first_core = links.sum_cores(*first_grad)
    first_sum = links.sum_all_small(first_core)
    second_sum = links.sum_z(second, 0)
    grad_pair = unpacked(got_pair)
    return (
        output.reshape(tokens.shape),
        grad_tokens.reshape(tokens.shape),
        second_sum[out_shard:, : HEADS * HEAD],
        first_sum[:, SMALL : SMALL + HEAD],
        first_sum[:, SMALL + HEAD :],
        second_sum[:out_shard, :width],
        grad_pair[0],
        grad_pair[1],
        grad_down,
        *(first_sum[:, k] for k in range(4)),
        *(first_sum[:head_shard, 4 + k] for k in range(2)),
    )


def solution(mesh):
    plane = mesh.shape["dp"] // 2
    by_chip = Mesh(mesh.devices.reshape(plane, 2, -1, plane), AXES)
    links = Links(by_chip)
    placed = P(("x", "core"), ("z", "y"), None)
    matrix = P(AXES, None)
    vector = P(AXES)
    in_specs = (placed, P(("x", "core"), ("z", "y"))) + (matrix,) * 7 + (vector,) * 6 + (placed,)
    out_specs = (placed, placed) + (matrix,) * 7 + (vector,) * 6

    def step(*arguments):
        return on_device(links, *arguments)

    return jax.shard_map(step, mesh=by_chip, in_specs=in_specs, out_specs=out_specs, check_vma=False)
```

```python
import functools
import math

import jax
import jax.numpy as jnp
from jax import lax
from jax.experimental import pallas as pl
from jax.experimental.pallas import tpu as pltpu
from jax.sharding import Mesh
from jax.sharding import PartitionSpec as P

HEADS = 4
HEAD = 256
HALF = HEAD // 2
DOC_LIMIT = 512
EPSILON = 1e-06
ROPE_BASE = 1000000.0
NEG_FILL = -1e30
SCORE_SCALE = HEAD ** (-0.5)
SLOPE = math.sqrt(2.0 / math.pi)
F32 = jnp.float32
BF16 = jnp.bfloat16
PLANE = ("x", "y")
AXES = ("x", "core", "z", "y")
SWAP = [(0, 1), (1, 0)]
IN, POST_ATTN, PRE_FFN, POST_FFN = range(4)
SMALL = 128
ROOM = 58 << 20


def dot(left, right, dims):
    return lax.dot_general(left, right, (dims, ((), ())), preferred_element_type=F32)


def mm(left, right):
    return dot(left, right, ((1,), (0,)))


def mm_t(left, right):
    return dot(left, right, ((1,), (1,)))


def t_mm(left, right):
    return dot(left, right, ((0,), (0,)))


def inv_rms(values):
    return lax.rsqrt(jnp.mean(values * values, axis=-1, keepdims=True) + EPSILON)


def rms_back(values, gain_vec, d_norm):
    scale = inv_rms(values)
    unit = values * scale
    weighted = d_norm * gain_vec
    d_values = scale * (weighted - unit * jnp.mean(weighted * unit, axis=-1, keepdims=True))
    return d_values, d_norm * unit


def rope_tables(positions):
    inverse = ROPE_BASE ** (-(jnp.arange(HALF, dtype=F32) * 2.0 / HEAD))
    angles = positions.astype(F32)[..., None] * inverse
    return jnp.cos(angles), jnp.sin(angles)


def rotate(values, cosine, sine):
    first, second = values[:, :HALF], values[:, HALF:]
    return jnp.concatenate([first * cosine - second * sine, second * cosine + first * sine], axis=-1)


def eights(rows):
    return -(-rows // 8) * 8


def column_sum(terms):
    return jnp.sum(terms, axis=0, keepdims=True)


def call(body, grid, in_specs, out_specs, out_shape, flops, scratch=()):
    moved = sum(math.prod(one.shape) * one.dtype.itemsize for one in jax.tree.leaves(out_shape))
    return pl.pallas_call(
        body,
        grid=grid,
        in_specs=in_specs,
        out_specs=out_specs,
        out_shape=out_shape,
        scratch_shapes=list(scratch),
        compiler_params=pltpu.CompilerParams(vmem_limit_bytes=ROOM),
        cost_estimate=pl.CostEstimate(flops=flops, bytes_accessed=2 * moved, transcendentals=0),
    )


def shaped(*shape, dtype=F32):
    return jax.ShapeDtypeStruct(shape, dtype)


def whole(*shape):
    return pl.BlockSpec(shape, lambda i: (0,) * len(shape))


def rows_of(tile, width):
    return pl.BlockSpec((tile, width), lambda i: (i, 0))


def row_block(*shape):
    return pl.BlockSpec((1,) + shape, lambda i: (i,) + (0,) * len(shape))


def part_specs(tile, width, arrays):
    if len(arrays) == 1:
        return [rows_of(tile, width)]
    half = arrays[0].shape[0] // tile
    return [
        pl.BlockSpec((tile, width), lambda i: (jnp.minimum(i, half - 1), 0)),
        pl.BlockSpec((tile, width), lambda i: (jnp.maximum(i - half, 0), 0)),
    ]


def in_second():
    return pl.program_id(0) >= pl.num_programs(0) // 2


def load_part(refs):
    if len(refs) == 1:
        return refs[0][...]
    return lax.select_n(in_second(), refs[0][...], refs[1][...])


def store_part(refs, value):
    if len(refs) == 1:
        refs[0][...] = value
        return

    @pl.when(in_second() == False)
    def _():
        refs[0][...] = value

    @pl.when(in_second())
    def _():
        refs[1][...] = value


def kv_body(tok_ref, wkv_ref, gains_ref, head_ref, cos_ref, sin_ref, h_ref, kproj_ref, kv_ref):
    tokens = tok_ref[...].astype(F32)
    h = (tokens * inv_rms(tokens) * gains_ref[IN : IN + 1]).astype(BF16)
    h_ref[...] = h
    proj = mm(h, wkv_ref[...])
    k_proj = proj[:, :HEAD]
    kproj_ref[...] = k_proj
    key = rotate(k_proj * inv_rms(k_proj) * head_ref[1:2], cos_ref[...], sin_ref[...])
    kv_ref[0, :, :HEAD] = key.astype(BF16)
    kv_ref[0, :, HEAD:] = proj[:, HEAD:].astype(BF16)


def kv_step(rows, length, tokens, wkv, gains, heads, cosine, sine):
    count, width = tokens.shape
    return call(
        kv_body,
        (rows,),
        [rows_of(length, width), whole(*wkv.shape), whole(*gains.shape), whole(*heads.shape)]
        + [whole(length, HALF)] * 2,
        [rows_of(length, width), rows_of(length, HEAD), row_block(length, 2 * HEAD)],
        [shaped(count, width, dtype=BF16), shaped(count, HEAD), shaped(rows, length, 2 * HEAD, dtype=BF16)],
        2 * count * width * 2 * HEAD,
    )(tokens, wkv, gains, heads, cosine, sine)


def by_head(array):
    return jnp.concatenate([array[:, h * HEAD : (h + 1) * HEAD] for h in range(HEADS)], axis=0)


def by_lane(array):
    part = array.shape[0] // HEADS
    return jnp.concatenate([array[h * part : (h + 1) * part] for h in range(HEADS)], axis=1)


def probs_of(links, query, keys, own_ref, seg_ref):
    length = own_ref.shape[0]
    bases = links.window_bases(length)
    here = links.position(length)
    step = lax.broadcasted_iota(jnp.int32, (1, length), 1)
    segs, later = [], []
    for base in bases:
        row = seg_ref[0, pl.ds(jnp.maximum(base, 0) // length, 1), :]
        segs.append(jnp.where(base >= 0, row, -1.0))
        later.append(base - here + step)
    own_step = lax.broadcasted_iota(jnp.int32, (length, 1), 0)
    allowed = (own_ref[...] == jnp.concatenate(segs, axis=1)) & (jnp.concatenate(later, axis=1) <= own_step)
    allowed = jnp.concatenate([allowed.astype(F32)] * HEADS, axis=0) > 0.5
    scores = jnp.where(allowed, mm_t(query, keys) * SCORE_SCALE, NEG_FILL)
    powers = jnp.exp(scores - jnp.max(scores, axis=-1, keepdims=True))
    return powers / jnp.sum(powers, axis=-1, keepdims=True)


def attend_body(links, blocks, *refs):
    (h_ref, tok_ref, wq_ref, wo_ref, gains_ref, head_ref, cos_ref, sin_ref) = refs[:8]
    masks, kv_refs = refs[8:10], refs[10 : 10 + blocks]
    qproj_ref, query_ref, mixed_ref, attn_ref, resid_ref, *hffn_refs = refs[10 + blocks :]
    proj = mm(h_ref[...], wq_ref[...])
    qproj_ref[...] = proj
    cosine, sine = cos_ref[...], sin_ref[...]
    query = []
    for h in range(HEADS):
        one = proj[:, h * HEAD : (h + 1) * HEAD]
        query.append(rotate(one * inv_rms(one) * head_ref[0:1], cosine, sine).astype(BF16))
    query_ref[...] = jnp.concatenate(query, axis=1)
    keys = jnp.concatenate([one[0, :, :HEAD] for one in kv_refs], axis=0)
    values = jnp.concatenate([one[0, :, HEAD:] for one in kv_refs], axis=0)
    probs = probs_of(links, jnp.concatenate(query, axis=0), keys, *masks).astype(BF16)
    mixed = by_lane(mm(probs, values).astype(BF16))
    mixed_ref[...] = mixed
    attn = mm(mixed, wo_ref[...])
    attn_ref[...] = attn
    resid = tok_ref[...].astype(F32) + attn * inv_rms(attn) * gains_ref[POST_ATTN : POST_ATTN + 1]
    resid_ref[...] = resid
    store_part(hffn_refs, (resid * inv_rms(resid) * gains_ref[PRE_FFN : PRE_FFN + 1]).astype(BF16))


def mask_specs(masks):
    own, segs = masks
    return [rows_of(own.shape[0] // segs.shape[0], 1), row_block(*segs.shape[1:])]


def attend(links, rows, length, h, tokens, wq, wo, gains, heads, cosine, sine, masks, kv):
    count, width = tokens.shape
    wide = HEADS * HEAD
    window = len(kv) * length
    halves = [shaped(count // 2, width, dtype=BF16)] * 2
    return call(
        functools.partial(attend_body, links, len(kv)),
        (rows,),
        [rows_of(length, width)] * 2
        + [whole(*one.shape) for one in (wq, wo, gains, heads)]
        + [whole(length, HALF)] * 2
        + mask_specs(masks)
        + [row_block(length, 2 * HEAD)] * len(kv),
        [rows_of(length, wide)] * 3 + [rows_of(length, width)] * 2 + part_specs(length, width, halves),
        [
            shaped(count, wide),
            shaped(count, wide, dtype=BF16),
            shaped(count, wide, dtype=BF16),
            shaped(count, width),
            shaped(count, width),
            *halves,
        ],
        4 * count * wide * (width + window),
    )(h, tokens, wq, wo, gains, heads, cosine, sine, *masks, *kv)


def attend_back_body(links, blocks, *refs):
    own_refs, far_refs, refs = refs[:2], refs[2:4], refs[4:]
    (cot_ref, resid_ref, attn_ref, qproj_ref, query_ref, wo_ref, gains_ref, head_ref, cos_ref, sin_ref) = refs[:10]
    masks, kv_refs = refs[10:12], refs[12 : 12 + blocks]
    dres_ref, dattn_ref, dq_ref, sums_ref, head_sums_ref = refs[12 + blocks : 17 + blocks]
    term_refs = refs[17 + blocks :]
    d_norm, pre_terms = rms_back(resid_ref[...], gains_ref[PRE_FFN : PRE_FFN + 1], load_part(own_refs) + load_part(far_refs).astype(F32))
    d_res = cot_ref[...].astype(F32) + d_norm
    dres_ref[...] = d_res
    d_attn, post_terms = rms_back(attn_ref[...], gains_ref[POST_ATTN : POST_ATTN + 1], d_res)
    d_attn = d_attn.astype(BF16)
    dattn_ref[...] = d_attn
    d_mixed = by_head(mm_t(d_attn, wo_ref[...]).astype(BF16))
    query = by_head(query_ref[...])
    keys = jnp.concatenate([one[0, :, :HEAD] for one in kv_refs], axis=0)
    values = jnp.concatenate([one[0, :, HEAD:] for one in kv_refs], axis=0)
    probs = probs_of(links, query, keys, *masks)
    d_probs = mm_t(d_mixed, values)
    d_scores = (probs * (d_probs - jnp.sum(d_probs * probs, axis=-1, keepdims=True))).astype(BF16)
    key_terms = t_mm(d_scores, query) * SCORE_SCALE
    value_terms = t_mm(probs.astype(BF16), d_mixed)
    length = query_ref.shape[0]
    for k, ref in enumerate(term_refs):
        at = slice(k * length, (k + 1) * length)
        ref[0, :, :HEAD] = key_terms[at].astype(ref.dtype)
        ref[0, :, HEAD:] = value_terms[at].astype(ref.dtype)
    d_query = mm(d_scores, keys) * SCORE_SCALE
    cosine, sine = cos_ref[...], -sin_ref[...]
    head_sum = jnp.zeros((1, HEAD), F32)
    for h in range(HEADS):
        turned = rotate(d_query[h * length : (h + 1) * length], cosine, sine)
        lanes = slice(h * HEAD, (h + 1) * HEAD)
        d_proj, terms = rms_back(qproj_ref[:, lanes], head_ref[0:1], turned)
        dq_ref[:, lanes] = d_proj.astype(BF16)
        head_sum += column_sum(terms)

    @pl.when(pl.program_id(0) == 0)
    def _():
        sums_ref[...] = jnp.zeros_like(sums_ref)
        head_sums_ref[...] = jnp.zeros_like(head_sums_ref)

    sums_ref[POST_ATTN : POST_ATTN + 1] += column_sum(post_terms)
    sums_ref[PRE_FFN : PRE_FFN + 1] += column_sum(pre_terms)
    head_sums_ref[0:1] += head_sum


def attend_back(links, rows, length, own, far, cot, resid, attn, qproj, query, wo, gains, heads, cosine, sine, masks, kv, kinds):
    count, width = cot.shape
    wide = HEADS * HEAD
    window = len(kv) * length
    return call(
        functools.partial(attend_back_body, links, len(kv)),
        (rows,),
        part_specs(length, width, own) * 2
        + [rows_of(length, width)] * 3
        + [rows_of(length, wide)] * 2
        + [whole(*one.shape) for one in (wo, gains, heads)]
        + [whole(length, HALF)] * 2
        + mask_specs(masks)
        + [row_block(length, 2 * HEAD)] * len(kv),
        [rows_of(length, width)] * 2
        + [rows_of(length, wide), whole(8, width), whole(8, HEAD)]
        + [row_block(length, 2 * HEAD)] * len(kv),
        [
            shaped(count, width),
            shaped(count, width, dtype=BF16),
            shaped(count, wide, dtype=BF16),
            shaped(8, width),
            shaped(8, HEAD),
        ]
        + [shaped(rows, length, 2 * HEAD, dtype=kind) for kind in kinds],
        2 * count * wide * (width + 5 * window),
    )(*own, *far, cot, resid, attn, qproj, query, wo, gains, heads, cosine, sine, *masks, *kv)


def finish_body(dkv_ref, kproj_ref, dq_ref, tok_ref, dres_ref, wq_ref, wkv_ref, gains_ref, head_ref, cos_ref, sin_ref,
                dkvp_ref, grad_ref, sums_ref, head_sums_ref):
    d_kv = dkv_ref[0]
    turned = rotate(d_kv[:, :HEAD], cos_ref[...], -sin_ref[...])
    d_key, key_terms = rms_back(kproj_ref[...], head_ref[1:2], turned)
    d_proj = jnp.concatenate([d_key.astype(BF16), d_kv[:, HEAD:].astype(BF16)], axis=1)
    dkvp_ref[...] = d_proj
    d_hin = mm_t(dq_ref[...], wq_ref[...]) + mm_t(d_proj, wkv_ref[...])
    d_tokens, in_terms = rms_back(tok_ref[...].astype(F32), gains_ref[IN : IN + 1], d_hin)
    grad_ref[...] = (dres_ref[...] + d_tokens).astype(BF16)

    @pl.when(pl.program_id(0) == 0)
    def _():
        sums_ref[...] = jnp.zeros_like(sums_ref)
        head_sums_ref[...] = jnp.zeros_like(head_sums_ref)

    sums_ref[IN : IN + 1] += column_sum(in_terms)
    head_sums_ref[1:2] += column_sum(key_terms)


def finish(rows, length, dkv, kproj, dq, tokens, dres, wq, wkv, gains, heads, cosine, sine):
    count, width = tokens.shape
    wide = HEADS * HEAD
    return call(
        finish_body,
        (rows,),
        [row_block(length, 2 * HEAD), rows_of(length, HEAD), rows_of(length, wide)]
        + [rows_of(length, width)] * 2
        + [whole(*one.shape) for one in (wq, wkv, gains, heads)]
        + [whole(length, HALF)] * 2,
        [rows_of(length, 2 * HEAD), rows_of(length, width), whole(8, width), whole(8, HEAD)],
        [shaped(count, 2 * HEAD, dtype=BF16), shaped(count, width, dtype=BF16), shaped(8, width), shaped(8, HEAD)],
        2 * count * width * (wide + 2 * HEAD),
    )(dkv, kproj, dq, tokens, dres, wq, wkv, gains, heads, cosine, sine)


def pieces_of(total, step):
    return [(k, min(step, total - k)) for k in range(0, total, step)]


def up_body(step, many, *refs):
    pair_ref, down_ref, hidden_ref, turn_ref, act_ref = refs[many : many + 5]
    h = load_part(refs[:many])
    for at, wide in pieces_of(hidden_ref.shape[1], step):
        cols = pl.ds(at, wide)
        gate = mm(h, pair_ref[0, :, cols])
        up = mm(h, pair_ref[1, :, cols])
        square = gate * gate
        bent = jnp.tanh(gate * (SLOPE + SLOPE * 0.044715 * square))
        half = 0.5 + 0.5 * bent
        act = gate * half
        d_act = half + 0.5 * gate * (1.0 - bent * bent) * (SLOPE + 3 * SLOPE * 0.044715 * square)
        hidden_ref[:, cols] = (act * up).astype(BF16)
        turn_ref[:, cols] = (up * d_act).astype(BF16)
        act_ref[:, cols] = act.astype(BF16)
    store_part(refs[many + 5 :], mm(hidden_ref[...], down_ref[...]).astype(BF16))


def ffn_forward(h, pair, down, tile=256, step=256):
    count, width = sum(one.shape[0] for one in h), h[0].shape[1]
    units = pair.shape[2]
    specs = part_specs(tile, width, h)
    hidden, turn, act, *terms = call(
        functools.partial(up_body, step, len(h)),
        (count // tile,),
        specs + [whole(2, width, units), whole(units, width)],
        [rows_of(tile, units)] * 3 + specs,
        [shaped(count, units, dtype=BF16)] * 3 + [shaped(*one.shape, dtype=BF16) for one in h],
        6 * count * width * units,
    )(*h, pair, down)
    return hidden, turn, act, terms


def down_body(step, many, *refs):
    turn_ref, act_ref, pair_ref, down_ref, pair_out = refs[many : many + 5]
    d = load_part(refs[:many])
    for at, wide in pieces_of(turn_ref.shape[1], step):
        cols = pl.ds(at, wide)
        d_hidden = mm_t(d, down_ref[cols, :])
        pair_out[0, :, cols] = (d_hidden * turn_ref[:, cols].astype(F32)).astype(BF16)
        pair_out[1, :, cols] = (d_hidden * act_ref[:, cols].astype(F32)).astype(BF16)
    store_part(refs[many + 5 :], (mm_t(pair_out[0], pair_ref[0]) + mm_t(pair_out[1], pair_ref[1])).astype(BF16))


def ffn_backward(d, turn, act, pair, down, tile=256, step=256):
    count, width = sum(one.shape[0] for one in d), d[0].shape[1]
    units = pair.shape[2]
    specs = part_specs(tile, width, d)
    d_pair, *terms = call(
        functools.partial(down_body, step, len(d)),
        (count // tile,),
        specs + [rows_of(tile, units), rows_of(tile, units), whole(2, width, units), whole(units, width)],
        [pl.BlockSpec((2, tile, units), lambda i: (0, i, 0))] + specs,
        [shaped(2, count, units, dtype=BF16)] + [shaped(*one.shape, dtype=BF16) for one in d],
        6 * count * width * units,
    )(*d, turn, act, pair, down)
    return d_pair, terms


def put(kept_ref, sent_ref, core, index, value):
    @pl.when(lax.axis_index("core") == core)
    def _():
        kept_ref[index] = value

    @pl.when(lax.axis_index("core") != core)
    def _():
        sent_ref[index] = value


def grads_body(places, sets, *refs):
    kept_ref, sent_ref = refs[-2:]
    total, at = None, 0
    for lefts, rights in sets:
        values = []
        for many in (lefts, rights):
            pieces = [ref[...] if len(ref.shape) == 2 else ref[0] for ref in refs[at : at + many]]
            values.append(jnp.concatenate(pieces, axis=0) if many > 1 else pieces[0])
            at += many
        term = t_mm(*values)
        total = term if total is None else total + term
    total = total.astype(BF16)
    tile = total.shape[0]
    for which, moves in enumerate(places):
        for k in range(sum(count for _, _, _, count in moves) // tile):

            @pl.when((pl.program_id(0) == which) & (pl.program_id(1) == k))
            def _(k=k, moves=moves):
                for core, at, row, count in moves:
                    begin, end = max(row, k * tile), min(row + count, (k + 1) * tile)
                    if begin < end:
                        to = at + begin - row
                        index = (slice(to, to + end - begin), slice(None))
                        put(kept_ref, sent_ref, core, index, total[begin - k * tile : end - k * tile])


def weight_grads(sets, places):
    rows, cols = sets[0][0][0].shape[1], sets[0][1][0].shape[2]
    count = sum(one.shape[0] for lefts, _ in sets for one in lefts)
    tile = 384 if rows % 384 == 0 else 256
    out = len(places) * rows // 2
    specs, arrays = [], []
    for lefts, rights in sets:
        specs += [pl.BlockSpec((one.shape[0], tile), lambda k, i: (0, i)) for one in lefts]
        specs += [pl.BlockSpec((1,) + one.shape[1:], lambda k, i: (k, 0, 0)) for one in rights]
        arrays += [*lefts, *rights]
    return call(
        functools.partial(grads_body, places, [(len(lefts), len(rights)) for lefts, rights in sets]),
        (len(places), rows // tile),
        specs,
        [pl.BlockSpec((out, cols), lambda k, i: (0, 0))] * 2,
        [shaped(out, cols, dtype=BF16)] * 2,
        2 * len(places) * count * rows * cols,
    )(*arrays)


def outer_body(order, shards, mixed_ref, dattn_ref, h_ref, dq_ref, kept_ref, sent_ref):
    lanes = kept_ref.shape[2]
    at = 0
    for rows, left, right in ((shards[0], mixed_ref, dattn_ref), (shards[1], h_ref, dq_ref)):
        total = t_mm(left[...], right[...]).astype(BF16)
        wide = total.shape[1]
        for core, place, number in order:
            index = (place, slice(at, at + rows), slice(0, wide))
            put(kept_ref, sent_ref, core, index, total[number * rows : (number + 1) * rows])
        for ref in (kept_ref, sent_ref):
            if wide < lanes:
                ref[:, at : at + rows, wide:] = jnp.zeros((ref.shape[0], rows, lanes - wide), BF16)
        at += rows
    for ref in (kept_ref, sent_ref):
        if at < ref.shape[1]:
            ref[:, at:, :] = jnp.zeros((ref.shape[0], ref.shape[1] - at, lanes), BF16)


def outer_grads(order, shards, mixed, d_attn, h, d_q):
    count = mixed.shape[0]
    shape = (len(order) // 2, eights(sum(shards)), max(d_attn.shape[1], d_q.shape[1]))
    return call(
        functools.partial(outer_body, order, shards),
        (1,),
        [whole(*one.shape) for one in (mixed, d_attn, h, d_q)],
        [whole(*shape)] * 2,
        [shaped(*shape, dtype=BF16)] * 2,
        2 * count * (mixed.shape[1] * d_attn.shape[1] + h.shape[1] * d_q.shape[1]),
    )(mixed, d_attn, h, d_q)


def first_body(order, shard, h_ref, dkv_ref, small_ref, kept_ref, sent_ref):
    small = small_ref[...].T.astype(BF16)
    total = t_mm(h_ref[...], dkv_ref[...]).astype(BF16)
    for core, place, number in order:
        rows = slice(number * shard, (number + 1) * shard)
        put(kept_ref, sent_ref, core, (place, slice(0, shard), slice(0, SMALL)), small[rows])
        put(kept_ref, sent_ref, core, (place, slice(0, shard), slice(SMALL, None)), total[rows])
    for ref in (kept_ref, sent_ref):
        if shard < ref.shape[1]:
            ref[:, shard:, :] = jnp.zeros((ref.shape[0], ref.shape[1] - shard, ref.shape[2]), BF16)


def first_grads(order, shard, h, d_kv, small):
    count, rows = h.shape
    shape = (len(order) // 2, eights(shard), d_kv.shape[1] + SMALL)
    return call(
        functools.partial(first_body, order, shard),
        (1,),
        [whole(*one.shape) for one in (h, d_kv, small)],
        [whole(*shape)] * 2,
        [shaped(*shape, dtype=BF16)] * 2,
        2 * count * rows * d_kv.shape[1],
    )(h, d_kv, small)


def middle_body(own_a, own_b, far_a, far_b, resid_ref, cot_ref, gains_ref, out_ref, dffn_a, dffn_b, sums_ref):
    ffn = load_part((own_a, own_b)) + load_part((far_a, far_b)).astype(F32)
    gain = gains_ref[POST_FFN : POST_FFN + 1]
    out_ref[...] = (resid_ref[...] + ffn * inv_rms(ffn) * gain).astype(BF16)
    d_ffn, terms = rms_back(ffn, gain, cot_ref[...].astype(F32))
    store_part((dffn_a, dffn_b), d_ffn.astype(BF16))

    @pl.when(pl.program_id(0) == 0)
    def _():
        sums_ref[...] = jnp.zeros_like(sums_ref)

    sums_ref[POST_FFN : POST_FFN + 1] += column_sum(terms)


def middle(rows, length, own, far, resid, cot, gains):
    count, width = resid.shape
    specs = part_specs(length, width, own)
    return call(
        middle_body,
        (rows,),
        specs * 2 + [rows_of(length, width)] * 2 + [whole(*gains.shape)],
        [rows_of(length, width)] + specs + [whole(8, width)],
        [shaped(count, width, dtype=BF16)] + [shaped(count // 2, width, dtype=BF16)] * 2 + [shaped(8, width)],
        20 * count * width,
    )(*own, *far, resid, cot, gains)


def place_body(links, shard, parts, own_ref, other_ref, *refs):
    outs, scratch = refs[:-1], refs[-1]
    depth = links.size["z"]
    at_x, at_c, at_z, at_y = (links.index(axis) for axis in AXES)
    number = 0
    for x in range(2):
        for core in range(2):
            for z in range(depth):
                for y in range(2):
                    slot = jnp.abs(at_x - x) + 2 * jnp.abs(at_y - y)
                    slot = slot * depth + jnp.remainder(at_z - z + depth, depth)
                    mine = own_ref[slot].astype(F32)
                    theirs = other_ref[slot].astype(F32)
                    piece = jnp.where(at_c == core, mine, theirs)
                    scratch[number] = piece
                    number += 1
    for part, out in zip(parts, outs, strict=True):
        for k in range(number):
            if len(part) == 4:
                first, count, at, lanes = part
                out[k * count : (k + 1) * count, :] = scratch[k, first : first + count, at : at + lanes].astype(out.dtype)
                continue
            if len(part) == 3:
                first, count, lanes = part
                if k < 2 * depth:
                    ids = scratch[(at_x * 2 + at_c) * 2 * depth + k]
                    for row in range(count):
                        out[row, k : k + 1, :] = ids[first + row : first + row + 1, :lanes]
                continue
            row, at, lanes, vectors = part[:4]
            for v in range(vectors):
                begin = at + v * lanes
                out[v : v + 1, k * lanes : (k + 1) * lanes] = scratch[k, row : row + 1, begin : begin + lanes]


def placed(links, own, other, parts):
    slots, rows, lanes = own.shape
    number = 2 * slots
    return pl.pallas_call(
        functools.partial(place_body, links, rows, parts),
        out_shape=[
            shaped(number * part[1], part[3], dtype=BF16)
            if len(part) == 4
            else shaped(part[1], slots // 2, part[2])
            if len(part) == 3
            else shaped(8, number * part[2])
            for part in parts
        ],
        scratch_shapes=[pltpu.VMEM((number, rows, lanes), F32)],
        compiler_params=pltpu.CompilerParams(vmem_limit_bytes=ROOM),
    )(own, other)


class Links:
    def __init__(self, mesh):
        self.size = dict(mesh.shape)
        self.pairs_only = self.size["x"] == 2 and self.size["y"] == 2

    def index(self, axis):
        return lax.axis_index(axis)

    def swap(self, array, axis):
        return lax.ppermute(array, axis, SWAP)

    def shift(self, array, step):
        depth = self.size["z"]
        pairs = [(i, i + step) for i in range(depth) if 0 <= i + step < depth]
        return lax.ppermute(array, "z", pairs)

    def turn(self, array, step):
        depth = self.size["z"]
        return lax.ppermute(array, "z", [(i, (i + step) % depth) for i in range(depth)])

    def ordered(self, own, other, axis):
        first = self.index(axis) == 0
        return jnp.where(first, jnp.stack([own, other]), jnp.stack([other, own]))

    def along_z(self, array):
        return jnp.stack([array] + [self.turn(array, k) for k in range(1, self.size["z"])])

    def across_plane(self, along):
        if not self.pairs_only:
            return along
        across = lax.ppermute(along, PLANE, [(k, 3 - k) for k in range(4)])
        return jnp.concatenate([along, self.swap(along, "x"), self.swap(along, "y"), across])

    def placed(self, array, own, parts, other=None):
        if self.pairs_only:
            other = self.swap(own, "core") if other is None else other
            return placed(self, own, other, parts)
        full = lax.all_gather(array, AXES, axis=0)
        cuts = []
        for part in parts:
            if len(part) == 4:
                r, n, c, w = part
                cuts.append(full[:, r : r + n, c : c + w].reshape(-1, w))
            elif len(part) == 3:
                r, n, w = part
                blocks = self.size["z"] * self.size["y"]
                at = (self.index("x") * 2 + self.index("core")) * blocks
                ids = lax.dynamic_slice_in_dim(full[:, r : r + n, :w], at, blocks)
                cuts.append(jnp.swapaxes(ids, 0, 1).astype(F32))
            else:
                r, c, w, n = part[:4]
                rows = jnp.swapaxes(full[:, r, c : c + n * w].reshape(-1, n, w), 0, 1).reshape(n, -1)
                cuts.append(jnp.pad(rows.astype(F32), ((0, 8 - n), (0, 0))))
        return cuts

    def order(self, axes):
        found = []
        counts = [self.size[axis] for axis in AXES]
        for number in range(math.prod(counts)):
            at, rest = {}, number
            for axis, many in zip(AXES[::-1], counts[::-1], strict=True):
                at[axis], rest = rest % many, rest // many
            place = 0
            for axis in axes:
                place = place * self.size[axis] + at[axis]
            found.append((at["core"], place, number))
        return found

    def gather_cz(self, array, dim):
        return lax.all_gather(array, ("core", "z"), axis=dim, tiled=True)

    def sum_halves(self, array, axis, dim):
        if self.size[axis] == 2:
            at = self.index(axis)
            sent = self.swap(lax.dynamic_index_in_dim(array, 1 - at, dim, False), axis)
            kept = lax.dynamic_index_in_dim(array, at, dim, False)
            return (kept.astype(F32) + sent.astype(F32)).astype(array.dtype)
        return lax.psum_scatter(array, axis, scatter_dimension=dim, tiled=False)

    def sum_cores(self, kept, sent):
        return (kept.astype(F32) + self.swap(sent, "core").astype(F32)).astype(kept.dtype)

    def sum_z(self, array, dim):
        depth = self.size["z"]
        z = self.index("z")

        def block(k):
            return lax.dynamic_index_in_dim(array, jnp.remainder(z + k, depth), dim, False)

        total = block(0).astype(F32)
        for k in range(1, depth):
            total = total + self.turn(block(k), k).astype(F32)
        return total

    def sum_z_low(self, array):
        return lax.psum_scatter(array, "z", scatter_dimension=0, tiled=True)

    def planes(self, array):
        sx, sy, sz = (self.size[axis] for axis in "xyz")
        return self.sum_halves(array.reshape((sx, sy, sz) + array.shape[1:]), "x", 0)

    def sum_all_small(self, array):
        got = lax.all_to_all(array, ("x", "z", "y"), 0, 0, tiled=True)
        return jnp.sum(got.astype(F32), axis=0)

    def exchange(self, array):
        count = self.size["x"] * self.size["y"]
        flat = array.reshape((count,) + array.shape[2:])
        return lax.all_to_all(flat, PLANE, 0, 0, tiled=True).reshape(array.shape)

    def over_plane(self, halves, first):
        if not self.pairs_only:
            return [first([lax.all_gather(jnp.concatenate(halves), PLANE, axis=0, tiled=True)])]
        upper, lower = halves
        size = 2 * upper.shape[0]
        near = lax.optimization_barrier((self.swap(upper, "x"), self.swap(lower, "y")))
        near = jnp.concatenate([upper, near[0], lower, near[1]])
        upper, lower, near = lax.optimization_barrier((near[:size], near[size:], near))
        upper, lower, done = lax.optimization_barrier((self.swap(upper, "y"), self.swap(lower, "x"), first([near])))
        return [done, first([upper, lower])]

    def sum_plane(self, parts, held=(), beside=(None, None)):
        works = [work or (lambda *given: ()) for work in beside]
        if not self.pairs_only:
            total = lax.psum_scatter(parts[0][0], PLANE, scatter_dimension=0, tiled=True).astype(F32)
            half = total.shape[0] // 2
            empty = [jnp.zeros((half, total.shape[1]), BF16)] * 2
            return [total[:half], total[half:]], empty, works[1](*works[0](*held))
        (near,), (upper, lower) = parts
        quarter = upper.shape[0] // 2
        upper, lower, held = lax.optimization_barrier((upper, lower, tuple(held)))
        upper, lower, extra = lax.optimization_barrier((self.swap(upper, "y"), self.swap(lower, "x"), works[0](*held)))
        at = [near[k * quarter : (k + 1) * quarter].astype(F32) for k in range(4)]
        own = [at[0] + upper[:quarter].astype(F32), at[2] + lower[:quarter].astype(F32)]
        upper = (at[1] + upper[quarter:].astype(F32)).astype(BF16)
        lower = (at[3] + lower[quarter:].astype(F32)).astype(BF16)
        upper, lower, extra = lax.optimization_barrier((upper, lower, extra))
        upper, lower, extra = lax.optimization_barrier((self.swap(upper, "x"), self.swap(lower, "y"), works[1](*extra)))
        return own, [upper, lower], extra

    def position(self, length):
        return (self.index("z") * self.size["y"] + self.index("y")) * length

    def window_bases(self, length):
        z, y, wide = self.index("z"), self.index("y"), self.size["y"]
        span = wide * length
        reach = -(-(DOC_LIMIT - 1) // span)
        base = self.position(length)
        if wide == 2 and reach == 2:
            cross = jnp.where(y == 0, z * span - length, z * span)
            return [base, base - span, base - 2 * span, cross, cross - span]
        return [(z - k) * span + j * length for k in range(reach + 1) for j in range(wide)]

    def window(self, array, length, beside):
        wide = self.size["y"]
        reach = -(-(DOC_LIMIT - 1) // (wide * length))
        if wide == 2 and reach == 2:
            first = self.index("y") == 0
            one, two, extra = lax.optimization_barrier((self.shift(array, 1), self.shift(array, 2), beside[0]()))
            near = self.swap(jnp.where(first, array, one), "y")
            far = self.swap(jnp.where(first, one, two), "y")
            near, far, extra = lax.optimization_barrier((near, far, beside[1](extra)))
            return [array, one, two, near, far], extra
        along = [lax.all_gather(array, "y", axis=0)]
        for _ in range(reach):
            along.append(self.shift(along[-1], 1))
        return [level[j] for level in along for j in range(wide)], beside[1](beside[0]())

    def window_kinds(self, length):
        if self.size["y"] == 2 and 2 * length * 2 >= DOC_LIMIT - 1 > 2 * length:
            return [F32, F32, F32, BF16, BF16]
        return [F32] * len(self.window_bases(length))

    def window_back(self, terms, length, beside=()):
        wide = self.size["y"]
        span = wide * length
        reach = -(-(DOC_LIMIT - 1) // span)
        results = []

        def follow(*arrays):
            if len(results) < len(beside):
                results.append(beside[len(results)](*(results[-1] if results else ())))
                *arrays, results[-1] = lax.optimization_barrier((*arrays, results[-1]))
            return arrays

        if wide == 2 and reach == 2:
            first = self.index("y") == 0
            own, one, two, near, far = terms
            far, near = follow(self.swap(far, "y"), self.swap(near, "y"))
            far, near = far.astype(F32), near.astype(F32)
            two = (two + jnp.where(first, 0.0, far)).astype(BF16)
            one = (one + jnp.where(first, far, near)).astype(BF16)
            two, one = follow(self.shift(two, -2), self.shift(one, -1))
            own = own + jnp.where(first, near, 0.0) + one.astype(F32) + two.astype(F32)
            (own,) = follow(own)
            return own, results
        total = None
        for k in range(reach, -1, -1):
            level = jnp.stack(terms[k * wide : (k + 1) * wide])
            total = level if total is None else level + self.shift(total.astype(BF16), -1).astype(F32)
        total = lax.psum_scatter(total.astype(BF16), "y", scatter_dimension=0, tiled=False).astype(F32)
        for _ in beside:
            (total,) = follow(total)
        return total, results


def on_device(
    links,
    tokens,
    segment_ids,
    w_query,
    w_key,
    w_value,
    w_out,
    w_gate,
    w_up,
    w_down,
    g_in,
    g_post_attn,
    g_pre_ffn,
    g_post_ffn,
    g_query,
    g_key,
    cotangent,
):
    rows, length, width = tokens.shape
    count = rows * length
    size = links.size
    sx, sc, sz, sy = (size[axis] for axis in AXES)
    parts = sx * sc * sz * sy
    shard = w_gate.shape[0]
    hidden_shard = w_down.shape[0]
    chunk = -(-hidden_shard // 16) * 16
    units = sc * sz * chunk
    head_shard = g_query.shape[0]
    tokens_flat = tokens.reshape(count, width)
    cot_flat = cotangent.reshape(count, width)

    step = jnp.arange(length, dtype=jnp.int32)
    pos_own = links.position(length) + step
    cosine, sine = rope_tables(pos_own)

    lanes = 2 * HEAD + SMALL
    vectors = jnp.concatenate([g_in, g_post_attn, g_pre_ffn, g_post_ffn, g_query, g_key])
    vectors = lax.optimization_barrier(jnp.pad(vectors, (0, 2 * HEAD - vectors.shape[0])))[None]
    seg_rows = jnp.pad(segment_ids.astype(F32), ((0, 0), (0, 2 * HEAD - length)))
    used = shard + rows + 1
    kv_shard = jnp.concatenate([jnp.concatenate([w_key, w_value], axis=1), seg_rows, vectors]).astype(BF16)
    kv_shard = jnp.pad(kv_shard, ((0, eights(used) - used), (0, 0)))
    own_ids = segment_ids.astype(F32).reshape(count, 1)
    kv_shard, own_ids, w_gate, w_up, w_down, w_query, w_out = lax.optimization_barrier(
        (kv_shard, own_ids, w_gate, w_up, w_down, w_query, w_out)
    )
    kv_along = links.along_z(kv_shard)
    full_down = links.gather_cz(jnp.pad(w_down.astype(BF16), ((0, chunk - hidden_shard), (0, 0))), 0)

    def columns(weight):
        split = weight.astype(BF16).reshape(shard, sx, sc, sz, sy, hidden_shard)
        split = jnp.pad(split, ((0, 0),) * 5 + ((0, chunk - hidden_shard),))
        return jnp.transpose(split, (1, 4, 0, 2, 3, 5)).reshape(sx, sy, shard, units)

    pair = jnp.stack([columns(w_gate), columns(w_up)], axis=2)
    wide = max(width, HEADS * HEAD)
    q_shard = jnp.pad(w_query.astype(BF16), ((0, 0), (0, wide - HEADS * HEAD)))
    o_shard = jnp.pad(w_out.astype(BF16), ((0, 0), (0, wide - width)))
    out_shard = w_out.shape[0]
    used = out_shard + shard
    qo_shard = jnp.pad(jnp.concatenate([o_shard, q_shard]), ((0, eights(used) - used), (0, 0)))
    pair, qo_shard, kv_along = lax.optimization_barrier((pair, qo_shard, kv_along))
    kv_own, pair, qo_shard = lax.optimization_barrier((links.across_plane(kv_along), pair, qo_shard))
    full_kv, gains, heads, seg_all = links.placed(
        kv_shard,
        kv_own,
        (
            (0, shard, 0, 2 * HEAD),
            (shard + rows, 0, shard, 4, True),
            (shard + rows, 4 * shard, head_shard, 2, True),
            (shard, rows, length),
        ),
    )
    h_in, k_proj, kv_low = kv_step(rows, length, tokens_flat, full_kv, gains, heads, cosine, sine)
    kv_low, qo_along, pair = lax.optimization_barrier((kv_low, links.along_z(qo_shard), links.exchange(pair)))
    pair = jnp.transpose(pair, (2, 0, 1, 3, 4)).reshape(2 * sx, sy * shard, units)
    kv, qo = links.window(
        kv_low,
        length,
        (
            lambda: (links.across_plane(qo_along),),
            lambda qo: (qo[0], links.swap(qo[0], "core") if links.pairs_only else qo[0]),
        ),
    )
    masks = (own_ids, seg_all)
    kv[2], pair = lax.optimization_barrier((kv[2], pair))
    full_pair = links.gather_cz(pair, 1).reshape(2, width, units)
    full_out, full_query = links.placed(
        qo_shard, qo[0], ((0, out_shard, 0, width), (out_shard, shard, 0, HEADS * HEAD)), qo[1]
    )

    q_proj, query, mixed, attn, resid, *h_ffn = attend(
        links, rows, length, h_in, tokens_flat, full_query, full_out, gains, heads, cosine, sine, masks, kv
    )
    parts_up = links.over_plane(h_ffn, lambda part: (part, *ffn_forward(part, full_pair, full_down)))
    h_parts, hidden, turn, act, ffn_terms = zip(*parts_up, strict=True)
    own, far, _ = links.sum_plane(ffn_terms)
    output, *d_ffn, sums_ffn = middle(rows, length, own, far, resid, cot_flat, gains)

    pending = list(zip(turn, act, strict=True))

    def back(part):
        return (part, *ffn_backward(part, *pending.pop(0), full_pair, full_down))

    d_parts, d_pairs, d_terms = zip(*links.over_plane(d_ffn, back), strict=True)
    block = sy * shard
    places = [
        [
            (c, ((z * 2 + k) * sx + x) * block, ((x * sc + c) * sz + z) * block, block)
            for x in range(sx)
            for c in range(sc)
            for z in range(sz)
        ]
        for k in range(2)
    ]
    half = units // 2
    down_places = [(c, 0, c * half, half) for c in range(sc)]

    def pair_down(kept, sent):
        sets = [([left], [one[None] for one in part]) for left, part in zip(hidden, d_parts, strict=True)]
        low = weight_grads(sets, [down_places])
        return (kept, links.swap(sent, "core"), *low)

    def pair_grads(*pairs):
        return weight_grads([(part, [pair]) for part, pair in zip(h_parts, pairs, strict=True)], places)

    own, far, (kept, got, *grad_down) = links.sum_plane(d_terms, d_pairs, (pair_grads, pair_down))
    own, far, half_pair = lax.optimization_barrier((own, far, (kept.astype(F32) + got.astype(F32)).astype(BF16)))
    grad_pair = links.sum_z_low(half_pair)

    def by_member(sums):
        return jnp.transpose(sums.reshape(2, sx, sy, shard, units), (1, 2, 0, 3, 4))

    def unpacked(got):
        got = got.reshape(sx, sy, 2, shard, sc, sz, chunk)[..., :hidden_shard]
        return jnp.transpose(got, (2, 3, 0, 4, 5, 1, 6)).reshape(2, shard, parts * hidden_shard).astype(F32)

    d_res, d_attn, d_qproj, sums_attn, heads_attn, *terms = attend_back(
        links, rows, length, own, far, cot_flat, resid, attn, q_proj, query, full_out, gains, heads, cosine, sine, masks, kv,
        links.window_kinds(length),
    )
    d_kv, beside = links.window_back(
        terms,
        length,
        (
            lambda: (
                links.sum_cores(*outer_grads(links.order("xyz"), (out_shard, shard), mixed, d_attn, h_in, d_qproj)),
                links.sum_cores(*grad_down),
            ),
            lambda second, low: (links.planes(second), low, grad_pair),
        ),
    )
    second, low, grad_pair = beside[1]
    grad_down = links.sum_z_low(low)[:hidden_shard].astype(F32)

    d_kvproj, grad_tokens, sums_in, heads_in = finish(
        rows, length, d_kv, k_proj, d_qproj, tokens_flat, d_res, full_query, full_kv, gains, heads, cosine, sine
    )
    gain_terms = (sums_ffn + sums_attn + sums_in)[:4]
    head_terms = (heads_attn + heads_in)[:2].reshape(2, parts, head_shard)
    head_terms = jnp.pad(head_terms, ((0, 0), (0, 0), (0, shard - head_shard))).reshape(2, width)
    small_terms = jnp.pad(jnp.concatenate([gain_terms, head_terms]), ((0, SMALL - 6), (0, 0)))
    d_kvproj, second, got_pair = lax.optimization_barrier(
        (d_kvproj, links.sum_halves(second, "y", 0), links.exchange(by_member(grad_pair)))
    )
    first_grad = first_grads(links.order("xzy"), shard, h_in, d_kvproj, small_terms)
    first_core = links.sum_cores(*first_grad)
    first_sum = links.sum_all_small(first_core)
    second_sum = links.sum_z(second, 0)
    grad_pair = unpacked(got_pair)
    return (
        output.reshape(tokens.shape),
        grad_tokens.reshape(tokens.shape),
        second_sum[out_shard : out_shard + shard, : HEADS * HEAD],
        first_sum[:shard, SMALL : SMALL + HEAD],
        first_sum[:shard, SMALL + HEAD :],
        second_sum[:out_shard, :width],
        grad_pair[0],
        grad_pair[1],
        grad_down,
        *(first_sum[:shard, k] for k in range(4)),
        *(first_sum[:head_shard, 4 + k] for k in range(2)),
    )


def solution(mesh):
    plane = mesh.shape["dp"] // 2
    by_chip = Mesh(mesh.devices.reshape(plane, 2, -1, plane), AXES)
    links = Links(by_chip)
    placed = P(("x", "core"), ("z", "y"), None)
    matrix = P(AXES, None)
    vector = P(AXES)
    in_specs = (placed, P(("x", "core"), ("z", "y"))) + (matrix,) * 7 + (vector,) * 6 + (placed,)
    out_specs = (placed, placed) + (matrix,) * 7 + (vector,) * 6

    def step(*arguments):
        return on_device(links, *arguments)

    return jax.shard_map(step, mesh=by_chip, in_specs=in_specs, out_specs=out_specs, check_vma=False)
```

```python
import functools
import math

import jax
import jax.numpy as jnp
from jax import lax
from jax.experimental import pallas as pl
from jax.experimental.pallas import tpu as pltpu
from jax.sharding import Mesh
from jax.sharding import PartitionSpec as P

HEADS = 4
HEAD = 256
HALF = HEAD // 2
DOC_LIMIT = 512
EPSILON = 1e-06
ROPE_BASE = 1000000.0
NEG_FILL = -1e30
SCORE_SCALE = HEAD ** (-0.5)
SLOPE = math.sqrt(2.0 / math.pi)
F32 = jnp.float32
BF16 = jnp.bfloat16
PLANE = ("x", "y")
AXES = ("x", "core", "z", "y")
SWAP = [(0, 1), (1, 0)]
IN, POST_ATTN, PRE_FFN, POST_FFN = range(4)
SMALL = 128
ROOM = 58 << 20


def dot(left, right, dims):
    return lax.dot_general(left, right, (dims, ((), ())), preferred_element_type=F32)


def mm(left, right):
    return dot(left, right, ((1,), (0,)))


def mm_t(left, right):
    return dot(left, right, ((1,), (1,)))


def t_mm(left, right):
    return dot(left, right, ((0,), (0,)))


def inv_rms(values):
    return lax.rsqrt(jnp.mean(values * values, axis=-1, keepdims=True) + EPSILON)


def rms_back(values, gain_vec, d_norm):
    scale = inv_rms(values)
    unit = values * scale
    weighted = d_norm * gain_vec
    d_values = scale * (weighted - unit * jnp.mean(weighted * unit, axis=-1, keepdims=True))
    return d_values, d_norm * unit


def rope_tables(positions):
    inverse = ROPE_BASE ** (-(jnp.arange(HALF, dtype=F32) * 2.0 / HEAD))
    angles = positions.astype(F32)[..., None] * inverse
    return jnp.cos(angles), jnp.sin(angles)


def rotate(values, cosine, sine):
    first, second = values[:, :HALF], values[:, HALF:]
    return jnp.concatenate([first * cosine - second * sine, second * cosine + first * sine], axis=-1)


def eights(rows):
    return -(-rows // 8) * 8


def column_sum(terms):
    return jnp.sum(terms, axis=0, keepdims=True)


def call(body, grid, in_specs, out_specs, out_shape, flops, scratch=()):
    moved = sum(math.prod(one.shape) * one.dtype.itemsize for one in jax.tree.leaves(out_shape))
    return pl.pallas_call(
        body,
        grid=grid,
        in_specs=in_specs,
        out_specs=out_specs,
        out_shape=out_shape,
        scratch_shapes=list(scratch),
        compiler_params=pltpu.CompilerParams(vmem_limit_bytes=ROOM),
        cost_estimate=pl.CostEstimate(flops=flops, bytes_accessed=2 * moved, transcendentals=0),
    )


def shaped(*shape, dtype=F32):
    return jax.ShapeDtypeStruct(shape, dtype)


def whole(*shape):
    return pl.BlockSpec(shape, lambda i: (0,) * len(shape))


def rows_of(tile, width):
    return pl.BlockSpec((tile, width), lambda i: (i, 0))


def row_block(*shape):
    return pl.BlockSpec((1,) + shape, lambda i: (i,) + (0,) * len(shape))


def part_specs(tile, width, arrays):
    if len(arrays) == 1:
        return [rows_of(tile, width)]
    half = arrays[0].shape[0] // tile
    return [
        pl.BlockSpec((tile, width), lambda i: (jnp.minimum(i, half - 1), 0)),
        pl.BlockSpec((tile, width), lambda i: (jnp.maximum(i - half, 0), 0)),
    ]


def in_second():
    return pl.program_id(0) >= pl.num_programs(0) // 2


def load_part(refs):
    if len(refs) == 1:
        return refs[0][...]
    return lax.select_n(in_second(), refs[0][...], refs[1][...])


def store_part(refs, value):
    if len(refs) == 1:
        refs[0][...] = value
        return

    @pl.when(in_second() == False)
    def _():
        refs[0][...] = value

    @pl.when(in_second())
    def _():
        refs[1][...] = value


def kv_body(tok_ref, wkv_ref, gains_ref, head_ref, cos_ref, sin_ref, h_ref, kproj_ref, kv_ref):
    tokens = tok_ref[...].astype(F32)
    h = (tokens * inv_rms(tokens) * gains_ref[IN : IN + 1]).astype(BF16)
    h_ref[...] = h
    proj = mm(h, wkv_ref[...])
    k_proj = proj[:, :HEAD]
    kproj_ref[...] = k_proj
    key = rotate(k_proj * inv_rms(k_proj) * head_ref[1:2], cos_ref[...], sin_ref[...])
    kv_ref[0, :, :HEAD] = key.astype(BF16)
    kv_ref[0, :, HEAD:] = proj[:, HEAD:].astype(BF16)


def kv_step(rows, length, tokens, wkv, gains, heads, cosine, sine):
    count, width = tokens.shape
    return call(
        kv_body,
        (rows,),
        [rows_of(length, width), whole(*wkv.shape), whole(*gains.shape), whole(*heads.shape)]
        + [whole(length, HALF)] * 2,
        [rows_of(length, width), rows_of(length, HEAD), row_block(length, 2 * HEAD)],
        [shaped(count, width, dtype=BF16), shaped(count, HEAD), shaped(rows, length, 2 * HEAD, dtype=BF16)],
        2 * count * width * 2 * HEAD,
    )(tokens, wkv, gains, heads, cosine, sine)


def by_head(array):
    return jnp.concatenate([array[:, h * HEAD : (h + 1) * HEAD] for h in range(HEADS)], axis=0)


def by_lane(array):
    part = array.shape[0] // HEADS
    return jnp.concatenate([array[h * part : (h + 1) * part] for h in range(HEADS)], axis=1)


def probs_of(links, query, keys, own_ref, seg_ref):
    length = own_ref.shape[0]
    bases = links.window_bases(length)
    here = links.position(length)
    step = lax.broadcasted_iota(jnp.int32, (1, length), 1)
    segs, later = [], []
    for base in bases:
        row = seg_ref[0, pl.ds(jnp.maximum(base, 0) // length, 1), :]
        segs.append(jnp.where(base >= 0, row, -1.0))
        later.append(base - here + step)
    own_step = lax.broadcasted_iota(jnp.int32, (length, 1), 0)
    allowed = (own_ref[...] == jnp.concatenate(segs, axis=1)) & (jnp.concatenate(later, axis=1) <= own_step)
    allowed = jnp.concatenate([allowed.astype(F32)] * HEADS, axis=0) > 0.5
    scores = jnp.where(allowed, mm_t(query, keys) * SCORE_SCALE, NEG_FILL)
    powers = jnp.exp(scores - jnp.max(scores, axis=-1, keepdims=True))
    return powers / jnp.sum(powers, axis=-1, keepdims=True)


def attend_body(links, blocks, *refs):
    (h_ref, tok_ref, wq_ref, wo_ref, gains_ref, head_ref, cos_ref, sin_ref) = refs[:8]
    masks, kv_refs = refs[8:10], refs[10 : 10 + blocks]
    qproj_ref, query_ref, mixed_ref, attn_ref, resid_ref, *hffn_refs = refs[10 + blocks :]
    proj = mm(h_ref[...], wq_ref[...])
    qproj_ref[...] = proj
    cosine, sine = cos_ref[...], sin_ref[...]
    query = []
    for h in range(HEADS):
        one = proj[:, h * HEAD : (h + 1) * HEAD]
        query.append(rotate(one * inv_rms(one) * head_ref[0:1], cosine, sine).astype(BF16))
    query_ref[...] = jnp.concatenate(query, axis=1)
    keys = jnp.concatenate([one[0, :, :HEAD] for one in kv_refs], axis=0)
    values = jnp.concatenate([one[0, :, HEAD:] for one in kv_refs], axis=0)
    probs = probs_of(links, jnp.concatenate(query, axis=0), keys, *masks).astype(BF16)
    mixed = by_lane(mm(probs, values).astype(BF16))
    mixed_ref[...] = mixed
    attn = mm(mixed, wo_ref[...])
    attn_ref[...] = attn
    resid = tok_ref[...].astype(F32) + attn * inv_rms(attn) * gains_ref[POST_ATTN : POST_ATTN + 1]
    resid_ref[...] = resid
    store_part(hffn_refs, (resid * inv_rms(resid) * gains_ref[PRE_FFN : PRE_FFN + 1]).astype(BF16))


def mask_specs(masks):
    own, segs = masks
    return [rows_of(own.shape[0] // segs.shape[0], 1), row_block(*segs.shape[1:])]


def attend(links, rows, length, h, tokens, wq, wo, gains, heads, cosine, sine, masks, kv):
    count, width = tokens.shape
    wide = HEADS * HEAD
    window = len(kv) * length
    halves = [shaped(count // 2, width, dtype=BF16)] * 2
    return call(
        functools.partial(attend_body, links, len(kv)),
        (rows,),
        [rows_of(length, width)] * 2
        + [whole(*one.shape) for one in (wq, wo, gains, heads)]
        + [whole(length, HALF)] * 2
        + mask_specs(masks)
        + [row_block(length, 2 * HEAD)] * len(kv),
        [rows_of(length, wide)] * 3 + [rows_of(length, width)] * 2 + part_specs(length, width, halves),
        [
            shaped(count, wide),
            shaped(count, wide, dtype=BF16),
            shaped(count, wide, dtype=BF16),
            shaped(count, width),
            shaped(count, width),
            *halves,
        ],
        4 * count * wide * (width + window),
    )(h, tokens, wq, wo, gains, heads, cosine, sine, *masks, *kv)


def attend_back_body(links, blocks, *refs):
    own_refs, far_refs, refs = refs[:2], refs[2:4], refs[4:]
    (cot_ref, resid_ref, attn_ref, qproj_ref, query_ref, wo_ref, gains_ref, head_ref, cos_ref, sin_ref) = refs[:10]
    masks, kv_refs = refs[10:12], refs[12 : 12 + blocks]
    dres_ref, dattn_ref, dq_ref, sums_ref, head_sums_ref = refs[12 + blocks : 17 + blocks]
    term_refs = refs[17 + blocks :]
    d_norm, pre_terms = rms_back(resid_ref[...], gains_ref[PRE_FFN : PRE_FFN + 1], load_part(own_refs) + load_part(far_refs).astype(F32))
    d_res = cot_ref[...].astype(F32) + d_norm
    dres_ref[...] = d_res
    d_attn, post_terms = rms_back(attn_ref[...], gains_ref[POST_ATTN : POST_ATTN + 1], d_res)
    d_attn = d_attn.astype(BF16)
    dattn_ref[...] = d_attn
    d_mixed = by_head(mm_t(d_attn, wo_ref[...]).astype(BF16))
    query = by_head(query_ref[...])
    keys = jnp.concatenate([one[0, :, :HEAD] for one in kv_refs], axis=0)
    values = jnp.concatenate([one[0, :, HEAD:] for one in kv_refs], axis=0)
    probs = probs_of(links, query, keys, *masks)
    d_probs = mm_t(d_mixed, values)
    d_scores = (probs * (d_probs - jnp.sum(d_probs * probs, axis=-1, keepdims=True))).astype(BF16)
    key_terms = t_mm(d_scores, query) * SCORE_SCALE
    value_terms = t_mm(probs.astype(BF16), d_mixed)
    length = query_ref.shape[0]
    for k, ref in enumerate(term_refs):
        at = slice(k * length, (k + 1) * length)
        ref[0, :, :HEAD] = key_terms[at].astype(ref.dtype)
        ref[0, :, HEAD:] = value_terms[at].astype(ref.dtype)
    d_query = mm(d_scores, keys) * SCORE_SCALE
    cosine, sine = cos_ref[...], -sin_ref[...]
    head_sum = jnp.zeros((1, HEAD), F32)
    for h in range(HEADS):
        turned = rotate(d_query[h * length : (h + 1) * length], cosine, sine)
        lanes = slice(h * HEAD, (h + 1) * HEAD)
        d_proj, terms = rms_back(qproj_ref[:, lanes], head_ref[0:1], turned)
        dq_ref[:, lanes] = d_proj.astype(BF16)
        head_sum += column_sum(terms)

    @pl.when(pl.program_id(0) == 0)
    def _():
        sums_ref[...] = jnp.zeros_like(sums_ref)
        head_sums_ref[...] = jnp.zeros_like(head_sums_ref)

    sums_ref[POST_ATTN : POST_ATTN + 1] += column_sum(post_terms)
    sums_ref[PRE_FFN : PRE_FFN + 1] += column_sum(pre_terms)
    head_sums_ref[0:1] += head_sum


def attend_back(links, rows, length, own, far, cot, resid, attn, qproj, query, wo, gains, heads, cosine, sine, masks, kv, kinds):
    count, width = cot.shape
    wide = HEADS * HEAD
    window = len(kv) * length
    return call(
        functools.partial(attend_back_body, links, len(kv)),
        (rows,),
        part_specs(length, width, own) * 2
        + [rows_of(length, width)] * 3
        + [rows_of(length, wide)] * 2
        + [whole(*one.shape) for one in (wo, gains, heads)]
        + [whole(length, HALF)] * 2
        + mask_specs(masks)
        + [row_block(length, 2 * HEAD)] * len(kv),
        [rows_of(length, width)] * 2
        + [rows_of(length, wide), whole(8, width), whole(8, HEAD)]
        + [row_block(length, 2 * HEAD)] * len(kv),
        [
            shaped(count, width),
            shaped(count, width, dtype=BF16),
            shaped(count, wide, dtype=BF16),
            shaped(8, width),
            shaped(8, HEAD),
        ]
        + [shaped(rows, length, 2 * HEAD, dtype=kind) for kind in kinds],
        2 * count * wide * (width + 5 * window),
    )(*own, *far, cot, resid, attn, qproj, query, wo, gains, heads, cosine, sine, *masks, *kv)


def finish_body(many, *refs):
    finish_rows(refs[:many], *refs[many:])


def finish_rows(dkv_refs, kproj_ref, dq_ref, tok_ref, dres_ref, wq_ref, wkv_ref, gains_ref, head_ref, cos_ref, sin_ref,
                dkvp_ref, grad_ref, sums_ref, head_sums_ref):
    d_kv = sum(ref[0].astype(F32) for ref in dkv_refs)
    turned = rotate(d_kv[:, :HEAD], cos_ref[...], -sin_ref[...])
    d_key, key_terms = rms_back(kproj_ref[...], head_ref[1:2], turned)
    d_proj = jnp.concatenate([d_key.astype(BF16), d_kv[:, HEAD:].astype(BF16)], axis=1)
    dkvp_ref[...] = d_proj
    d_hin = mm_t(dq_ref[...], wq_ref[...]) + mm_t(d_proj, wkv_ref[...])
    d_tokens, in_terms = rms_back(tok_ref[...].astype(F32), gains_ref[IN : IN + 1], d_hin)
    grad_ref[...] = (dres_ref[...] + d_tokens).astype(BF16)

    @pl.when(pl.program_id(0) == 0)
    def _():
        sums_ref[...] = jnp.zeros_like(sums_ref)
        head_sums_ref[...] = jnp.zeros_like(head_sums_ref)

    sums_ref[IN : IN + 1] += column_sum(in_terms)
    head_sums_ref[1:2] += column_sum(key_terms)


def finish(rows, length, dkv, kproj, dq, tokens, dres, wq, wkv, gains, heads, cosine, sine):
    count, width = tokens.shape
    wide = HEADS * HEAD
    return call(
        functools.partial(finish_body, len(dkv)),
        (rows,),
        [row_block(length, 2 * HEAD)] * len(dkv)
        + [rows_of(length, HEAD), rows_of(length, wide)]
        + [rows_of(length, width)] * 2
        + [whole(*one.shape) for one in (wq, wkv, gains, heads)]
        + [whole(length, HALF)] * 2,
        [rows_of(length, 2 * HEAD), rows_of(length, width), whole(8, width), whole(8, HEAD)],
        [shaped(count, 2 * HEAD, dtype=BF16), shaped(count, width, dtype=BF16), shaped(8, width), shaped(8, HEAD)],
        2 * count * width * (wide + 2 * HEAD),
    )(*dkv, kproj, dq, tokens, dres, wq, wkv, gains, heads, cosine, sine)


def pieces_of(total, step):
    return [(k, min(step, total - k)) for k in range(0, total, step)]


def up_body(step, many, *refs):
    pair_ref, down_ref, hidden_ref, turn_ref, act_ref = refs[many : many + 5]
    h = load_part(refs[:many])
    for at, wide in pieces_of(hidden_ref.shape[1], step):
        cols = pl.ds(at, wide)
        gate = mm(h, pair_ref[0, :, cols])
        up = mm(h, pair_ref[1, :, cols])
        square = gate * gate
        bent = jnp.tanh(gate * (SLOPE + SLOPE * 0.044715 * square))
        half = 0.5 + 0.5 * bent
        act = gate * half
        d_act = half + 0.5 * gate * (1.0 - bent * bent) * (SLOPE + 3 * SLOPE * 0.044715 * square)
        hidden_ref[:, cols] = (act * up).astype(BF16)
        turn_ref[:, cols] = (up * d_act).astype(BF16)
        act_ref[:, cols] = act.astype(BF16)
    store_part(refs[many + 5 :], mm(hidden_ref[...], down_ref[...]).astype(BF16))


def ffn_forward(h, pair, down, tile=256, step=256):
    count, width = sum(one.shape[0] for one in h), h[0].shape[1]
    units = pair.shape[2]
    specs = part_specs(tile, width, h)
    hidden, turn, act, *terms = call(
        functools.partial(up_body, step, len(h)),
        (count // tile,),
        specs + [whole(2, width, units), whole(units, width)],
        [rows_of(tile, units)] * 3 + specs,
        [shaped(count, units, dtype=BF16)] * 3 + [shaped(*one.shape, dtype=BF16) for one in h],
        6 * count * width * units,
    )(*h, pair, down)
    return hidden, turn, act, terms


def down_body(step, many, *refs):
    turn_ref, act_ref, pair_ref, down_ref, pair_out = refs[many : many + 5]
    d = load_part(refs[:many])
    for at, wide in pieces_of(turn_ref.shape[1], step):
        cols = pl.ds(at, wide)
        d_hidden = mm_t(d, down_ref[cols, :])
        pair_out[0, :, cols] = (d_hidden * turn_ref[:, cols].astype(F32)).astype(BF16)
        pair_out[1, :, cols] = (d_hidden * act_ref[:, cols].astype(F32)).astype(BF16)
    store_part(refs[many + 5 :], (mm_t(pair_out[0], pair_ref[0]) + mm_t(pair_out[1], pair_ref[1])).astype(BF16))


def ffn_backward(d, turn, act, pair, down, tile=256, step=256):
    count, width = sum(one.shape[0] for one in d), d[0].shape[1]
    units = pair.shape[2]
    specs = part_specs(tile, width, d)
    d_pair, *terms = call(
        functools.partial(down_body, step, len(d)),
        (count // tile,),
        specs + [rows_of(tile, units), rows_of(tile, units), whole(2, width, units), whole(units, width)],
        [pl.BlockSpec((2, tile, units), lambda i: (0, i, 0))] + specs,
        [shaped(2, count, units, dtype=BF16)] + [shaped(*one.shape, dtype=BF16) for one in d],
        6 * count * width * units,
    )(*d, turn, act, pair, down)
    return d_pair, terms


def put(kept_ref, sent_ref, core, index, value):
    @pl.when(lax.axis_index("core") == core)
    def _():
        kept_ref[index] = value

    @pl.when(lax.axis_index("core") != core)
    def _():
        sent_ref[index] = value


def grads_body(places, sets, *refs):
    kept_ref, sent_ref = refs[-2:]
    total, at = None, 0
    for lefts, rights in sets:
        values = []
        for many in (lefts, rights):
            pieces = [ref[...] if len(ref.shape) == 2 else ref[0] for ref in refs[at : at + many]]
            values.append(jnp.concatenate(pieces, axis=0) if many > 1 else pieces[0])
            at += many
        term = t_mm(*values)
        total = term if total is None else total + term
    total = total.astype(BF16)
    tile = total.shape[0]
    for which, moves in enumerate(places):
        for k in range(sum(count for _, _, _, count in moves) // tile):

            @pl.when((pl.program_id(0) == which) & (pl.program_id(1) == k))
            def _(k=k, moves=moves):
                for core, at, row, count in moves:
                    begin, end = max(row, k * tile), min(row + count, (k + 1) * tile)
                    if begin < end:
                        to = at + begin - row
                        index = (slice(to, to + end - begin), slice(None))
                        put(kept_ref, sent_ref, core, index, total[begin - k * tile : end - k * tile])


def weight_grads(sets, places):
    rows, cols = sets[0][0][0].shape[1], sets[0][1][0].shape[2]
    count = sum(one.shape[0] for lefts, _ in sets for one in lefts)
    tile = 384 if rows % 384 == 0 else 256
    out = len(places) * rows // 2
    specs, arrays = [], []
    for lefts, rights in sets:
        specs += [pl.BlockSpec((one.shape[0], tile), lambda k, i: (0, i)) for one in lefts]
        specs += [pl.BlockSpec((1,) + one.shape[1:], lambda k, i: (k, 0, 0)) for one in rights]
        arrays += [*lefts, *rights]
    return call(
        functools.partial(grads_body, places, [(len(lefts), len(rights)) for lefts, rights in sets]),
        (len(places), rows // tile),
        specs,
        [pl.BlockSpec((out, cols), lambda k, i: (0, 0))] * 2,
        [shaped(out, cols, dtype=BF16)] * 2,
        2 * len(places) * count * rows * cols,
    )(*arrays)


def outer_body(order, shards, mixed_ref, dattn_ref, h_ref, dq_ref, kept_ref, sent_ref):
    lanes = kept_ref.shape[2]
    at = 0
    for rows, left, right in ((shards[0], mixed_ref, dattn_ref), (shards[1], h_ref, dq_ref)):
        total = t_mm(left[...], right[...]).astype(BF16)
        wide = total.shape[1]
        for core, place, number in order:
            index = (place, slice(at, at + rows), slice(0, wide))
            put(kept_ref, sent_ref, core, index, total[number * rows : (number + 1) * rows])
        for ref in (kept_ref, sent_ref):
            if wide < lanes:
                ref[:, at : at + rows, wide:] = jnp.zeros((ref.shape[0], rows, lanes - wide), BF16)
        at += rows
    for ref in (kept_ref, sent_ref):
        if at < ref.shape[1]:
            ref[:, at:, :] = jnp.zeros((ref.shape[0], ref.shape[1] - at, lanes), BF16)


def outer_grads(order, shards, mixed, d_attn, h, d_q):
    count = mixed.shape[0]
    shape = (len(order) // 2, eights(sum(shards)), max(d_attn.shape[1], d_q.shape[1]))
    return call(
        functools.partial(outer_body, order, shards),
        (1,),
        [whole(*one.shape) for one in (mixed, d_attn, h, d_q)],
        [whole(*shape)] * 2,
        [shaped(*shape, dtype=BF16)] * 2,
        2 * count * (mixed.shape[1] * d_attn.shape[1] + h.shape[1] * d_q.shape[1]),
    )(mixed, d_attn, h, d_q)


def first_body(order, shard, h_ref, dkv_ref, small_ref, kept_ref, sent_ref):
    small = small_ref[...].T.astype(BF16)
    total = t_mm(h_ref[...], dkv_ref[...]).astype(BF16)
    for core, place, number in order:
        rows = slice(number * shard, (number + 1) * shard)
        put(kept_ref, sent_ref, core, (place, slice(0, shard), slice(0, SMALL)), small[rows])
        put(kept_ref, sent_ref, core, (place, slice(0, shard), slice(SMALL, None)), total[rows])
    for ref in (kept_ref, sent_ref):
        if shard < ref.shape[1]:
            ref[:, shard:, :] = jnp.zeros((ref.shape[0], ref.shape[1] - shard, ref.shape[2]), BF16)


def first_grads(order, shard, h, d_kv, small):
    count, rows = h.shape
    shape = (len(order) // 2, eights(shard), d_kv.shape[1] + SMALL)
    return call(
        functools.partial(first_body, order, shard),
        (1,),
        [whole(*one.shape) for one in (h, d_kv, small)],
        [whole(*shape)] * 2,
        [shaped(*shape, dtype=BF16)] * 2,
        2 * count * rows * d_kv.shape[1],
    )(h, d_kv, small)


def middle_body(own_a, own_b, far_a, far_b, resid_ref, cot_ref, gains_ref, out_ref, dffn_a, dffn_b, sums_ref):
    ffn = load_part((own_a, own_b)) + load_part((far_a, far_b)).astype(F32)
    gain = gains_ref[POST_FFN : POST_FFN + 1]
    out_ref[...] = (resid_ref[...] + ffn * inv_rms(ffn) * gain).astype(BF16)
    d_ffn, terms = rms_back(ffn, gain, cot_ref[...].astype(F32))
    store_part((dffn_a, dffn_b), d_ffn.astype(BF16))

    @pl.when(pl.program_id(0) == 0)
    def _():
        sums_ref[...] = jnp.zeros_like(sums_ref)

    sums_ref[POST_FFN : POST_FFN + 1] += column_sum(terms)


def middle(rows, length, own, far, resid, cot, gains):
    count, width = resid.shape
    specs = part_specs(length, width, own)
    return call(
        middle_body,
        (rows,),
        specs * 2 + [rows_of(length, width)] * 2 + [whole(*gains.shape)],
        [rows_of(length, width)] + specs + [whole(8, width)],
        [shaped(count, width, dtype=BF16)] + [shaped(count // 2, width, dtype=BF16)] * 2 + [shaped(8, width)],
        20 * count * width,
    )(*own, *far, resid, cot, gains)


def place_body(links, shard, parts, own_ref, other_ref, *refs):
    outs, scratch = refs[:-1], refs[-1]
    depth = links.size["z"]
    at_x, at_c, at_z, at_y = (links.index(axis) for axis in AXES)
    number = 0
    for x in range(2):
        for core in range(2):
            for z in range(depth):
                for y in range(2):
                    slot = jnp.abs(at_x - x) + 2 * jnp.abs(at_y - y)
                    slot = slot * depth + jnp.remainder(at_z - z + depth, depth)
                    mine = own_ref[slot].astype(F32)
                    theirs = other_ref[slot].astype(F32)
                    piece = jnp.where(at_c == core, mine, theirs)
                    scratch[number] = piece
                    number += 1
    for part, out in zip(parts, outs, strict=True):
        for k in range(number):
            if len(part) == 4:
                first, count, at, lanes = part
                out[k * count : (k + 1) * count, :] = scratch[k, first : first + count, at : at + lanes].astype(out.dtype)
                continue
            if len(part) == 3:
                first, count, lanes = part
                if k < 2 * depth:
                    ids = scratch[(at_x * 2 + at_c) * 2 * depth + k]
                    for row in range(count):
                        out[row, k : k + 1, :] = ids[first + row : first + row + 1, :lanes]
                continue
            row, at, lanes, vectors = part[:4]
            for v in range(vectors):
                begin = at + v * lanes
                out[v : v + 1, k * lanes : (k + 1) * lanes] = scratch[k, row : row + 1, begin : begin + lanes]


def placed(links, own, other, parts):
    slots, rows, lanes = own.shape
    number = 2 * slots
    return pl.pallas_call(
        functools.partial(place_body, links, rows, parts),
        out_shape=[
            shaped(number * part[1], part[3], dtype=BF16)
            if len(part) == 4
            else shaped(part[1], slots // 2, part[2])
            if len(part) == 3
            else shaped(8, number * part[2])
            for part in parts
        ],
        scratch_shapes=[pltpu.VMEM((number, rows, lanes), F32)],
        compiler_params=pltpu.CompilerParams(vmem_limit_bytes=ROOM),
    )(own, other)


class Links:
    def __init__(self, mesh):
        self.size = dict(mesh.shape)
        self.pairs_only = self.size["x"] == 2 and self.size["y"] == 2

    def index(self, axis):
        return lax.axis_index(axis)

    def swap(self, array, axis):
        return lax.ppermute(array, axis, SWAP)

    def shift(self, array, step):
        depth = self.size["z"]
        pairs = [(i, i + step) for i in range(depth) if 0 <= i + step < depth]
        return lax.ppermute(array, "z", pairs)

    def turn(self, array, step):
        depth = self.size["z"]
        return lax.ppermute(array, "z", [(i, (i + step) % depth) for i in range(depth)])

    def ordered(self, own, other, axis):
        first = self.index(axis) == 0
        return jnp.where(first, jnp.stack([own, other]), jnp.stack([other, own]))

    def along_z(self, array):
        return jnp.stack([array] + [self.turn(array, k) for k in range(1, self.size["z"])])

    def across_plane(self, along):
        if not self.pairs_only:
            return along
        across = lax.ppermute(along, PLANE, [(k, 3 - k) for k in range(4)])
        return jnp.concatenate([along, self.swap(along, "x"), self.swap(along, "y"), across])

    def placed(self, array, own, parts, other=None):
        if self.pairs_only:
            other = self.swap(own, "core") if other is None else other
            return placed(self, own, other, parts)
        full = lax.all_gather(array, AXES, axis=0)
        cuts = []
        for part in parts:
            if len(part) == 4:
                r, n, c, w = part
                cuts.append(full[:, r : r + n, c : c + w].reshape(-1, w))
            elif len(part) == 3:
                r, n, w = part
                blocks = self.size["z"] * self.size["y"]
                at = (self.index("x") * 2 + self.index("core")) * blocks
                ids = lax.dynamic_slice_in_dim(full[:, r : r + n, :w], at, blocks)
                cuts.append(jnp.swapaxes(ids, 0, 1).astype(F32))
            else:
                r, c, w, n = part[:4]
                rows = jnp.swapaxes(full[:, r, c : c + n * w].reshape(-1, n, w), 0, 1).reshape(n, -1)
                cuts.append(jnp.pad(rows.astype(F32), ((0, 8 - n), (0, 0))))
        return cuts

    def order(self, axes):
        found = []
        counts = [self.size[axis] for axis in AXES]
        for number in range(math.prod(counts)):
            at, rest = {}, number
            for axis, many in zip(AXES[::-1], counts[::-1], strict=True):
                at[axis], rest = rest % many, rest // many
            place = 0
            for axis in axes:
                place = place * self.size[axis] + at[axis]
            found.append((at["core"], place, number))
        return found

    def gather_cz(self, array, dim):
        return lax.all_gather(array, ("core", "z"), axis=dim, tiled=True)

    def sum_halves(self, array, axis, dim):
        if self.size[axis] == 2:
            at = self.index(axis)
            sent = self.swap(lax.dynamic_index_in_dim(array, 1 - at, dim, False), axis)
            kept = lax.dynamic_index_in_dim(array, at, dim, False)
            return (kept.astype(F32) + sent.astype(F32)).astype(array.dtype)
        return lax.psum_scatter(array, axis, scatter_dimension=dim, tiled=False)

    def sum_cores(self, kept, sent):
        return (kept.astype(F32) + self.swap(sent, "core").astype(F32)).astype(kept.dtype)

    def sum_z(self, array, dim):
        depth = self.size["z"]
        z = self.index("z")

        def block(k):
            return lax.dynamic_index_in_dim(array, jnp.remainder(z + k, depth), dim, False)

        total = block(0).astype(F32)
        for k in range(1, depth):
            total = total + self.turn(block(k), k).astype(F32)
        return total

    def sum_z_low(self, array):
        return lax.psum_scatter(array, "z", scatter_dimension=0, tiled=True)

    def planes(self, array):
        sx, sy, sz = (self.size[axis] for axis in "xyz")
        return self.sum_halves(array.reshape((sx, sy, sz) + array.shape[1:]), "x", 0)

    def to_members(self, array):
        count = self.size["x"] * self.size["y"]
        got = lax.all_to_all(array.reshape((count, -1) + array.shape[2:]), PLANE, 0, 0, tiled=True)
        return got.reshape((count, self.size["z"]) + array.shape[1:])

    def exchange(self, array):
        count = self.size["x"] * self.size["y"]
        flat = array.reshape((count,) + array.shape[2:])
        return lax.all_to_all(flat, PLANE, 0, 0, tiled=True).reshape(array.shape)

    def over_plane(self, halves, first):
        if not self.pairs_only:
            return [first([lax.all_gather(jnp.concatenate(halves), PLANE, axis=0, tiled=True)])]
        upper, lower = halves
        size = 2 * upper.shape[0]
        near = lax.optimization_barrier((self.swap(upper, "x"), self.swap(lower, "y")))
        near = jnp.concatenate([upper, near[0], lower, near[1]])
        upper, lower, near = lax.optimization_barrier((near[:size], near[size:], near))
        upper, lower, done = lax.optimization_barrier((self.swap(upper, "y"), self.swap(lower, "x"), first([near])))
        return [done, first([upper, lower])]

    def sum_plane(self, parts, held=(), beside=(None, None)):
        works = [work or (lambda *given: ()) for work in beside]
        if not self.pairs_only:
            total = lax.psum_scatter(parts[0][0], PLANE, scatter_dimension=0, tiled=True).astype(F32)
            half = total.shape[0] // 2
            empty = [jnp.zeros((half, total.shape[1]), BF16)] * 2
            return [total[:half], total[half:]], empty, works[1](*works[0](*held))
        (near,), (upper, lower) = parts
        quarter = upper.shape[0] // 2
        upper, lower, held = lax.optimization_barrier((upper, lower, tuple(held)))
        upper, lower, extra = lax.optimization_barrier((self.swap(upper, "y"), self.swap(lower, "x"), works[0](*held)))
        at = [near[k * quarter : (k + 1) * quarter].astype(F32) for k in range(4)]
        own = [at[0] + upper[:quarter].astype(F32), at[2] + lower[:quarter].astype(F32)]
        upper = (at[1] + upper[quarter:].astype(F32)).astype(BF16)
        lower = (at[3] + lower[quarter:].astype(F32)).astype(BF16)
        upper, lower, extra = lax.optimization_barrier((upper, lower, extra))
        upper, lower, extra = lax.optimization_barrier((self.swap(upper, "x"), self.swap(lower, "y"), works[1](*extra)))
        return own, [upper, lower], extra

    def position(self, length):
        return (self.index("z") * self.size["y"] + self.index("y")) * length

    def window_bases(self, length):
        z, y, wide = self.index("z"), self.index("y"), self.size["y"]
        span = wide * length
        reach = -(-(DOC_LIMIT - 1) // span)
        base = self.position(length)
        if wide == 2 and reach == 2:
            cross = jnp.where(y == 0, z * span - length, z * span)
            return [base, base - span, base - 2 * span, cross, cross - span]
        return [(z - k) * span + j * length for k in range(reach + 1) for j in range(wide)]

    def window(self, array, length, beside):
        wide = self.size["y"]
        reach = -(-(DOC_LIMIT - 1) // (wide * length))
        if wide == 2 and reach == 2:
            first = self.index("y") == 0
            one, two, extra = lax.optimization_barrier((self.shift(array, 1), self.shift(array, 2), beside[0]()))
            near = self.swap(jnp.where(first, array, one), "y")
            far = self.swap(jnp.where(first, one, two), "y")
            near, far, extra = lax.optimization_barrier((near, far, beside[1](extra)))
            return [array, one, two, near, far], extra
        along = [lax.all_gather(array, "y", axis=0)]
        for _ in range(reach):
            along.append(self.shift(along[-1], 1))
        return [level[j] for level in along for j in range(wide)], beside[1](beside[0]())

    def window_kinds(self, length):
        if self.size["y"] == 2 and 2 * length * 2 >= DOC_LIMIT - 1 > 2 * length:
            return [F32, F32, F32, BF16, BF16]
        return [F32] * len(self.window_bases(length))

    def window_back(self, terms, length, beside=()):
        wide = self.size["y"]
        span = wide * length
        reach = -(-(DOC_LIMIT - 1) // span)
        results = []

        def follow(*arrays):
            if len(results) < len(beside):
                results.append(beside[len(results)](*(results[-1] if results else ())))
                *arrays, results[-1] = lax.optimization_barrier((*arrays, results[-1]))
            return arrays

        if wide == 2 and reach == 2:
            first = self.index("y") == 0
            own, one, two, near, far = terms
            far, near = follow(self.swap(far, "y"), self.swap(near, "y"))
            far, near = far.astype(F32), near.astype(F32)
            two = (two + jnp.where(first, 0.0, far)).astype(BF16)
            one = (one + jnp.where(first, far, near)).astype(BF16)
            own = own + jnp.where(first, near, 0.0)
            two, one, own = follow(self.shift(two, -2), self.shift(one, -1), own)
            return [own, one, two], results
        total = None
        for k in range(reach, -1, -1):
            level = jnp.stack(terms[k * wide : (k + 1) * wide])
            total = level if total is None else level + self.shift(total.astype(BF16), -1).astype(F32)
        total = lax.psum_scatter(total.astype(BF16), "y", scatter_dimension=0, tiled=False).astype(F32)
        for _ in beside:
            (total,) = follow(total)
        return [total], results


def on_device(
    links,
    tokens,
    segment_ids,
    w_query,
    w_key,
    w_value,
    w_out,
    w_gate,
    w_up,
    w_down,
    g_in,
    g_post_attn,
    g_pre_ffn,
    g_post_ffn,
    g_query,
    g_key,
    cotangent,
):
    rows, length, width = tokens.shape
    count = rows * length
    size = links.size
    sx, sc, sz, sy = (size[axis] for axis in AXES)
    parts = sx * sc * sz * sy
    shard = w_gate.shape[0]
    hidden_shard = w_down.shape[0]
    chunk = -(-hidden_shard // 16) * 16
    units = sc * sz * chunk
    head_shard = g_query.shape[0]
    tokens_flat = tokens.reshape(count, width)
    cot_flat = cotangent.reshape(count, width)

    step = jnp.arange(length, dtype=jnp.int32)
    pos_own = links.position(length) + step
    cosine, sine = rope_tables(pos_own)

    lanes = 2 * HEAD + SMALL
    vectors = jnp.concatenate([g_in, g_post_attn, g_pre_ffn, g_post_ffn, g_query, g_key])
    vectors = lax.optimization_barrier(jnp.pad(vectors, (0, 2 * HEAD - vectors.shape[0])))[None]
    seg_rows = jnp.pad(segment_ids.astype(F32), ((0, 0), (0, 2 * HEAD - length)))
    used = shard + rows + 1
    kv_shard = jnp.concatenate([jnp.concatenate([w_key, w_value], axis=1), seg_rows, vectors]).astype(BF16)
    kv_shard = jnp.pad(kv_shard, ((0, eights(used) - used), (0, 0)))
    own_ids = segment_ids.astype(F32).reshape(count, 1)
    kv_shard, own_ids, w_gate, w_up, w_down, w_query, w_out = lax.optimization_barrier(
        (kv_shard, own_ids, w_gate, w_up, w_down, w_query, w_out)
    )
    kv_along = links.along_z(kv_shard)
    full_down = links.gather_cz(jnp.pad(w_down.astype(BF16), ((0, chunk - hidden_shard), (0, 0))), 0)

    def columns(weight):
        split = weight.astype(BF16).reshape(shard, sx, sc, sz, sy, hidden_shard)
        split = jnp.pad(split, ((0, 0),) * 5 + ((0, chunk - hidden_shard),))
        return jnp.transpose(split, (1, 4, 0, 2, 3, 5)).reshape(sx, sy, shard, units)

    pair = jnp.stack([columns(w_gate), columns(w_up)], axis=2)
    wide = max(width, HEADS * HEAD)
    q_shard = jnp.pad(w_query.astype(BF16), ((0, 0), (0, wide - HEADS * HEAD)))
    o_shard = jnp.pad(w_out.astype(BF16), ((0, 0), (0, wide - width)))
    out_shard = w_out.shape[0]
    used = out_shard + shard
    qo_shard = jnp.pad(jnp.concatenate([o_shard, q_shard]), ((0, eights(used) - used), (0, 0)))
    pair, qo_shard, kv_along = lax.optimization_barrier((pair, qo_shard, kv_along))
    kv_own, pair, qo_shard = lax.optimization_barrier((links.across_plane(kv_along), pair, qo_shard))
    full_kv, gains, heads, seg_all = links.placed(
        kv_shard,
        kv_own,
        (
            (0, shard, 0, 2 * HEAD),
            (shard + rows, 0, shard, 4, True),
            (shard + rows, 4 * shard, head_shard, 2, True),
            (shard, rows, length),
        ),
    )
    h_in, k_proj, kv_low = kv_step(rows, length, tokens_flat, full_kv, gains, heads, cosine, sine)
    kv_low, qo_along, pair = lax.optimization_barrier((kv_low, links.along_z(qo_shard), links.exchange(pair)))
    pair = jnp.transpose(pair, (2, 0, 1, 3, 4)).reshape(2 * sx, sy * shard, units)
    kv, qo = links.window(
        kv_low,
        length,
        (
            lambda: (links.across_plane(qo_along),),
            lambda qo: (qo[0], links.swap(qo[0], "core") if links.pairs_only else qo[0]),
        ),
    )
    masks = (own_ids, seg_all)
    kv[2], pair = lax.optimization_barrier((kv[2], pair))
    full_pair = links.gather_cz(pair, 1).reshape(2, width, units)
    full_out, full_query = links.placed(
        qo_shard, qo[0], ((0, out_shard, 0, width), (out_shard, shard, 0, HEADS * HEAD)), qo[1]
    )

    q_proj, query, mixed, attn, resid, *h_ffn = attend(
        links, rows, length, h_in, tokens_flat, full_query, full_out, gains, heads, cosine, sine, masks, kv
    )
    parts_up = links.over_plane(h_ffn, lambda part: (part, *ffn_forward(part, full_pair, full_down)))
    h_parts, hidden, turn, act, ffn_terms = zip(*parts_up, strict=True)
    own, far, _ = links.sum_plane(ffn_terms)
    output, *d_ffn, sums_ffn = middle(rows, length, own, far, resid, cot_flat, gains)

    pending = list(zip(turn, act, strict=True))

    def back(part):
        return (part, *ffn_backward(part, *pending.pop(0), full_pair, full_down))

    d_parts, d_pairs, d_terms = zip(*links.over_plane(d_ffn, back), strict=True)
    block = sy * shard
    places = [
        [
            (c, ((z * 2 + k) * sx + x) * block, ((x * sc + c) * sz + z) * block, block)
            for x in range(sx)
            for c in range(sc)
            for z in range(sz)
        ]
        for k in range(2)
    ]
    half = units // 2
    down_places = [(c, 0, c * half, half) for c in range(sc)]

    def pair_down(kept, sent):
        sets = [([left], [one[None] for one in part]) for left, part in zip(hidden, d_parts, strict=True)]
        low = weight_grads(sets, [down_places])
        return (kept, links.swap(sent, "core"), *low)

    def pair_grads(*pairs):
        return weight_grads([(part, [pair]) for part, pair in zip(h_parts, pairs, strict=True)], places)

    own, far, (kept, got, *grad_down) = links.sum_plane(d_terms, d_pairs, (pair_grads, pair_down))
    own, far, half_pair = lax.optimization_barrier((own, far, (kept.astype(F32) + got.astype(F32)).astype(BF16)))
    grad_pair = links.sum_z_low(half_pair)

    def by_member(sums):
        return jnp.transpose(sums.reshape(2, sx, sy, shard, units), (1, 2, 0, 3, 4))

    def unpacked(got):
        got = got.reshape(sx, sy, 2, shard, sc, sz, chunk)[..., :hidden_shard]
        return jnp.transpose(got, (2, 3, 0, 4, 5, 1, 6)).reshape(2, shard, parts * hidden_shard).astype(F32)

    d_res, d_attn, d_qproj, sums_attn, heads_attn, *terms = attend_back(
        links, rows, length, own, far, cot_flat, resid, attn, q_proj, query, full_out, gains, heads, cosine, sine, masks, kv,
        links.window_kinds(length),
    )
    d_kv, beside = links.window_back(
        terms,
        length,
        (
            lambda: (
                links.sum_cores(*outer_grads(links.order("xyz"), (out_shard, shard), mixed, d_attn, h_in, d_qproj)),
                links.sum_cores(*grad_down),
            ),
            lambda second, low: (links.planes(second), low, grad_pair),
        ),
    )
    second, low, grad_pair = beside[1]
    grad_down = links.sum_z_low(low)[:hidden_shard].astype(F32)

    d_kvproj, grad_tokens, sums_in, heads_in = finish(
        rows, length, d_kv, k_proj, d_qproj, tokens_flat, d_res, full_query, full_kv, gains, heads, cosine, sine
    )
    gain_terms = (sums_ffn + sums_attn + sums_in)[:4]
    head_terms = (heads_attn + heads_in)[:2].reshape(2, parts, head_shard)
    head_terms = jnp.pad(head_terms, ((0, 0), (0, 0), (0, shard - head_shard))).reshape(2, width)
    small_terms = jnp.pad(jnp.concatenate([gain_terms, head_terms]), ((0, SMALL - 6), (0, 0)))
    d_kvproj, second, got_pair = lax.optimization_barrier(
        (d_kvproj, links.sum_halves(second, "y", 0), links.exchange(by_member(grad_pair)))
    )
    first_grad = first_grads(links.order("xyz"), shard, h_in, d_kvproj, small_terms)
    first_core, second, grad_down = lax.optimization_barrier((links.sum_cores(*first_grad), second, grad_down))
    first_got, second_sum = lax.optimization_barrier((links.to_members(first_core), links.sum_z(second, 0)))
    first_sum = links.sum_z(jnp.sum(first_got.astype(F32), axis=0).astype(BF16), 0)
    grad_pair = unpacked(got_pair)
    return (
        output.reshape(tokens.shape),
        grad_tokens.reshape(tokens.shape),
        second_sum[out_shard : out_shard + shard, : HEADS * HEAD],
        first_sum[:shard, SMALL : SMALL + HEAD],
        first_sum[:shard, SMALL + HEAD :],
        second_sum[:out_shard, :width],
        grad_pair[0],
        grad_pair[1],
        grad_down,
        *(first_sum[:shard, k] for k in range(4)),
        *(first_sum[:head_shard, 4 + k] for k in range(2)),
    )


def solution(mesh):
    plane = mesh.shape["dp"] // 2
    by_chip = Mesh(mesh.devices.reshape(plane, 2, -1, plane), AXES)
    links = Links(by_chip)
    placed = P(("x", "core"), ("z", "y"), None)
    matrix = P(AXES, None)
    vector = P(AXES)
    in_specs = (placed, P(("x", "core"), ("z", "y"))) + (matrix,) * 7 + (vector,) * 6 + (placed,)
    out_specs = (placed, placed) + (matrix,) * 7 + (vector,) * 6

    def step(*arguments):
        return on_device(links, *arguments)

    return jax.shard_map(step, mesh=by_chip, in_specs=in_specs, out_specs=out_specs, check_vma=False)
```

```python
import functools
import math

import jax
import jax.numpy as jnp
from jax import lax
from jax.experimental import pallas as pl
from jax.experimental.pallas import tpu as pltpu
from jax.sharding import Mesh
from jax.sharding import PartitionSpec as P

HEADS = 4
HEAD = 256
HALF = HEAD // 2
DOC_LIMIT = 512
EPSILON = 1e-06
ROPE_BASE = 1000000.0
NEG_FILL = -1e30
SCORE_SCALE = HEAD ** (-0.5)
SLOPE = math.sqrt(2.0 / math.pi)
F32 = jnp.float32
BF16 = jnp.bfloat16
PLANE = ("x", "y")
AXES = ("x", "core", "z", "y")
SWAP = [(0, 1), (1, 0)]
IN, POST_ATTN, PRE_FFN, POST_FFN = range(4)
SMALL = 128
ROOM = 58 << 20


def dot(left, right, dims):
    return lax.dot_general(left, right, (dims, ((), ())), preferred_element_type=F32)


def mm(left, right):
    return dot(left, right, ((1,), (0,)))


def mm_t(left, right):
    return dot(left, right, ((1,), (1,)))


def t_mm(left, right):
    return dot(left, right, ((0,), (0,)))


def inv_rms(values):
    return lax.rsqrt(jnp.mean(values * values, axis=-1, keepdims=True) + EPSILON)


def rms_back(values, gain_vec, d_norm):
    scale = inv_rms(values)
    unit = values * scale
    weighted = d_norm * gain_vec
    d_values = scale * (weighted - unit * jnp.mean(weighted * unit, axis=-1, keepdims=True))
    return d_values, d_norm * unit


def rope_tables(positions):
    inverse = ROPE_BASE ** (-(jnp.arange(HALF, dtype=F32) * 2.0 / HEAD))
    angles = positions.astype(F32)[..., None] * inverse
    return jnp.cos(angles), jnp.sin(angles)


def rotate(values, cosine, sine):
    first, second = values[:, :HALF], values[:, HALF:]
    return jnp.concatenate([first * cosine - second * sine, second * cosine + first * sine], axis=-1)


def eights(rows):
    return -(-rows // 8) * 8


def column_sum(terms):
    return jnp.sum(terms, axis=0, keepdims=True)


def call(body, grid, in_specs, out_specs, out_shape, flops, scratch=()):
    moved = sum(math.prod(one.shape) * one.dtype.itemsize for one in jax.tree.leaves(out_shape))
    return pl.pallas_call(
        body,
        grid=grid,
        in_specs=in_specs,
        out_specs=out_specs,
        out_shape=out_shape,
        scratch_shapes=list(scratch),
        compiler_params=pltpu.CompilerParams(vmem_limit_bytes=ROOM),
        cost_estimate=pl.CostEstimate(flops=flops, bytes_accessed=2 * moved, transcendentals=0),
    )


def shaped(*shape, dtype=F32):
    return jax.ShapeDtypeStruct(shape, dtype)


def whole(*shape):
    return pl.BlockSpec(shape, lambda i: (0,) * len(shape))


def rows_of(tile, width):
    return pl.BlockSpec((tile, width), lambda i: (i, 0))


def row_block(*shape):
    return pl.BlockSpec((1,) + shape, lambda i: (i,) + (0,) * len(shape))


def part_specs(tile, width, arrays):
    if len(arrays) == 1:
        return [rows_of(tile, width)]
    half = arrays[0].shape[0] // tile
    return [
        pl.BlockSpec((tile, width), lambda i: (jnp.minimum(i, half - 1), 0)),
        pl.BlockSpec((tile, width), lambda i: (jnp.maximum(i - half, 0), 0)),
    ]


def in_second():
    return pl.program_id(0) >= pl.num_programs(0) // 2


def load_part(refs):
    if len(refs) == 1:
        return refs[0][...]
    return lax.select_n(in_second(), refs[0][...], refs[1][...])


def store_part(refs, value):
    if len(refs) == 1:
        refs[0][...] = value
        return

    @pl.when(in_second() == False)
    def _():
        refs[0][...] = value

    @pl.when(in_second())
    def _():
        refs[1][...] = value


def kv_body(tok_ref, wkv_ref, gains_ref, head_ref, cos_ref, sin_ref, h_ref, kproj_ref, kv_ref):
    tokens = tok_ref[...].astype(F32)
    h = (tokens * inv_rms(tokens) * gains_ref[IN : IN + 1]).astype(BF16)
    h_ref[...] = h
    proj = mm(h, wkv_ref[...])
    k_proj = proj[:, :HEAD]
    kproj_ref[...] = k_proj
    key = rotate(k_proj * inv_rms(k_proj) * head_ref[1:2], cos_ref[...], sin_ref[...])
    kv_ref[0, :, :HEAD] = key.astype(BF16)
    kv_ref[0, :, HEAD:] = proj[:, HEAD:].astype(BF16)


def kv_step(rows, length, tokens, wkv, gains, heads, cosine, sine):
    count, width = tokens.shape
    return call(
        kv_body,
        (rows,),
        [rows_of(length, width), whole(*wkv.shape), whole(*gains.shape), whole(*heads.shape)]
        + [whole(length, HALF)] * 2,
        [rows_of(length, width), rows_of(length, HEAD), row_block(length, 2 * HEAD)],
        [shaped(count, width, dtype=BF16), shaped(count, HEAD), shaped(rows, length, 2 * HEAD, dtype=BF16)],
        2 * count * width * 2 * HEAD,
    )(tokens, wkv, gains, heads, cosine, sine)


def by_head(array):
    return jnp.concatenate([array[:, h * HEAD : (h + 1) * HEAD] for h in range(HEADS)], axis=0)


def by_lane(array):
    part = array.shape[0] // HEADS
    return jnp.concatenate([array[h * part : (h + 1) * part] for h in range(HEADS)], axis=1)


def probs_of(links, query, keys, own_ref, seg_ref):
    length = own_ref.shape[0]
    bases = links.window_bases(length)
    here = links.position(length)
    step = lax.broadcasted_iota(jnp.int32, (1, length), 1)
    segs, later = [], []
    for base in bases:
        row = seg_ref[0, pl.ds(jnp.maximum(base, 0) // length, 1), :]
        segs.append(jnp.where(base >= 0, row, -1.0))
        later.append(base - here + step)
    own_step = lax.broadcasted_iota(jnp.int32, (length, 1), 0)
    allowed = (own_ref[...] == jnp.concatenate(segs, axis=1)) & (jnp.concatenate(later, axis=1) <= own_step)
    allowed = jnp.concatenate([allowed.astype(F32)] * HEADS, axis=0) > 0.5
    scores = jnp.where(allowed, mm_t(query, keys) * SCORE_SCALE, NEG_FILL)
    powers = jnp.exp(scores - jnp.max(scores, axis=-1, keepdims=True))
    return powers / jnp.sum(powers, axis=-1, keepdims=True)


def attend_body(links, blocks, *refs):
    (h_ref, tok_ref, wq_ref, wo_ref, gains_ref, head_ref, cos_ref, sin_ref) = refs[:8]
    masks, kv_refs = refs[8:10], refs[10 : 10 + blocks]
    qproj_ref, query_ref, mixed_ref, attn_ref, resid_ref, *hffn_refs = refs[10 + blocks :]
    proj = mm(h_ref[...], wq_ref[...])
    qproj_ref[...] = proj
    cosine, sine = cos_ref[...], sin_ref[...]
    query = []
    for h in range(HEADS):
        one = proj[:, h * HEAD : (h + 1) * HEAD]
        query.append(rotate(one * inv_rms(one) * head_ref[0:1], cosine, sine).astype(BF16))
    query_ref[...] = jnp.concatenate(query, axis=1)
    keys = jnp.concatenate([one[0, :, :HEAD] for one in kv_refs], axis=0)
    values = jnp.concatenate([one[0, :, HEAD:] for one in kv_refs], axis=0)
    probs = probs_of(links, jnp.concatenate(query, axis=0), keys, *masks).astype(BF16)
    mixed = by_lane(mm(probs, values).astype(BF16))
    mixed_ref[...] = mixed
    attn = mm(mixed, wo_ref[...])
    attn_ref[...] = attn
    resid = tok_ref[...].astype(F32) + attn * inv_rms(attn) * gains_ref[POST_ATTN : POST_ATTN + 1]
    resid_ref[...] = resid
    store_part(hffn_refs, (resid * inv_rms(resid) * gains_ref[PRE_FFN : PRE_FFN + 1]).astype(BF16))


def mask_specs(masks):
    own, segs = masks
    return [rows_of(own.shape[0] // segs.shape[0], 1), row_block(*segs.shape[1:])]


def attend(links, rows, length, h, tokens, wq, wo, gains, heads, cosine, sine, masks, kv):
    count, width = tokens.shape
    wide = HEADS * HEAD
    window = len(kv) * length
    halves = [shaped(count // 2, width, dtype=BF16)] * 2
    return call(
        functools.partial(attend_body, links, len(kv)),
        (rows,),
        [rows_of(length, width)] * 2
        + [whole(*one.shape) for one in (wq, wo, gains, heads)]
        + [whole(length, HALF)] * 2
        + mask_specs(masks)
        + [row_block(length, 2 * HEAD)] * len(kv),
        [rows_of(length, wide)] * 3 + [rows_of(length, width)] * 2 + part_specs(length, width, halves),
        [
            shaped(count, wide),
            shaped(count, wide, dtype=BF16),
            shaped(count, wide, dtype=BF16),
            shaped(count, width),
            shaped(count, width),
            *halves,
        ],
        4 * count * wide * (width + window),
    )(h, tokens, wq, wo, gains, heads, cosine, sine, *masks, *kv)


def attend_back_body(links, blocks, *refs):
    own_refs, far_refs, refs = refs[:2], refs[2:4], refs[4:]
    (cot_ref, resid_ref, attn_ref, qproj_ref, query_ref, wo_ref, gains_ref, head_ref, cos_ref, sin_ref) = refs[:10]
    masks, kv_refs = refs[10:12], refs[12 : 12 + blocks]
    dres_ref, dattn_ref, dq_ref, sums_ref, head_sums_ref = refs[12 + blocks : 17 + blocks]
    term_refs = refs[17 + blocks :]
    d_norm, pre_terms = rms_back(resid_ref[...], gains_ref[PRE_FFN : PRE_FFN + 1], load_part(own_refs) + load_part(far_refs).astype(F32))
    d_res = cot_ref[...].astype(F32) + d_norm
    dres_ref[...] = d_res
    d_attn, post_terms = rms_back(attn_ref[...], gains_ref[POST_ATTN : POST_ATTN + 1], d_res)
    d_attn = d_attn.astype(BF16)
    dattn_ref[...] = d_attn
    d_mixed = by_head(mm_t(d_attn, wo_ref[...]).astype(BF16))
    query = by_head(query_ref[...])
    keys = jnp.concatenate([one[0, :, :HEAD] for one in kv_refs], axis=0)
    values = jnp.concatenate([one[0, :, HEAD:] for one in kv_refs], axis=0)
    probs = probs_of(links, query, keys, *masks)
    d_probs = mm_t(d_mixed, values)
    d_scores = (probs * (d_probs - jnp.sum(d_probs * probs, axis=-1, keepdims=True))).astype(BF16)
    key_terms = t_mm(d_scores, query) * SCORE_SCALE
    value_terms = t_mm(probs.astype(BF16), d_mixed)
    length = query_ref.shape[0]
    for k, ref in enumerate(term_refs):
        at = slice(k * length, (k + 1) * length)
        ref[0, :, :HEAD] = key_terms[at].astype(ref.dtype)
        ref[0, :, HEAD:] = value_terms[at].astype(ref.dtype)
    d_query = mm(d_scores, keys) * SCORE_SCALE
    cosine, sine = cos_ref[...], -sin_ref[...]
    head_sum = jnp.zeros((1, HEAD), F32)
    for h in range(HEADS):
        turned = rotate(d_query[h * length : (h + 1) * length], cosine, sine)
        lanes = slice(h * HEAD, (h + 1) * HEAD)
        d_proj, terms = rms_back(qproj_ref[:, lanes], head_ref[0:1], turned)
        dq_ref[:, lanes] = d_proj.astype(BF16)
        head_sum += column_sum(terms)

    @pl.when(pl.program_id(0) == 0)
    def _():
        sums_ref[...] = jnp.zeros_like(sums_ref)
        head_sums_ref[...] = jnp.zeros_like(head_sums_ref)

    sums_ref[POST_ATTN : POST_ATTN + 1] += column_sum(post_terms)
    sums_ref[PRE_FFN : PRE_FFN + 1] += column_sum(pre_terms)
    head_sums_ref[0:1] += head_sum


def attend_back(links, rows, length, own, far, cot, resid, attn, qproj, query, wo, gains, heads, cosine, sine, masks, kv, kinds):
    count, width = cot.shape
    wide = HEADS * HEAD
    window = len(kv) * length
    return call(
        functools.partial(attend_back_body, links, len(kv)),
        (rows,),
        part_specs(length, width, own) * 2
        + [rows_of(length, width)] * 3
        + [rows_of(length, wide)] * 2
        + [whole(*one.shape) for one in (wo, gains, heads)]
        + [whole(length, HALF)] * 2
        + mask_specs(masks)
        + [row_block(length, 2 * HEAD)] * len(kv),
        [rows_of(length, width)] * 2
        + [rows_of(length, wide), whole(8, width), whole(8, HEAD)]
        + [row_block(length, 2 * HEAD)] * len(kv),
        [
            shaped(count, width),
            shaped(count, width, dtype=BF16),
            shaped(count, wide, dtype=BF16),
            shaped(8, width),
            shaped(8, HEAD),
        ]
        + [shaped(rows, length, 2 * HEAD, dtype=kind) for kind in kinds],
        2 * count * wide * (width + 5 * window),
    )(*own, *far, cot, resid, attn, qproj, query, wo, gains, heads, cosine, sine, *masks, *kv)


def finish_body(many, *refs):
    finish_rows(refs[:many], *refs[many:])


def finish_rows(dkv_refs, kproj_ref, dq_ref, tok_ref, dres_ref, wq_ref, wkv_ref, gains_ref, head_ref, cos_ref, sin_ref,
                dkvp_ref, grad_ref, sums_ref, head_sums_ref):
    d_kv = sum(ref[0].astype(F32) for ref in dkv_refs)
    turned = rotate(d_kv[:, :HEAD], cos_ref[...], -sin_ref[...])
    d_key, key_terms = rms_back(kproj_ref[...], head_ref[1:2], turned)
    d_proj = jnp.concatenate([d_key.astype(BF16), d_kv[:, HEAD:].astype(BF16)], axis=1)
    dkvp_ref[...] = d_proj
    d_hin = mm_t(dq_ref[...], wq_ref[...]) + mm_t(d_proj, wkv_ref[...])
    d_tokens, in_terms = rms_back(tok_ref[...].astype(F32), gains_ref[IN : IN + 1], d_hin)
    grad_ref[...] = (dres_ref[...] + d_tokens).astype(BF16)

    @pl.when(pl.program_id(0) == 0)
    def _():
        sums_ref[...] = jnp.zeros_like(sums_ref)
        head_sums_ref[...] = jnp.zeros_like(head_sums_ref)

    sums_ref[IN : IN + 1] += column_sum(in_terms)
    head_sums_ref[1:2] += column_sum(key_terms)


def finish(rows, length, dkv, kproj, dq, tokens, dres, wq, wkv, gains, heads, cosine, sine):
    count, width = tokens.shape
    wide = HEADS * HEAD
    return call(
        functools.partial(finish_body, len(dkv)),
        (rows,),
        [row_block(length, 2 * HEAD)] * len(dkv)
        + [rows_of(length, HEAD), rows_of(length, wide)]
        + [rows_of(length, width)] * 2
        + [whole(*one.shape) for one in (wq, wkv, gains, heads)]
        + [whole(length, HALF)] * 2,
        [rows_of(length, 2 * HEAD), rows_of(length, width), whole(8, width), whole(8, HEAD)],
        [shaped(count, 2 * HEAD, dtype=BF16), shaped(count, width, dtype=BF16), shaped(8, width), shaped(8, HEAD)],
        2 * count * width * (wide + 2 * HEAD),
    )(*dkv, kproj, dq, tokens, dres, wq, wkv, gains, heads, cosine, sine)


def pieces_of(total, step):
    return [(k, min(step, total - k)) for k in range(0, total, step)]


def up_body(step, many, *refs):
    pair_ref, down_ref, hidden_ref, turn_ref, act_ref = refs[many : many + 5]
    h = load_part(refs[:many])
    for at, wide in pieces_of(hidden_ref.shape[1], step):
        cols = pl.ds(at, wide)
        gate = mm(h, pair_ref[0, :, cols])
        up = mm(h, pair_ref[1, :, cols])
        square = gate * gate
        bent = jnp.tanh(gate * (SLOPE + SLOPE * 0.044715 * square))
        half = 0.5 + 0.5 * bent
        act = gate * half
        d_act = half + 0.5 * gate * (1.0 - bent * bent) * (SLOPE + 3 * SLOPE * 0.044715 * square)
        hidden_ref[:, cols] = (act * up).astype(BF16)
        turn_ref[:, cols] = (up * d_act).astype(BF16)
        act_ref[:, cols] = act.astype(BF16)
    store_part(refs[many + 5 :], mm(hidden_ref[...], down_ref[...]).astype(BF16))


def ffn_forward(h, pair, down, tile=256, step=256):
    count, width = sum(one.shape[0] for one in h), h[0].shape[1]
    units = pair.shape[2]
    specs = part_specs(tile, width, h)
    hidden, turn, act, *terms = call(
        functools.partial(up_body, step, len(h)),
        (count // tile,),
        specs + [whole(2, width, units), whole(units, width)],
        [rows_of(tile, units)] * 3 + specs,
        [shaped(count, units, dtype=BF16)] * 3 + [shaped(*one.shape, dtype=BF16) for one in h],
        6 * count * width * units,
    )(*h, pair, down)
    return hidden, turn, act, terms


def down_body(step, many, *refs):
    turn_ref, act_ref, pair_ref, down_ref, pair_out = refs[many : many + 5]
    d = load_part(refs[:many])
    for at, wide in pieces_of(turn_ref.shape[1], step):
        cols = pl.ds(at, wide)
        d_hidden = mm_t(d, down_ref[cols, :])
        pair_out[0, :, cols] = (d_hidden * turn_ref[:, cols].astype(F32)).astype(BF16)
        pair_out[1, :, cols] = (d_hidden * act_ref[:, cols].astype(F32)).astype(BF16)
    store_part(refs[many + 5 :], (mm_t(pair_out[0], pair_ref[0]) + mm_t(pair_out[1], pair_ref[1])).astype(BF16))


def ffn_backward(d, turn, act, pair, down, tile=256, step=256):
    count, width = sum(one.shape[0] for one in d), d[0].shape[1]
    units = pair.shape[2]
    specs = part_specs(tile, width, d)
    d_pair, *terms = call(
        functools.partial(down_body, step, len(d)),
        (count // tile,),
        specs + [rows_of(tile, units), rows_of(tile, units), whole(2, width, units), whole(units, width)],
        [pl.BlockSpec((2, tile, units), lambda i: (0, i, 0))] + specs,
        [shaped(2, count, units, dtype=BF16)] + [shaped(*one.shape, dtype=BF16) for one in d],
        6 * count * width * units,
    )(*d, turn, act, pair, down)
    return d_pair, terms


def put(kept_ref, sent_ref, core, index, value):
    @pl.when(lax.axis_index("core") == core)
    def _():
        kept_ref[index] = value

    @pl.when(lax.axis_index("core") != core)
    def _():
        sent_ref[index] = value


def grads_body(places, sets, *refs):
    kept_ref, sent_ref = refs[-2:]
    total, at = None, 0
    for lefts, rights in sets:
        values = []
        for many in (lefts, rights):
            pieces = [ref[...] if len(ref.shape) == 2 else ref[0] for ref in refs[at : at + many]]
            values.append(jnp.concatenate(pieces, axis=0) if many > 1 else pieces[0])
            at += many
        term = t_mm(*values)
        total = term if total is None else total + term
    total = total.astype(BF16)
    tile = total.shape[0]
    for which, moves in enumerate(places):
        for k in range(sum(count for _, _, _, count in moves) // tile):

            @pl.when((pl.program_id(0) == which) & (pl.program_id(1) == k))
            def _(k=k, moves=moves):
                for core, at, row, count in moves:
                    begin, end = max(row, k * tile), min(row + count, (k + 1) * tile)
                    if begin < end:
                        to = at + begin - row
                        index = (slice(to, to + end - begin), slice(None))
                        put(kept_ref, sent_ref, core, index, total[begin - k * tile : end - k * tile])


def weight_grads(sets, places):
    rows, cols = sets[0][0][0].shape[1], sets[0][1][0].shape[2]
    count = sum(one.shape[0] for lefts, _ in sets for one in lefts)
    tile = 384 if rows % 384 == 0 else 256
    out = len(places) * rows // 2
    specs, arrays = [], []
    for lefts, rights in sets:
        specs += [pl.BlockSpec((one.shape[0], tile), lambda k, i: (0, i)) for one in lefts]
        specs += [pl.BlockSpec((1,) + one.shape[1:], lambda k, i: (k, 0, 0)) for one in rights]
        arrays += [*lefts, *rights]
    return call(
        functools.partial(grads_body, places, [(len(lefts), len(rights)) for lefts, rights in sets]),
        (len(places), rows // tile),
        specs,
        [pl.BlockSpec((out, cols), lambda k, i: (0, 0))] * 2,
        [shaped(out, cols, dtype=BF16)] * 2,
        2 * len(places) * count * rows * cols,
    )(*arrays)


def outer_body(order, shards, mixed_ref, dattn_ref, h_ref, dq_ref, kept_ref, sent_ref):
    lanes = kept_ref.shape[2]
    at = 0
    for rows, left, right in ((shards[0], mixed_ref, dattn_ref), (shards[1], h_ref, dq_ref)):
        total = t_mm(left[...], right[...]).astype(BF16)
        wide = total.shape[1]
        for core, place, number in order:
            index = (place, slice(at, at + rows), slice(0, wide))
            put(kept_ref, sent_ref, core, index, total[number * rows : (number + 1) * rows])
        for ref in (kept_ref, sent_ref):
            if wide < lanes:
                ref[:, at : at + rows, wide:] = jnp.zeros((ref.shape[0], rows, lanes - wide), BF16)
        at += rows
    for ref in (kept_ref, sent_ref):
        if at < ref.shape[1]:
            ref[:, at:, :] = jnp.zeros((ref.shape[0], ref.shape[1] - at, lanes), BF16)


def outer_grads(order, shards, mixed, d_attn, h, d_q):
    count = mixed.shape[0]
    shape = (len(order) // 2, eights(sum(shards)), max(d_attn.shape[1], d_q.shape[1]))
    return call(
        functools.partial(outer_body, order, shards),
        (1,),
        [whole(*one.shape) for one in (mixed, d_attn, h, d_q)],
        [whole(*shape)] * 2,
        [shaped(*shape, dtype=BF16)] * 2,
        2 * count * (mixed.shape[1] * d_attn.shape[1] + h.shape[1] * d_q.shape[1]),
    )(mixed, d_attn, h, d_q)


def first_body(order, shard, h_ref, dkv_ref, small_ref, kept_ref, sent_ref):
    small = small_ref[...].T.astype(BF16)
    total = t_mm(h_ref[...], dkv_ref[...]).astype(BF16)
    for core, place, number in order:
        rows = slice(number * shard, (number + 1) * shard)
        put(kept_ref, sent_ref, core, (place, slice(0, shard), slice(0, SMALL)), small[rows])
        put(kept_ref, sent_ref, core, (place, slice(0, shard), slice(SMALL, None)), total[rows])
    for ref in (kept_ref, sent_ref):
        if shard < ref.shape[1]:
            ref[:, shard:, :] = jnp.zeros((ref.shape[0], ref.shape[1] - shard, ref.shape[2]), BF16)


def first_grads(order, shard, h, d_kv, small):
    count, rows = h.shape
    shape = (len(order) // 2, eights(shard), d_kv.shape[1] + SMALL)
    return call(
        functools.partial(first_body, order, shard),
        (1,),
        [whole(*one.shape) for one in (h, d_kv, small)],
        [whole(*shape)] * 2,
        [shaped(*shape, dtype=BF16)] * 2,
        2 * count * rows * d_kv.shape[1],
    )(h, d_kv, small)


def middle_body(own_a, own_b, far_a, far_b, resid_ref, cot_ref, gains_ref, out_ref, dffn_a, dffn_b, sums_ref):
    ffn = load_part((own_a, own_b)) + load_part((far_a, far_b)).astype(F32)
    gain = gains_ref[POST_FFN : POST_FFN + 1]
    out_ref[...] = (resid_ref[...] + ffn * inv_rms(ffn) * gain).astype(BF16)
    d_ffn, terms = rms_back(ffn, gain, cot_ref[...].astype(F32))
    store_part((dffn_a, dffn_b), d_ffn.astype(BF16))

    @pl.when(pl.program_id(0) == 0)
    def _():
        sums_ref[...] = jnp.zeros_like(sums_ref)

    sums_ref[POST_FFN : POST_FFN + 1] += column_sum(terms)


def middle(rows, length, own, far, resid, cot, gains):
    count, width = resid.shape
    specs = part_specs(length, width, own)
    return call(
        middle_body,
        (rows,),
        specs * 2 + [rows_of(length, width)] * 2 + [whole(*gains.shape)],
        [rows_of(length, width)] + specs + [whole(8, width)],
        [shaped(count, width, dtype=BF16)] + [shaped(count // 2, width, dtype=BF16)] * 2 + [shaped(8, width)],
        20 * count * width,
    )(*own, *far, resid, cot, gains)


def place_body(links, shard, parts, own_ref, other_ref, *refs):
    outs, scratch = refs[:-1], refs[-1]
    depth = links.size["z"]
    at_x, at_c, at_z, at_y = (links.index(axis) for axis in AXES)
    number = 0
    for x in range(2):
        for core in range(2):
            for z in range(depth):
                for y in range(2):
                    slot = jnp.abs(at_x - x) + 2 * jnp.abs(at_y - y)
                    slot = slot * depth + jnp.remainder(at_z - z + depth, depth)
                    mine = own_ref[slot].astype(F32)
                    theirs = other_ref[slot].astype(F32)
                    piece = jnp.where(at_c == core, mine, theirs)
                    scratch[number] = piece
                    number += 1
    for part, out in zip(parts, outs, strict=True):
        for k in range(number):
            if len(part) == 4:
                first, count, at, lanes = part
                out[k * count : (k + 1) * count, :] = scratch[k, first : first + count, at : at + lanes].astype(out.dtype)
                continue
            if len(part) == 3:
                first, count, lanes = part
                if k < 2 * depth:
                    ids = scratch[(at_x * 2 + at_c) * 2 * depth + k]
                    for row in range(count):
                        out[row, k : k + 1, :] = ids[first + row : first + row + 1, :lanes]
                continue
            row, at, lanes, vectors = part[:4]
            for v in range(vectors):
                begin = at + v * lanes
                out[v : v + 1, k * lanes : (k + 1) * lanes] = scratch[k, row : row + 1, begin : begin + lanes]


def placed(links, own, other, parts):
    slots, rows, lanes = own.shape
    number = 2 * slots
    return pl.pallas_call(
        functools.partial(place_body, links, rows, parts),
        out_shape=[
            shaped(number * part[1], part[3], dtype=BF16)
            if len(part) == 4
            else shaped(part[1], slots // 2, part[2])
            if len(part) == 3
            else shaped(8, number * part[2])
            for part in parts
        ],
        scratch_shapes=[pltpu.VMEM((number, rows, lanes), F32)],
        compiler_params=pltpu.CompilerParams(vmem_limit_bytes=ROOM),
    )(own, other)


class Links:
    def __init__(self, mesh):
        self.size = dict(mesh.shape)
        self.pairs_only = self.size["x"] == 2 and self.size["y"] == 2

    def index(self, axis):
        return lax.axis_index(axis)

    def swap(self, array, axis):
        return lax.ppermute(array, axis, SWAP)

    def shift(self, array, step):
        depth = self.size["z"]
        pairs = [(i, i + step) for i in range(depth) if 0 <= i + step < depth]
        return lax.ppermute(array, "z", pairs)

    def turn(self, array, step):
        depth = self.size["z"]
        return lax.ppermute(array, "z", [(i, (i + step) % depth) for i in range(depth)])

    def ordered(self, own, other, axis):
        first = self.index(axis) == 0
        return jnp.where(first, jnp.stack([own, other]), jnp.stack([other, own]))

    def along_z(self, array):
        return jnp.stack([array] + [self.turn(array, k) for k in range(1, self.size["z"])])

    def across_plane(self, along):
        if not self.pairs_only:
            return along
        across = lax.ppermute(along, PLANE, [(k, 3 - k) for k in range(4)])
        return jnp.concatenate([along, self.swap(along, "x"), self.swap(along, "y"), across])

    def placed(self, array, own, parts, other=None):
        if self.pairs_only:
            other = self.swap(own, "core") if other is None else other
            return placed(self, own, other, parts)
        full = lax.all_gather(array, AXES, axis=0)
        cuts = []
        for part in parts:
            if len(part) == 4:
                r, n, c, w = part
                cuts.append(full[:, r : r + n, c : c + w].reshape(-1, w))
            elif len(part) == 3:
                r, n, w = part
                blocks = self.size["z"] * self.size["y"]
                at = (self.index("x") * 2 + self.index("core")) * blocks
                ids = lax.dynamic_slice_in_dim(full[:, r : r + n, :w], at, blocks)
                cuts.append(jnp.swapaxes(ids, 0, 1).astype(F32))
            else:
                r, c, w, n = part[:4]
                rows = jnp.swapaxes(full[:, r, c : c + n * w].reshape(-1, n, w), 0, 1).reshape(n, -1)
                cuts.append(jnp.pad(rows.astype(F32), ((0, 8 - n), (0, 0))))
        return cuts

    def order(self, axes):
        found = []
        counts = [self.size[axis] for axis in AXES]
        for number in range(math.prod(counts)):
            at, rest = {}, number
            for axis, many in zip(AXES[::-1], counts[::-1], strict=True):
                at[axis], rest = rest % many, rest // many
            place = 0
            for axis in axes:
                place = place * self.size[axis] + at[axis]
            found.append((at["core"], place, number))
        return found

    def gather_cz(self, array, dim):
        return lax.all_gather(array, ("core", "z"), axis=dim, tiled=True)

    def sum_halves(self, array, axis, dim):
        if self.size[axis] == 2:
            at = self.index(axis)
            sent = self.swap(lax.dynamic_index_in_dim(array, 1 - at, dim, False), axis)
            kept = lax.dynamic_index_in_dim(array, at, dim, False)
            return (kept.astype(F32) + sent.astype(F32)).astype(array.dtype)
        return lax.psum_scatter(array, axis, scatter_dimension=dim, tiled=False)

    def sum_cores(self, kept, sent):
        return (kept.astype(F32) + self.swap(sent, "core").astype(F32)).astype(kept.dtype)

    def sum_z(self, array, dim):
        depth = self.size["z"]
        z = self.index("z")

        def block(k):
            return lax.dynamic_index_in_dim(array, jnp.remainder(z + k, depth), dim, False)

        total = block(0).astype(F32)
        for k in range(1, depth):
            total = total + self.turn(block(k), k).astype(F32)
        return total

    def sum_z_low(self, array):
        return lax.psum_scatter(array, "z", scatter_dimension=0, tiled=True)

    def planes(self, array):
        sx, sy, sz = (self.size[axis] for axis in "xyz")
        return self.sum_halves(array.reshape((sx, sy, sz) + array.shape[1:]), "x", 0)

    def to_members(self, array):
        count = self.size["x"] * self.size["y"]
        got = lax.all_to_all(array.reshape((count, -1) + array.shape[2:]), PLANE, 0, 0, tiled=True)
        return got.reshape((count, self.size["z"]) + array.shape[1:])

    def exchange(self, array):
        count = self.size["x"] * self.size["y"]
        flat = array.reshape((count,) + array.shape[2:])
        return lax.all_to_all(flat, PLANE, 0, 0, tiled=True).reshape(array.shape)

    def over_plane(self, halves, first):
        if not self.pairs_only:
            return [first([lax.all_gather(jnp.concatenate(halves), PLANE, axis=0, tiled=True)])]
        upper, lower = halves
        size = 2 * upper.shape[0]
        near = lax.optimization_barrier((self.swap(upper, "x"), self.swap(lower, "y")))
        near = jnp.concatenate([upper, near[0], lower, near[1]])
        upper, lower, near = lax.optimization_barrier((near[:size], near[size:], near))
        upper, lower, done = lax.optimization_barrier((self.swap(upper, "y"), self.swap(lower, "x"), first([near])))
        return [done, first([upper, lower])]

    def sum_plane(self, parts, held=(), beside=(None, None)):
        works = [work or (lambda *given: ()) for work in beside]
        if not self.pairs_only:
            total = lax.psum_scatter(parts[0][0], PLANE, scatter_dimension=0, tiled=True).astype(F32)
            half = total.shape[0] // 2
            empty = [jnp.zeros((half, total.shape[1]), BF16)] * 2
            return [total[:half], total[half:]], empty, works[1](*works[0](*held))
        (near,), (upper, lower) = parts
        quarter = upper.shape[0] // 2
        upper, lower, held = lax.optimization_barrier((upper, lower, tuple(held)))
        upper, lower, extra = lax.optimization_barrier((self.swap(upper, "y"), self.swap(lower, "x"), works[0](*held)))
        at = [near[k * quarter : (k + 1) * quarter].astype(F32) for k in range(4)]
        own = [at[0] + upper[:quarter].astype(F32), at[2] + lower[:quarter].astype(F32)]
        upper = (at[1] + upper[quarter:].astype(F32)).astype(BF16)
        lower = (at[3] + lower[quarter:].astype(F32)).astype(BF16)
        upper, lower, extra = lax.optimization_barrier((upper, lower, extra))
        upper, lower, extra = lax.optimization_barrier((self.swap(upper, "x"), self.swap(lower, "y"), works[1](*extra)))
        return own, [upper, lower], extra

    def position(self, length):
        return (self.index("z") * self.size["y"] + self.index("y")) * length

    def window_bases(self, length):
        z, y, wide = self.index("z"), self.index("y"), self.size["y"]
        span = wide * length
        reach = -(-(DOC_LIMIT - 1) // span)
        base = self.position(length)
        if wide == 2 and reach == 2:
            cross = jnp.where(y == 0, z * span - length, z * span)
            return [base, base - span, base - 2 * span, cross, cross - span]
        return [(z - k) * span + j * length for k in range(reach + 1) for j in range(wide)]

    def window(self, array, length, beside):
        wide = self.size["y"]
        reach = -(-(DOC_LIMIT - 1) // (wide * length))
        if wide == 2 and reach == 2:
            first = self.index("y") == 0
            one, two, extra = lax.optimization_barrier((self.shift(array, 1), self.shift(array, 2), beside[0]()))
            near = self.swap(jnp.where(first, array, one), "y")
            far = self.swap(jnp.where(first, one, two), "y")
            near, far, extra = lax.optimization_barrier((near, far, beside[1](extra)))
            return [array, one, two, near, far], extra
        along = [lax.all_gather(array, "y", axis=0)]
        for _ in range(reach):
            along.append(self.shift(along[-1], 1))
        return [level[j] for level in along for j in range(wide)], beside[1](beside[0]())

    def window_kinds(self, length):
        if self.size["y"] == 2 and 2 * length * 2 >= DOC_LIMIT - 1 > 2 * length:
            return [F32, F32, F32, BF16, BF16]
        return [F32] * len(self.window_bases(length))

    def window_back(self, terms, length, beside=()):
        wide = self.size["y"]
        span = wide * length
        reach = -(-(DOC_LIMIT - 1) // span)
        results = []

        def follow(*arrays):
            if len(results) < len(beside):
                results.append(beside[len(results)](*(results[-1] if results else ())))
                *arrays, results[-1] = lax.optimization_barrier((*arrays, results[-1]))
            return arrays

        if wide == 2 and reach == 2:
            first = self.index("y") == 0
            own, one, two, near, far = terms
            far, near = follow(self.swap(far, "y"), self.swap(near, "y"))
            far, near = far.astype(F32), near.astype(F32)
            two = (two + jnp.where(first, 0.0, far)).astype(BF16)
            one = (one + jnp.where(first, far, near)).astype(BF16)
            own = own + jnp.where(first, near, 0.0)
            two, one, own = follow(self.shift(two, -2), self.shift(one, -1), own)
            return [own, one, two], results
        total = None
        for k in range(reach, -1, -1):
            level = jnp.stack(terms[k * wide : (k + 1) * wide])
            total = level if total is None else level + self.shift(total.astype(BF16), -1).astype(F32)
        total = lax.psum_scatter(total.astype(BF16), "y", scatter_dimension=0, tiled=False).astype(F32)
        for _ in beside:
            (total,) = follow(total)
        return [total], results


def on_device(
    links,
    tokens,
    segment_ids,
    w_query,
    w_key,
    w_value,
    w_out,
    w_gate,
    w_up,
    w_down,
    g_in,
    g_post_attn,
    g_pre_ffn,
    g_post_ffn,
    g_query,
    g_key,
    cotangent,
):
    rows, length, width = tokens.shape
    count = rows * length
    size = links.size
    sx, sc, sz, sy = (size[axis] for axis in AXES)
    parts = sx * sc * sz * sy
    shard = w_gate.shape[0]
    hidden_shard = w_down.shape[0]
    chunk = -(-hidden_shard // 16) * 16
    units = sc * sz * chunk
    head_shard = g_query.shape[0]
    tokens_flat = tokens.reshape(count, width)
    cot_flat = cotangent.reshape(count, width)

    step = jnp.arange(length, dtype=jnp.int32)
    pos_own = links.position(length) + step
    cosine, sine = rope_tables(pos_own)

    lanes = 2 * HEAD + SMALL
    vectors = jnp.concatenate([g_in, g_post_attn, g_pre_ffn, g_post_ffn, g_query, g_key])
    vectors = lax.optimization_barrier(jnp.pad(vectors, (0, 2 * HEAD - vectors.shape[0])))[None]
    seg_rows = jnp.pad(segment_ids.astype(F32), ((0, 0), (0, 2 * HEAD - length)))
    used = shard + rows + 1
    kv_shard = jnp.concatenate([jnp.concatenate([w_key, w_value], axis=1), seg_rows, vectors]).astype(BF16)
    kv_shard = jnp.pad(kv_shard, ((0, eights(used) - used), (0, 0)))
    own_ids = segment_ids.astype(F32).reshape(count, 1)
    kv_shard, own_ids, w_gate, w_up, w_down, w_query, w_out = lax.optimization_barrier(
        (kv_shard, own_ids, w_gate, w_up, w_down, w_query, w_out)
    )
    kv_along = links.along_z(kv_shard)
    full_down = links.gather_cz(jnp.pad(w_down.astype(BF16), ((0, chunk - hidden_shard), (0, 0))), 0)

    def columns(weight):
        split = weight.astype(BF16).reshape(shard, sx, sc, sz, sy, hidden_shard)
        split = jnp.pad(split, ((0, 0),) * 5 + ((0, chunk - hidden_shard),))
        return jnp.transpose(split, (1, 4, 0, 2, 3, 5)).reshape(sx, sy, shard, units)

    pair = jnp.stack([columns(w_gate), columns(w_up)], axis=2)
    wide = max(width, HEADS * HEAD)
    q_shard = jnp.pad(w_query.astype(BF16), ((0, 0), (0, wide - HEADS * HEAD)))
    o_shard = jnp.pad(w_out.astype(BF16), ((0, 0), (0, wide - width)))
    out_shard = w_out.shape[0]
    used = out_shard + shard
    qo_shard = jnp.pad(jnp.concatenate([o_shard, q_shard]), ((0, eights(used) - used), (0, 0)))
    pair, qo_shard, kv_along = lax.optimization_barrier((pair, qo_shard, kv_along))
    kv_own, pair, qo_shard = lax.optimization_barrier((links.across_plane(kv_along), pair, qo_shard))
    full_kv, gains, heads, seg_all = links.placed(
        kv_shard,
        kv_own,
        (
            (0, shard, 0, 2 * HEAD),
            (shard + rows, 0, shard, 4, True),
            (shard + rows, 4 * shard, head_shard, 2, True),
            (shard, rows, length),
        ),
    )
    h_in, k_proj, kv_low = kv_step(rows, length, tokens_flat, full_kv, gains, heads, cosine, sine)
    kv_low, qo_along, pair = lax.optimization_barrier((kv_low, links.along_z(qo_shard), links.exchange(pair)))
    pair = jnp.transpose(pair, (2, 0, 1, 3, 4)).reshape(2 * sx, sy * shard, units)
    kv, qo = links.window(
        kv_low,
        length,
        (
            lambda: (links.across_plane(qo_along),),
            lambda qo: (qo[0], links.swap(qo[0], "core") if links.pairs_only else qo[0]),
        ),
    )
    masks = (own_ids, seg_all)
    kv[2], pair = lax.optimization_barrier((kv[2], pair))
    full_pair = links.gather_cz(pair, 1).reshape(2, width, units)
    full_out, full_query = links.placed(
        qo_shard, qo[0], ((0, out_shard, 0, width), (out_shard, shard, 0, HEADS * HEAD)), qo[1]
    )

    q_proj, query, mixed, attn, resid, *h_ffn = attend(
        links, rows, length, h_in, tokens_flat, full_query, full_out, gains, heads, cosine, sine, masks, kv
    )
    parts_up = links.over_plane(h_ffn, lambda part: (part, *ffn_forward(part, full_pair, full_down)))
    h_parts, hidden, turn, act, ffn_terms = zip(*parts_up, strict=True)
    own, far, _ = links.sum_plane(ffn_terms)
    output, *d_ffn, sums_ffn = middle(rows, length, own, far, resid, cot_flat, gains)

    pending = list(zip(turn, act, strict=True))

    def back(part):
        return (part, *ffn_backward(part, *pending.pop(0), full_pair, full_down))

    d_parts, d_pairs, d_terms = zip(*links.over_plane(d_ffn, back), strict=True)
    block = sy * shard
    places = [
        [
            (c, ((z * 2 + k) * sx + x) * block, ((x * sc + c) * sz + z) * block, block)
            for x in range(sx)
            for c in range(sc)
            for z in range(sz)
        ]
        for k in range(2)
    ]
    half = units // 2
    down_places = [(c, 0, c * half, half) for c in range(sc)]

    def pair_down(kept, sent):
        sets = [([left], [one[None] for one in part]) for left, part in zip(hidden, d_parts, strict=True)]
        low = weight_grads(sets, [down_places])
        return (kept, links.swap(sent, "core"), *low)

    def pair_grads(*pairs):
        return weight_grads([(part, [pair]) for part, pair in zip(h_parts, pairs, strict=True)], places)

    own, far, (kept, got, *grad_down) = links.sum_plane(d_terms, d_pairs, (pair_grads, pair_down))
    own, far, half_pair = lax.optimization_barrier((own, far, (kept.astype(F32) + got.astype(F32)).astype(BF16)))
    grad_pair = links.sum_z_low(half_pair)

    def by_member(sums):
        return jnp.transpose(sums.reshape(2, sx, sy, shard, units), (1, 2, 0, 3, 4))

    def unpacked(got):
        got = got.reshape(sx, sy, 2, shard, sc, sz, chunk)[..., :hidden_shard]
        return jnp.transpose(got, (2, 3, 0, 4, 5, 1, 6)).reshape(2, shard, parts * hidden_shard).astype(F32)

    d_res, d_attn, d_qproj, sums_attn, heads_attn, *terms = attend_back(
        links, rows, length, own, far, cot_flat, resid, attn, q_proj, query, full_out, gains, heads, cosine, sine, masks, kv,
        links.window_kinds(length),
    )
    d_kv, beside = links.window_back(
        terms,
        length,
        (
            lambda: (
                links.sum_cores(*outer_grads(links.order("xyz"), (out_shard, shard), mixed, d_attn, h_in, d_qproj)),
                links.sum_cores(*grad_down),
            ),
            lambda second, low: (links.planes(second), low, grad_pair),
        ),
    )
    second, low, grad_pair = beside[1]
    grad_down = links.sum_z_low(low)[:hidden_shard].astype(F32)

    d_kvproj, grad_tokens, sums_in, heads_in = finish(
        rows, length, d_kv, k_proj, d_qproj, tokens_flat, d_res, full_query, full_kv, gains, heads, cosine, sine
    )
    gain_terms = (sums_ffn + sums_attn + sums_in)[:4]
    head_terms = (heads_attn + heads_in)[:2].reshape(2, parts, head_shard)
    head_terms = jnp.pad(head_terms, ((0, 0), (0, 0), (0, shard - head_shard))).reshape(2, width)
    small_terms = jnp.pad(jnp.concatenate([gain_terms, head_terms]), ((0, SMALL - 6), (0, 0)))
    d_kvproj, second, got_pair = lax.optimization_barrier(
        (d_kvproj, links.sum_halves(second, "y", 0), links.exchange(by_member(grad_pair)))
    )
    first_grad = first_grads(links.order("xyz"), shard, h_in, d_kvproj, small_terms)
    first_core = links.sum_cores(*first_grad)
    first_got, second_sum, grad_down = lax.optimization_barrier(
        (links.to_members(first_core), links.sum_z(second, 0), grad_down)
    )
    first_sum = links.sum_z(jnp.sum(first_got.astype(F32), axis=0).astype(BF16), 0)
    grad_pair = unpacked(got_pair)
    return (
        output.reshape(tokens.shape),
        grad_tokens.reshape(tokens.shape),
        second_sum[out_shard : out_shard + shard, : HEADS * HEAD],
        first_sum[:shard, SMALL : SMALL + HEAD],
        first_sum[:shard, SMALL + HEAD :],
        second_sum[:out_shard, :width],
        grad_pair[0],
        grad_pair[1],
        grad_down,
        *(first_sum[:shard, k] for k in range(4)),
        *(first_sum[:head_shard, 4 + k] for k in range(2)),
    )


def solution(mesh):
    plane = mesh.shape["dp"] // 2
    by_chip = Mesh(mesh.devices.reshape(plane, 2, -1, plane), AXES)
    links = Links(by_chip)
    placed = P(("x", "core"), ("z", "y"), None)
    matrix = P(AXES, None)
    vector = P(AXES)
    in_specs = (placed, P(("x", "core"), ("z", "y"))) + (matrix,) * 7 + (vector,) * 6 + (placed,)
    out_specs = (placed, placed) + (matrix,) * 7 + (vector,) * 6

    def step(*arguments):
        return on_device(links, *arguments)

    return jax.shard_map(step, mesh=by_chip, in_specs=in_specs, out_specs=out_specs, check_vma=False)
```

```python
import functools
import math

import jax
import jax.numpy as jnp
from jax import lax
from jax.experimental import pallas as pl
from jax.experimental.pallas import tpu as pltpu
from jax.sharding import Mesh
from jax.sharding import PartitionSpec as P

HEADS = 4
HEAD = 256
HALF = HEAD // 2
DOC_LIMIT = 512
EPSILON = 1e-06
ROPE_BASE = 1000000.0
NEG_FILL = -1e30
SCORE_SCALE = HEAD ** (-0.5)
SLOPE = math.sqrt(2.0 / math.pi)
F32 = jnp.float32
BF16 = jnp.bfloat16
PLANE = ("x", "y")
AXES = ("x", "core", "z", "y")
SWAP = [(0, 1), (1, 0)]
IN, POST_ATTN, PRE_FFN, POST_FFN = range(4)
SMALL = 128
ROOM = 58 << 20


def dot(left, right, dims):
    return lax.dot_general(left, right, (dims, ((), ())), preferred_element_type=F32)


def mm(left, right):
    return dot(left, right, ((1,), (0,)))


def mm_t(left, right):
    return dot(left, right, ((1,), (1,)))


def t_mm(left, right):
    return dot(left, right, ((0,), (0,)))


def inv_rms(values):
    return lax.rsqrt(jnp.mean(values * values, axis=-1, keepdims=True) + EPSILON)


def rms_back(values, gain_vec, d_norm):
    scale = inv_rms(values)
    unit = values * scale
    weighted = d_norm * gain_vec
    d_values = scale * (weighted - unit * jnp.mean(weighted * unit, axis=-1, keepdims=True))
    return d_values, d_norm * unit


def rope_tables(positions):
    inverse = ROPE_BASE ** (-(jnp.arange(HALF, dtype=F32) * 2.0 / HEAD))
    angles = positions.astype(F32)[..., None] * inverse
    return jnp.cos(angles), jnp.sin(angles)


def rotate(values, cosine, sine):
    first, second = values[:, :HALF], values[:, HALF:]
    return jnp.concatenate([first * cosine - second * sine, second * cosine + first * sine], axis=-1)


def eights(rows):
    return -(-rows // 8) * 8


def column_sum(terms):
    return jnp.sum(terms, axis=0, keepdims=True)


def call(body, grid, in_specs, out_specs, out_shape, flops, scratch=()):
    moved = sum(math.prod(one.shape) * one.dtype.itemsize for one in jax.tree.leaves(out_shape))
    return pl.pallas_call(
        body,
        grid=grid,
        in_specs=in_specs,
        out_specs=out_specs,
        out_shape=out_shape,
        scratch_shapes=list(scratch),
        compiler_params=pltpu.CompilerParams(vmem_limit_bytes=ROOM),
        cost_estimate=pl.CostEstimate(flops=flops, bytes_accessed=2 * moved, transcendentals=0),
    )


def shaped(*shape, dtype=F32):
    return jax.ShapeDtypeStruct(shape, dtype)


def whole(*shape):
    return pl.BlockSpec(shape, lambda i: (0,) * len(shape))


def rows_of(tile, width):
    return pl.BlockSpec((tile, width), lambda i: (i, 0))


def row_block(*shape):
    return pl.BlockSpec((1,) + shape, lambda i: (i,) + (0,) * len(shape))


def part_specs(tile, width, arrays):
    if len(arrays) == 1:
        return [rows_of(tile, width)]
    half = arrays[0].shape[0] // tile
    return [
        pl.BlockSpec((tile, width), lambda i: (jnp.minimum(i, half - 1), 0)),
        pl.BlockSpec((tile, width), lambda i: (jnp.maximum(i - half, 0), 0)),
    ]


def in_second():
    return pl.program_id(0) >= pl.num_programs(0) // 2


def load_part(refs):
    if len(refs) == 1:
        return refs[0][...]
    return lax.select_n(in_second(), refs[0][...], refs[1][...])


def store_part(refs, value):
    if len(refs) == 1:
        refs[0][...] = value
        return

    @pl.when(in_second() == False)
    def _():
        refs[0][...] = value

    @pl.when(in_second())
    def _():
        refs[1][...] = value


def kv_body(tok_ref, wkv_ref, gains_ref, head_ref, cos_ref, sin_ref, h_ref, kproj_ref, kv_ref):
    tokens = tok_ref[...].astype(F32)
    h = (tokens * inv_rms(tokens) * gains_ref[IN : IN + 1]).astype(BF16)
    h_ref[...] = h
    proj = mm(h, wkv_ref[...])
    k_proj = proj[:, :HEAD]
    kproj_ref[...] = k_proj
    key = rotate(k_proj * inv_rms(k_proj) * head_ref[1:2], cos_ref[...], sin_ref[...])
    kv_ref[0, :, :HEAD] = key.astype(BF16)
    kv_ref[0, :, HEAD:] = proj[:, HEAD:].astype(BF16)


def kv_step(rows, length, tokens, wkv, gains, heads, cosine, sine):
    count, width = tokens.shape
    return call(
        kv_body,
        (rows,),
        [rows_of(length, width), whole(*wkv.shape), whole(*gains.shape), whole(*heads.shape)]
        + [whole(length, HALF)] * 2,
        [rows_of(length, width), rows_of(length, HEAD), row_block(length, 2 * HEAD)],
        [shaped(count, width, dtype=BF16), shaped(count, HEAD), shaped(rows, length, 2 * HEAD, dtype=BF16)],
        2 * count * width * 2 * HEAD,
    )(tokens, wkv, gains, heads, cosine, sine)


def by_head(array):
    return jnp.concatenate([array[:, h * HEAD : (h + 1) * HEAD] for h in range(HEADS)], axis=0)


def by_lane(array):
    part = array.shape[0] // HEADS
    return jnp.concatenate([array[h * part : (h + 1) * part] for h in range(HEADS)], axis=1)


def probs_of(links, query, keys, own_ref, seg_ref):
    length = own_ref.shape[0]
    bases = links.window_bases(length)
    here = links.position(length)
    step = lax.broadcasted_iota(jnp.int32, (1, length), 1)
    segs, later = [], []
    for base in bases:
        row = seg_ref[0, pl.ds(jnp.maximum(base, 0) // length, 1), :]
        segs.append(jnp.where(base >= 0, row, -1.0))
        later.append(base - here + step)
    own_step = lax.broadcasted_iota(jnp.int32, (length, 1), 0)
    allowed = (own_ref[...] == jnp.concatenate(segs, axis=1)) & (jnp.concatenate(later, axis=1) <= own_step)
    allowed = jnp.concatenate([allowed.astype(F32)] * HEADS, axis=0) > 0.5
    scores = jnp.where(allowed, mm_t(query, keys) * SCORE_SCALE, NEG_FILL)
    powers = jnp.exp(scores - jnp.max(scores, axis=-1, keepdims=True))
    return powers / jnp.sum(powers, axis=-1, keepdims=True)


def attend_body(links, blocks, *refs):
    (h_ref, tok_ref, wq_ref, wo_ref, gains_ref, head_ref, cos_ref, sin_ref) = refs[:8]
    masks, kv_refs = refs[8:10], refs[10 : 10 + blocks]
    qproj_ref, query_ref, mixed_ref, attn_ref, resid_ref, *hffn_refs = refs[10 + blocks :]
    proj = mm(h_ref[...], wq_ref[...])
    qproj_ref[...] = proj
    cosine, sine = cos_ref[...], sin_ref[...]
    query = []
    for h in range(HEADS):
        one = proj[:, h * HEAD : (h + 1) * HEAD]
        query.append(rotate(one * inv_rms(one) * head_ref[0:1], cosine, sine).astype(BF16))
    query_ref[...] = jnp.concatenate(query, axis=1)
    keys = jnp.concatenate([one[0, :, :HEAD] for one in kv_refs], axis=0)
    values = jnp.concatenate([one[0, :, HEAD:] for one in kv_refs], axis=0)
    probs = probs_of(links, jnp.concatenate(query, axis=0), keys, *masks).astype(BF16)
    mixed = by_lane(mm(probs, values).astype(BF16))
    mixed_ref[...] = mixed
    attn = mm(mixed, wo_ref[...])
    attn_ref[...] = attn
    resid = tok_ref[...].astype(F32) + attn * inv_rms(attn) * gains_ref[POST_ATTN : POST_ATTN + 1]
    resid_ref[...] = resid
    store_part(hffn_refs, (resid * inv_rms(resid) * gains_ref[PRE_FFN : PRE_FFN + 1]).astype(BF16))


def mask_specs(masks):
    own, segs = masks
    return [rows_of(own.shape[0] // segs.shape[0], 1), row_block(*segs.shape[1:])]


def attend(links, rows, length, h, tokens, wq, wo, gains, heads, cosine, sine, masks, kv):
    count, width = tokens.shape
    wide = HEADS * HEAD
    window = len(kv) * length
    halves = [shaped(count // 2, width, dtype=BF16)] * 2
    return call(
        functools.partial(attend_body, links, len(kv)),
        (rows,),
        [rows_of(length, width)] * 2
        + [whole(*one.shape) for one in (wq, wo, gains, heads)]
        + [whole(length, HALF)] * 2
        + mask_specs(masks)
        + [row_block(length, 2 * HEAD)] * len(kv),
        [rows_of(length, wide)] * 3 + [rows_of(length, width)] * 2 + part_specs(length, width, halves),
        [
            shaped(count, wide),
            shaped(count, wide, dtype=BF16),
            shaped(count, wide, dtype=BF16),
            shaped(count, width),
            shaped(count, width),
            *halves,
        ],
        4 * count * wide * (width + window),
    )(h, tokens, wq, wo, gains, heads, cosine, sine, *masks, *kv)


def attend_back_body(links, blocks, *refs):
    own_refs, far_refs, refs = refs[:2], refs[2:4], refs[4:]
    (cot_ref, resid_ref, attn_ref, qproj_ref, query_ref, wo_ref, gains_ref, head_ref, cos_ref, sin_ref) = refs[:10]
    masks, kv_refs = refs[10:12], refs[12 : 12 + blocks]
    dres_ref, dattn_ref, dq_ref, sums_ref, head_sums_ref = refs[12 + blocks : 17 + blocks]
    term_refs = refs[17 + blocks :]
    d_norm, pre_terms = rms_back(resid_ref[...], gains_ref[PRE_FFN : PRE_FFN + 1], load_part(own_refs) + load_part(far_refs).astype(F32))
    d_res = cot_ref[...].astype(F32) + d_norm
    dres_ref[...] = d_res
    d_attn, post_terms = rms_back(attn_ref[...], gains_ref[POST_ATTN : POST_ATTN + 1], d_res)
    d_attn = d_attn.astype(BF16)
    dattn_ref[...] = d_attn
    d_mixed = by_head(mm_t(d_attn, wo_ref[...]).astype(BF16))
    query = by_head(query_ref[...])
    keys = jnp.concatenate([one[0, :, :HEAD] for one in kv_refs], axis=0)
    values = jnp.concatenate([one[0, :, HEAD:] for one in kv_refs], axis=0)
    probs = probs_of(links, query, keys, *masks)
    d_probs = mm_t(d_mixed, values)
    d_scores = (probs * (d_probs - jnp.sum(d_probs * probs, axis=-1, keepdims=True))).astype(BF16)
    key_terms = t_mm(d_scores, query) * SCORE_SCALE
    value_terms = t_mm(probs.astype(BF16), d_mixed)
    length = query_ref.shape[0]
    for k, ref in enumerate(term_refs):
        at = slice(k * length, (k + 1) * length)
        ref[0, :, :HEAD] = key_terms[at].astype(ref.dtype)
        ref[0, :, HEAD:] = value_terms[at].astype(ref.dtype)
    d_query = mm(d_scores, keys) * SCORE_SCALE
    cosine, sine = cos_ref[...], -sin_ref[...]
    head_sum = jnp.zeros((1, HEAD), F32)
    for h in range(HEADS):
        turned = rotate(d_query[h * length : (h + 1) * length], cosine, sine)
        lanes = slice(h * HEAD, (h + 1) * HEAD)
        d_proj, terms = rms_back(qproj_ref[:, lanes], head_ref[0:1], turned)
        dq_ref[:, lanes] = d_proj.astype(BF16)
        head_sum += column_sum(terms)

    @pl.when(pl.program_id(0) == 0)
    def _():
        sums_ref[...] = jnp.zeros_like(sums_ref)
        head_sums_ref[...] = jnp.zeros_like(head_sums_ref)

    sums_ref[POST_ATTN : POST_ATTN + 1] += column_sum(post_terms)
    sums_ref[PRE_FFN : PRE_FFN + 1] += column_sum(pre_terms)
    head_sums_ref[0:1] += head_sum


def attend_back(links, rows, length, own, far, cot, resid, attn, qproj, query, wo, gains, heads, cosine, sine, masks, kv, kinds):
    count, width = cot.shape
    wide = HEADS * HEAD
    window = len(kv) * length
    return call(
        functools.partial(attend_back_body, links, len(kv)),
        (rows,),
        part_specs(length, width, own) * 2
        + [rows_of(length, width)] * 3
        + [rows_of(length, wide)] * 2
        + [whole(*one.shape) for one in (wo, gains, heads)]
        + [whole(length, HALF)] * 2
        + mask_specs(masks)
        + [row_block(length, 2 * HEAD)] * len(kv),
        [rows_of(length, width)] * 2
        + [rows_of(length, wide), whole(8, width), whole(8, HEAD)]
        + [row_block(length, 2 * HEAD)] * len(kv),
        [
            shaped(count, width),
            shaped(count, width, dtype=BF16),
            shaped(count, wide, dtype=BF16),
            shaped(8, width),
            shaped(8, HEAD),
        ]
        + [shaped(rows, length, 2 * HEAD, dtype=kind) for kind in kinds],
        2 * count * wide * (width + 5 * window),
    )(*own, *far, cot, resid, attn, qproj, query, wo, gains, heads, cosine, sine, *masks, *kv)


def finish_body(many, *refs):
    finish_rows(refs[:many], *refs[many:])


def finish_rows(dkv_refs, kproj_ref, dq_ref, tok_ref, dres_ref, wq_ref, wkv_ref, gains_ref, head_ref, cos_ref, sin_ref,
                dkvp_ref, grad_ref, sums_ref, head_sums_ref):
    d_kv = sum(ref[0].astype(F32) for ref in dkv_refs)
    turned = rotate(d_kv[:, :HEAD], cos_ref[...], -sin_ref[...])
    d_key, key_terms = rms_back(kproj_ref[...], head_ref[1:2], turned)
    d_proj = jnp.concatenate([d_key.astype(BF16), d_kv[:, HEAD:].astype(BF16)], axis=1)
    dkvp_ref[...] = d_proj
    d_hin = mm_t(dq_ref[...], wq_ref[...]) + mm_t(d_proj, wkv_ref[...])
    d_tokens, in_terms = rms_back(tok_ref[...].astype(F32), gains_ref[IN : IN + 1], d_hin)
    grad_ref[...] = (dres_ref[...] + d_tokens).astype(BF16)

    @pl.when(pl.program_id(0) == 0)
    def _():
        sums_ref[...] = jnp.zeros_like(sums_ref)
        head_sums_ref[...] = jnp.zeros_like(head_sums_ref)

    sums_ref[IN : IN + 1] += column_sum(in_terms)
    head_sums_ref[1:2] += column_sum(key_terms)


def finish(rows, length, dkv, kproj, dq, tokens, dres, wq, wkv, gains, heads, cosine, sine):
    count, width = tokens.shape
    wide = HEADS * HEAD
    return call(
        functools.partial(finish_body, len(dkv)),
        (rows,),
        [row_block(length, 2 * HEAD)] * len(dkv)
        + [rows_of(length, HEAD), rows_of(length, wide)]
        + [rows_of(length, width)] * 2
        + [whole(*one.shape) for one in (wq, wkv, gains, heads)]
        + [whole(length, HALF)] * 2,
        [rows_of(length, 2 * HEAD), rows_of(length, width), whole(8, width), whole(8, HEAD)],
        [shaped(count, 2 * HEAD, dtype=BF16), shaped(count, width, dtype=BF16), shaped(8, width), shaped(8, HEAD)],
        2 * count * width * (wide + 2 * HEAD),
    )(*dkv, kproj, dq, tokens, dres, wq, wkv, gains, heads, cosine, sine)


def pieces_of(total, step):
    return [(k, min(step, total - k)) for k in range(0, total, step)]


def up_body(step, many, *refs):
    pair_ref, down_ref, hidden_ref, turn_ref, act_ref = refs[many : many + 5]
    h = load_part(refs[:many])
    for at, wide in pieces_of(hidden_ref.shape[1], step):
        cols = pl.ds(at, wide)
        gate = mm(h, pair_ref[0, :, cols])
        up = mm(h, pair_ref[1, :, cols])
        square = gate * gate
        bent = jnp.tanh(gate * (SLOPE + SLOPE * 0.044715 * square))
        half = 0.5 + 0.5 * bent
        act = gate * half
        d_act = half + 0.5 * gate * (1.0 - bent * bent) * (SLOPE + 3 * SLOPE * 0.044715 * square)
        hidden_ref[:, cols] = (act * up).astype(BF16)
        turn_ref[:, cols] = (up * d_act).astype(BF16)
        act_ref[:, cols] = act.astype(BF16)
    store_part(refs[many + 5 :], mm(hidden_ref[...], down_ref[...]).astype(BF16))


def ffn_forward(h, pair, down, tile=256, step=256):
    count, width = sum(one.shape[0] for one in h), h[0].shape[1]
    units = pair.shape[2]
    specs = part_specs(tile, width, h)
    hidden, turn, act, *terms = call(
        functools.partial(up_body, step, len(h)),
        (count // tile,),
        specs + [whole(2, width, units), whole(units, width)],
        [rows_of(tile, units)] * 3 + specs,
        [shaped(count, units, dtype=BF16)] * 3 + [shaped(*one.shape, dtype=BF16) for one in h],
        6 * count * width * units,
    )(*h, pair, down)
    return hidden, turn, act, terms


def down_body(step, many, *refs):
    turn_ref, act_ref, pair_ref, down_ref, pair_out = refs[many : many + 5]
    d = load_part(refs[:many])
    for at, wide in pieces_of(turn_ref.shape[1], step):
        cols = pl.ds(at, wide)
        d_hidden = mm_t(d, down_ref[cols, :])
        pair_out[0, :, cols] = (d_hidden * turn_ref[:, cols].astype(F32)).astype(BF16)
        pair_out[1, :, cols] = (d_hidden * act_ref[:, cols].astype(F32)).astype(BF16)
    store_part(refs[many + 5 :], (mm_t(pair_out[0], pair_ref[0]) + mm_t(pair_out[1], pair_ref[1])).astype(BF16))


def ffn_backward(d, turn, act, pair, down, tile=256, step=512):
    count, width = sum(one.shape[0] for one in d), d[0].shape[1]
    units = pair.shape[2]
    specs = part_specs(tile, width, d)
    d_pair, *terms = call(
        functools.partial(down_body, step, len(d)),
        (count // tile,),
        specs + [rows_of(tile, units), rows_of(tile, units), whole(2, width, units), whole(units, width)],
        [pl.BlockSpec((2, tile, units), lambda i: (0, i, 0))] + specs,
        [shaped(2, count, units, dtype=BF16)] + [shaped(*one.shape, dtype=BF16) for one in d],
        6 * count * width * units,
    )(*d, turn, act, pair, down)
    return d_pair, terms


def put(kept_ref, sent_ref, core, index, value):
    @pl.when(lax.axis_index("core") == core)
    def _():
        kept_ref[index] = value

    @pl.when(lax.axis_index("core") != core)
    def _():
        sent_ref[index] = value


def grads_body(places, sets, *refs):
    kept_ref, sent_ref = refs[-2:]
    total, at = None, 0
    for lefts, rights in sets:
        values = []
        for many in (lefts, rights):
            pieces = [ref[...] if len(ref.shape) == 2 else ref[0] for ref in refs[at : at + many]]
            values.append(jnp.concatenate(pieces, axis=0) if many > 1 else pieces[0])
            at += many
        term = t_mm(*values)
        total = term if total is None else total + term
    total = total.astype(BF16)
    tile = total.shape[0]
    for which, moves in enumerate(places):
        for k in range(sum(count for _, _, _, count in moves) // tile):

            @pl.when((pl.program_id(0) == which) & (pl.program_id(1) == k))
            def _(k=k, moves=moves):
                for core, at, row, count in moves:
                    begin, end = max(row, k * tile), min(row + count, (k + 1) * tile)
                    if begin < end:
                        to = at + begin - row
                        index = (slice(to, to + end - begin), slice(None))
                        put(kept_ref, sent_ref, core, index, total[begin - k * tile : end - k * tile])


def weight_grads(sets, places):
    rows, cols = sets[0][0][0].shape[1], sets[0][1][0].shape[2]
    count = sum(one.shape[0] for lefts, _ in sets for one in lefts)
    tile = 384 if rows % 384 == 0 else 256
    out = len(places) * rows // 2
    specs, arrays = [], []
    for lefts, rights in sets:
        specs += [pl.BlockSpec((one.shape[0], tile), lambda k, i: (0, i)) for one in lefts]
        specs += [pl.BlockSpec((1,) + one.shape[1:], lambda k, i: (k, 0, 0)) for one in rights]
        arrays += [*lefts, *rights]
    return call(
        functools.partial(grads_body, places, [(len(lefts), len(rights)) for lefts, rights in sets]),
        (len(places), rows // tile),
        specs,
        [pl.BlockSpec((out, cols), lambda k, i: (0, 0))] * 2,
        [shaped(out, cols, dtype=BF16)] * 2,
        2 * len(places) * count * rows * cols,
    )(*arrays)


def outer_body(order, shards, mixed_ref, dattn_ref, h_ref, dq_ref, kept_ref, sent_ref):
    lanes = kept_ref.shape[2]
    at = 0
    for rows, left, right in ((shards[0], mixed_ref, dattn_ref), (shards[1], h_ref, dq_ref)):
        total = t_mm(left[...], right[...]).astype(BF16)
        wide = total.shape[1]
        for core, place, number in order:
            index = (place, slice(at, at + rows), slice(0, wide))
            put(kept_ref, sent_ref, core, index, total[number * rows : (number + 1) * rows])
        for ref in (kept_ref, sent_ref):
            if wide < lanes:
                ref[:, at : at + rows, wide:] = jnp.zeros((ref.shape[0], rows, lanes - wide), BF16)
        at += rows
    for ref in (kept_ref, sent_ref):
        if at < ref.shape[1]:
            ref[:, at:, :] = jnp.zeros((ref.shape[0], ref.shape[1] - at, lanes), BF16)


def outer_grads(order, shards, mixed, d_attn, h, d_q):
    count = mixed.shape[0]
    shape = (len(order) // 2, eights(sum(shards)), max(d_attn.shape[1], d_q.shape[1]))
    return call(
        functools.partial(outer_body, order, shards),
        (1,),
        [whole(*one.shape) for one in (mixed, d_attn, h, d_q)],
        [whole(*shape)] * 2,
        [shaped(*shape, dtype=BF16)] * 2,
        2 * count * (mixed.shape[1] * d_attn.shape[1] + h.shape[1] * d_q.shape[1]),
    )(mixed, d_attn, h, d_q)


def first_body(order, shard, h_ref, dkv_ref, small_ref, kept_ref, sent_ref):
    small = small_ref[...].T.astype(BF16)
    total = t_mm(h_ref[...], dkv_ref[...]).astype(BF16)
    for core, place, number in order:
        rows = slice(number * shard, (number + 1) * shard)
        put(kept_ref, sent_ref, core, (place, slice(0, shard), slice(0, SMALL)), small[rows])
        put(kept_ref, sent_ref, core, (place, slice(0, shard), slice(SMALL, None)), total[rows])
    for ref in (kept_ref, sent_ref):
        if shard < ref.shape[1]:
            ref[:, shard:, :] = jnp.zeros((ref.shape[0], ref.shape[1] - shard, ref.shape[2]), BF16)


def first_grads(order, shard, h, d_kv, small):
    count, rows = h.shape
    shape = (len(order) // 2, eights(shard), d_kv.shape[1] + SMALL)
    return call(
        functools.partial(first_body, order, shard),
        (1,),
        [whole(*one.shape) for one in (h, d_kv, small)],
        [whole(*shape)] * 2,
        [shaped(*shape, dtype=BF16)] * 2,
        2 * count * rows * d_kv.shape[1],
    )(h, d_kv, small)


def middle_body(own_a, own_b, far_a, far_b, resid_ref, cot_ref, gains_ref, out_ref, dffn_a, dffn_b, sums_ref):
    ffn = load_part((own_a, own_b)) + load_part((far_a, far_b)).astype(F32)
    gain = gains_ref[POST_FFN : POST_FFN + 1]
    out_ref[...] = (resid_ref[...] + ffn * inv_rms(ffn) * gain).astype(BF16)
    d_ffn, terms = rms_back(ffn, gain, cot_ref[...].astype(F32))
    store_part((dffn_a, dffn_b), d_ffn.astype(BF16))

    @pl.when(pl.program_id(0) == 0)
    def _():
        sums_ref[...] = jnp.zeros_like(sums_ref)

    sums_ref[POST_FFN : POST_FFN + 1] += column_sum(terms)


def middle(rows, length, own, far, resid, cot, gains):
    count, width = resid.shape
    specs = part_specs(length, width, own)
    return call(
        middle_body,
        (rows,),
        specs * 2 + [rows_of(length, width)] * 2 + [whole(*gains.shape)],
        [rows_of(length, width)] + specs + [whole(8, width)],
        [shaped(count, width, dtype=BF16)] + [shaped(count // 2, width, dtype=BF16)] * 2 + [shaped(8, width)],
        20 * count * width,
    )(*own, *far, resid, cot, gains)


def place_body(links, shard, parts, own_ref, other_ref, *refs):
    outs, scratch = refs[:-1], refs[-1]
    depth = links.size["z"]
    at_x, at_c, at_z, at_y = (links.index(axis) for axis in AXES)
    number = 0
    for x in range(2):
        for core in range(2):
            for z in range(depth):
                for y in range(2):
                    slot = jnp.abs(at_x - x) + 2 * jnp.abs(at_y - y)
                    slot = slot * depth + jnp.remainder(at_z - z + depth, depth)
                    mine = own_ref[slot].astype(F32)
                    theirs = other_ref[slot].astype(F32)
                    piece = jnp.where(at_c == core, mine, theirs)
                    scratch[number] = piece
                    number += 1
    for part, out in zip(parts, outs, strict=True):
        for k in range(number):
            if len(part) == 4:
                first, count, at, lanes = part
                out[k * count : (k + 1) * count, :] = scratch[k, first : first + count, at : at + lanes].astype(out.dtype)
                continue
            if len(part) == 3:
                first, count, lanes = part
                if k < 2 * depth:
                    ids = scratch[(at_x * 2 + at_c) * 2 * depth + k]
                    for row in range(count):
                        out[row, k : k + 1, :] = ids[first + row : first + row + 1, :lanes]
                continue
            row, at, lanes, vectors = part[:4]
            for v in range(vectors):
                begin = at + v * lanes
                out[v : v + 1, k * lanes : (k + 1) * lanes] = scratch[k, row : row + 1, begin : begin + lanes]


def placed(links, own, other, parts):
    slots, rows, lanes = own.shape
    number = 2 * slots
    return pl.pallas_call(
        functools.partial(place_body, links, rows, parts),
        out_shape=[
            shaped(number * part[1], part[3], dtype=BF16)
            if len(part) == 4
            else shaped(part[1], slots // 2, part[2])
            if len(part) == 3
            else shaped(8, number * part[2])
            for part in parts
        ],
        scratch_shapes=[pltpu.VMEM((number, rows, lanes), F32)],
        compiler_params=pltpu.CompilerParams(vmem_limit_bytes=ROOM),
    )(own, other)


class Links:
    def __init__(self, mesh):
        self.size = dict(mesh.shape)
        self.pairs_only = self.size["x"] == 2 and self.size["y"] == 2

    def index(self, axis):
        return lax.axis_index(axis)

    def swap(self, array, axis):
        return lax.ppermute(array, axis, SWAP)

    def shift(self, array, step):
        depth = self.size["z"]
        pairs = [(i, i + step) for i in range(depth) if 0 <= i + step < depth]
        return lax.ppermute(array, "z", pairs)

    def turn(self, array, step):
        depth = self.size["z"]
        return lax.ppermute(array, "z", [(i, (i + step) % depth) for i in range(depth)])

    def ordered(self, own, other, axis):
        first = self.index(axis) == 0
        return jnp.where(first, jnp.stack([own, other]), jnp.stack([other, own]))

    def along_z(self, array):
        return jnp.stack([array] + [self.turn(array, k) for k in range(1, self.size["z"])])

    def across_plane(self, along):
        if not self.pairs_only:
            return along
        across = lax.ppermute(along, PLANE, [(k, 3 - k) for k in range(4)])
        return jnp.concatenate([along, self.swap(along, "x"), self.swap(along, "y"), across])

    def placed(self, array, own, parts, other=None):
        if self.pairs_only:
            other = self.swap(own, "core") if other is None else other
            return placed(self, own, other, parts)
        full = lax.all_gather(array, AXES, axis=0)
        cuts = []
        for part in parts:
            if len(part) == 4:
                r, n, c, w = part
                cuts.append(full[:, r : r + n, c : c + w].reshape(-1, w))
            elif len(part) == 3:
                r, n, w = part
                blocks = self.size["z"] * self.size["y"]
                at = (self.index("x") * 2 + self.index("core")) * blocks
                ids = lax.dynamic_slice_in_dim(full[:, r : r + n, :w], at, blocks)
                cuts.append(jnp.swapaxes(ids, 0, 1).astype(F32))
            else:
                r, c, w, n = part[:4]
                rows = jnp.swapaxes(full[:, r, c : c + n * w].reshape(-1, n, w), 0, 1).reshape(n, -1)
                cuts.append(jnp.pad(rows.astype(F32), ((0, 8 - n), (0, 0))))
        return cuts

    def order(self, axes):
        found = []
        counts = [self.size[axis] for axis in AXES]
        for number in range(math.prod(counts)):
            at, rest = {}, number
            for axis, many in zip(AXES[::-1], counts[::-1], strict=True):
                at[axis], rest = rest % many, rest // many
            place = 0
            for axis in axes:
                place = place * self.size[axis] + at[axis]
            found.append((at["core"], place, number))
        return found

    def gather_cz(self, array, dim):
        return lax.all_gather(array, ("core", "z"), axis=dim, tiled=True)

    def sum_halves(self, array, axis, dim):
        if self.size[axis] == 2:
            at = self.index(axis)
            sent = self.swap(lax.dynamic_index_in_dim(array, 1 - at, dim, False), axis)
            kept = lax.dynamic_index_in_dim(array, at, dim, False)
            return (kept.astype(F32) + sent.astype(F32)).astype(array.dtype)
        return lax.psum_scatter(array, axis, scatter_dimension=dim, tiled=False)

    def sum_cores(self, kept, sent):
        return (kept.astype(F32) + self.swap(sent, "core").astype(F32)).astype(kept.dtype)

    def sum_z(self, array, dim):
        depth = self.size["z"]
        z = self.index("z")

        def block(k):
            return lax.dynamic_index_in_dim(array, jnp.remainder(z + k, depth), dim, False)

        total = block(0).astype(F32)
        for k in range(1, depth):
            total = total + self.turn(block(k), k).astype(F32)
        return total

    def sum_z_low(self, array):
        return lax.psum_scatter(array, "z", scatter_dimension=0, tiled=True)

    def planes(self, array):
        sx, sy, sz = (self.size[axis] for axis in "xyz")
        return self.sum_halves(array.reshape((sx, sy, sz) + array.shape[1:]), "x", 0)

    def to_members(self, array):
        count = self.size["x"] * self.size["y"]
        got = lax.all_to_all(array.reshape((count, -1) + array.shape[2:]), PLANE, 0, 0, tiled=True)
        return got.reshape((count, self.size["z"]) + array.shape[1:])

    def exchange(self, array):
        count = self.size["x"] * self.size["y"]
        flat = array.reshape((count,) + array.shape[2:])
        return lax.all_to_all(flat, PLANE, 0, 0, tiled=True).reshape(array.shape)

    def over_plane(self, halves, first):
        if not self.pairs_only:
            return [first([lax.all_gather(jnp.concatenate(halves), PLANE, axis=0, tiled=True)])]
        upper, lower = halves
        size = 2 * upper.shape[0]
        near = lax.optimization_barrier((self.swap(upper, "x"), self.swap(lower, "y")))
        near = jnp.concatenate([upper, near[0], lower, near[1]])
        upper, lower, near = lax.optimization_barrier((near[:size], near[size:], near))
        upper, lower, done = lax.optimization_barrier((self.swap(upper, "y"), self.swap(lower, "x"), first([near])))
        return [done, first([upper, lower])]

    def sum_plane(self, parts, held=(), beside=(None, None)):
        works = [work or (lambda *given: ()) for work in beside]
        if not self.pairs_only:
            total = lax.psum_scatter(parts[0][0], PLANE, scatter_dimension=0, tiled=True).astype(F32)
            half = total.shape[0] // 2
            empty = [jnp.zeros((half, total.shape[1]), BF16)] * 2
            return [total[:half], total[half:]], empty, works[1](*works[0](*held))
        (near,), (upper, lower) = parts
        quarter = upper.shape[0] // 2
        upper, lower, held = lax.optimization_barrier((upper, lower, tuple(held)))
        upper, lower, extra = lax.optimization_barrier((self.swap(upper, "y"), self.swap(lower, "x"), works[0](*held)))
        at = [near[k * quarter : (k + 1) * quarter].astype(F32) for k in range(4)]
        own = [at[0] + upper[:quarter].astype(F32), at[2] + lower[:quarter].astype(F32)]
        upper = (at[1] + upper[quarter:].astype(F32)).astype(BF16)
        lower = (at[3] + lower[quarter:].astype(F32)).astype(BF16)
        upper, lower, extra = lax.optimization_barrier((upper, lower, extra))
        upper, lower, extra = lax.optimization_barrier((self.swap(upper, "x"), self.swap(lower, "y"), works[1](*extra)))
        return own, [upper, lower], extra

    def position(self, length):
        return (self.index("z") * self.size["y"] + self.index("y")) * length

    def window_bases(self, length):
        z, y, wide = self.index("z"), self.index("y"), self.size["y"]
        span = wide * length
        reach = -(-(DOC_LIMIT - 1) // span)
        base = self.position(length)
        if wide == 2 and reach == 2:
            cross = jnp.where(y == 0, z * span - length, z * span)
            return [base, base - span, base - 2 * span, cross, cross - span]
        return [(z - k) * span + j * length for k in range(reach + 1) for j in range(wide)]

    def window(self, array, length, beside):
        wide = self.size["y"]
        reach = -(-(DOC_LIMIT - 1) // (wide * length))
        if wide == 2 and reach == 2:
            first = self.index("y") == 0
            one, two, extra = lax.optimization_barrier((self.shift(array, 1), self.shift(array, 2), beside[0]()))
            near = self.swap(jnp.where(first, array, one), "y")
            far = self.swap(jnp.where(first, one, two), "y")
            near, far, extra = lax.optimization_barrier((near, far, beside[1](extra)))
            return [array, one, two, near, far], extra
        along = [lax.all_gather(array, "y", axis=0)]
        for _ in range(reach):
            along.append(self.shift(along[-1], 1))
        return [level[j] for level in along for j in range(wide)], beside[1](beside[0]())

    def window_kinds(self, length):
        if self.size["y"] == 2 and 2 * length * 2 >= DOC_LIMIT - 1 > 2 * length:
            return [F32, F32, F32, BF16, BF16]
        return [F32] * len(self.window_bases(length))

    def window_back(self, terms, length, beside=()):
        wide = self.size["y"]
        span = wide * length
        reach = -(-(DOC_LIMIT - 1) // span)
        results = []

        def follow(*arrays):
            if len(results) < len(beside):
                results.append(beside[len(results)](*(results[-1] if results else ())))
                *arrays, results[-1] = lax.optimization_barrier((*arrays, results[-1]))
            return arrays

        if wide == 2 and reach == 2:
            first = self.index("y") == 0
            own, one, two, near, far = terms
            far, near = follow(self.swap(far, "y"), self.swap(near, "y"))
            far, near = far.astype(F32), near.astype(F32)
            two = (two + jnp.where(first, 0.0, far)).astype(BF16)
            one = (one + jnp.where(first, far, near)).astype(BF16)
            own = own + jnp.where(first, near, 0.0)
            two, one, own = follow(self.shift(two, -2), self.shift(one, -1), own)
            return [own, one, two], results
        total = None
        for k in range(reach, -1, -1):
            level = jnp.stack(terms[k * wide : (k + 1) * wide])
            total = level if total is None else level + self.shift(total.astype(BF16), -1).astype(F32)
        total = lax.psum_scatter(total.astype(BF16), "y", scatter_dimension=0, tiled=False).astype(F32)
        for _ in beside:
            (total,) = follow(total)
        return [total], results


def on_device(
    links,
    tokens,
    segment_ids,
    w_query,
    w_key,
    w_value,
    w_out,
    w_gate,
    w_up,
    w_down,
    g_in,
    g_post_attn,
    g_pre_ffn,
    g_post_ffn,
    g_query,
    g_key,
    cotangent,
):
    rows, length, width = tokens.shape
    count = rows * length
    size = links.size
    sx, sc, sz, sy = (size[axis] for axis in AXES)
    parts = sx * sc * sz * sy
    shard = w_gate.shape[0]
    hidden_shard = w_down.shape[0]
    chunk = -(-hidden_shard // 16) * 16
    units = sc * sz * chunk
    head_shard = g_query.shape[0]
    tokens_flat = tokens.reshape(count, width)
    cot_flat = cotangent.reshape(count, width)

    step = jnp.arange(length, dtype=jnp.int32)
    pos_own = links.position(length) + step
    cosine, sine = rope_tables(pos_own)

    lanes = 2 * HEAD + SMALL
    vectors = jnp.concatenate([g_in, g_post_attn, g_pre_ffn, g_post_ffn, g_query, g_key])
    vectors = lax.optimization_barrier(jnp.pad(vectors, (0, 2 * HEAD - vectors.shape[0])))[None]
    seg_rows = jnp.pad(segment_ids.astype(F32), ((0, 0), (0, 2 * HEAD - length)))
    used = shard + rows + 1
    kv_shard = jnp.concatenate([jnp.concatenate([w_key, w_value], axis=1), seg_rows, vectors]).astype(BF16)
    kv_shard = jnp.pad(kv_shard, ((0, eights(used) - used), (0, 0)))
    own_ids = segment_ids.astype(F32).reshape(count, 1)
    kv_shard, own_ids, w_gate, w_up, w_query, w_out = lax.optimization_barrier(
        (kv_shard, own_ids, w_gate, w_up, w_query, w_out)
    )
    kv_along = links.along_z(kv_shard)
    full_down = links.gather_cz(jnp.pad(w_down.astype(BF16), ((0, chunk - hidden_shard), (0, 0))), 0)

    def columns(weight):
        split = weight.astype(BF16).reshape(shard, sx, sc, sz, sy, hidden_shard)
        split = jnp.pad(split, ((0, 0),) * 5 + ((0, chunk - hidden_shard),))
        return jnp.transpose(split, (1, 4, 0, 2, 3, 5)).reshape(sx, sy, shard, units)

    pair = jnp.stack([columns(w_gate), columns(w_up)], axis=2)
    wide = max(width, HEADS * HEAD)
    q_shard = jnp.pad(w_query.astype(BF16), ((0, 0), (0, wide - HEADS * HEAD)))
    o_shard = jnp.pad(w_out.astype(BF16), ((0, 0), (0, wide - width)))
    out_shard = w_out.shape[0]
    used = out_shard + shard
    qo_shard = jnp.pad(jnp.concatenate([o_shard, q_shard]), ((0, eights(used) - used), (0, 0)))
    pair, qo_shard, kv_along = lax.optimization_barrier((pair, qo_shard, kv_along))
    kv_own, pair, qo_shard = lax.optimization_barrier((links.across_plane(kv_along), pair, qo_shard))
    full_kv, gains, heads, seg_all = links.placed(
        kv_shard,
        kv_own,
        (
            (0, shard, 0, 2 * HEAD),
            (shard + rows, 0, shard, 4, True),
            (shard + rows, 4 * shard, head_shard, 2, True),
            (shard, rows, length),
        ),
    )
    h_in, k_proj, kv_low = kv_step(rows, length, tokens_flat, full_kv, gains, heads, cosine, sine)
    kv_low, qo_along, pair = lax.optimization_barrier((kv_low, links.along_z(qo_shard), links.exchange(pair)))
    pair = jnp.transpose(pair, (2, 0, 1, 3, 4)).reshape(2 * sx, sy * shard, units)
    kv, qo = links.window(
        kv_low,
        length,
        (
            lambda: (links.across_plane(qo_along),),
            lambda qo: (qo[0], links.swap(qo[0], "core") if links.pairs_only else qo[0]),
        ),
    )
    masks = (own_ids, seg_all)
    kv[2], pair = lax.optimization_barrier((kv[2], pair))
    full_pair = links.gather_cz(pair, 1).reshape(2, width, units)
    full_out, full_query = links.placed(
        qo_shard, qo[0], ((0, out_shard, 0, width), (out_shard, shard, 0, HEADS * HEAD)), qo[1]
    )

    q_proj, query, mixed, attn, resid, *h_ffn = attend(
        links, rows, length, h_in, tokens_flat, full_query, full_out, gains, heads, cosine, sine, masks, kv
    )
    parts_up = links.over_plane(h_ffn, lambda part: (part, *ffn_forward(part, full_pair, full_down)))
    h_parts, hidden, turn, act, ffn_terms = zip(*parts_up, strict=True)
    own, far, _ = links.sum_plane(ffn_terms)
    output, *d_ffn, sums_ffn = middle(rows, length, own, far, resid, cot_flat, gains)

    pending = list(zip(turn, act, strict=True))

    def back(part):
        return (part, *ffn_backward(part, *pending.pop(0), full_pair, full_down))

    d_parts, d_pairs, d_terms = zip(*links.over_plane(d_ffn, back), strict=True)
    block = sy * shard
    places = [
        [
            (c, ((z * 2 + k) * sx + x) * block, ((x * sc + c) * sz + z) * block, block)
            for x in range(sx)
            for c in range(sc)
            for z in range(sz)
        ]
        for k in range(2)
    ]
    half = units // 2
    down_places = [(c, 0, c * half, half) for c in range(sc)]

    def pair_down(kept, sent):
        sets = [([left], [one[None] for one in part]) for left, part in zip(hidden, d_parts, strict=True)]
        low = weight_grads(sets, [down_places])
        return (kept, links.swap(sent, "core"), *low)

    def pair_grads(*pairs):
        return weight_grads([(part, [pair]) for part, pair in zip(h_parts, pairs, strict=True)], places)

    own, far, (kept, got, *grad_down) = links.sum_plane(d_terms, d_pairs, (pair_grads, pair_down))
    own, far, half_pair = lax.optimization_barrier((own, far, (kept.astype(F32) + got.astype(F32)).astype(BF16)))
    grad_pair = links.sum_z_low(half_pair)

    def by_member(sums):
        return jnp.transpose(sums.reshape(2, sx, sy, shard, units), (1, 2, 0, 3, 4))

    def unpacked(got):
        got = got.reshape(sx, sy, 2, shard, sc, sz, chunk)[..., :hidden_shard]
        return jnp.transpose(got, (2, 3, 0, 4, 5, 1, 6)).reshape(2, shard, parts * hidden_shard).astype(F32)

    d_res, d_attn, d_qproj, sums_attn, heads_attn, *terms = attend_back(
        links, rows, length, own, far, cot_flat, resid, attn, q_proj, query, full_out, gains, heads, cosine, sine, masks, kv,
        links.window_kinds(length),
    )
    d_kv, beside = links.window_back(
        terms,
        length,
        (
            lambda: (
                links.sum_cores(*outer_grads(links.order("xyz"), (out_shard, shard), mixed, d_attn, h_in, d_qproj)),
                links.sum_cores(*grad_down),
            ),
            lambda second, low: (links.planes(second), low, grad_pair),
        ),
    )
    second, low, grad_pair = beside[1]
    grad_down = links.sum_z_low(low)[:hidden_shard].astype(F32)

    d_kvproj, grad_tokens, sums_in, heads_in = finish(
        rows, length, d_kv, k_proj, d_qproj, tokens_flat, d_res, full_query, full_kv, gains, heads, cosine, sine
    )
    gain_terms = (sums_ffn + sums_attn + sums_in)[:4]
    head_terms = (heads_attn + heads_in)[:2].reshape(2, parts, head_shard)
    head_terms = jnp.pad(head_terms, ((0, 0), (0, 0), (0, shard - head_shard))).reshape(2, width)
    small_terms = jnp.pad(jnp.concatenate([gain_terms, head_terms]), ((0, SMALL - 6), (0, 0)))
    first_grad = first_grads(links.order("xyz"), shard, h_in, d_kvproj, small_terms)
    first_grad, second, got_pair = lax.optimization_barrier(
        (first_grad, links.sum_halves(second, "y", 0), links.exchange(by_member(grad_pair)))
    )
    first_core = links.sum_cores(*first_grad)
    first_got, second_sum, grad_down = lax.optimization_barrier(
        (links.to_members(first_core), links.sum_z(second, 0), grad_down)
    )
    first_sum = links.sum_z(jnp.sum(first_got.astype(F32), axis=0).astype(BF16), 0)
    grad_pair = unpacked(got_pair)
    return (
        output.reshape(tokens.shape),
        grad_tokens.reshape(tokens.shape),
        second_sum[out_shard : out_shard + shard, : HEADS * HEAD],
        first_sum[:shard, SMALL : SMALL + HEAD],
        first_sum[:shard, SMALL + HEAD :],
        second_sum[:out_shard, :width],
        grad_pair[0],
        grad_pair[1],
        grad_down,
        *(first_sum[:shard, k] for k in range(4)),
        *(first_sum[:head_shard, 4 + k] for k in range(2)),
    )


def solution(mesh):
    plane = mesh.shape["dp"] // 2
    by_chip = Mesh(mesh.devices.reshape(plane, 2, -1, plane), AXES)
    links = Links(by_chip)
    placed = P(("x", "core"), ("z", "y"), None)
    matrix = P(AXES, None)
    vector = P(AXES)
    in_specs = (placed, P(("x", "core"), ("z", "y"))) + (matrix,) * 7 + (vector,) * 6 + (placed,)
    out_specs = (placed, placed) + (matrix,) * 7 + (vector,) * 6

    def step(*arguments):
        return on_device(links, *arguments)

    return jax.shard_map(step, mesh=by_chip, in_specs=in_specs, out_specs=out_specs, check_vma=False)
```

```python
import functools
import math

import jax
import jax.numpy as jnp
from jax import lax
from jax.experimental import pallas as pl
from jax.experimental.pallas import tpu as pltpu
from jax.sharding import Mesh
from jax.sharding import PartitionSpec as P

HEADS = 4
HEAD = 256
HALF = HEAD // 2
DOC_LIMIT = 512
EPSILON = 1e-06
ROPE_BASE = 1000000.0
NEG_FILL = -1e30
SCORE_SCALE = HEAD ** (-0.5)
SLOPE = math.sqrt(2.0 / math.pi)
F32 = jnp.float32
BF16 = jnp.bfloat16
PLANE = ("x", "y")
AXES = ("x", "core", "z", "y")
SWAP = [(0, 1), (1, 0)]
IN, POST_ATTN, PRE_FFN, POST_FFN = range(4)
SMALL = 128
ROOM = 58 << 20


def dot(left, right, dims):
    return lax.dot_general(left, right, (dims, ((), ())), preferred_element_type=F32)


def mm(left, right):
    return dot(left, right, ((1,), (0,)))


def mm_t(left, right):
    return dot(left, right, ((1,), (1,)))


def t_mm(left, right):
    return dot(left, right, ((0,), (0,)))


def inv_rms(values):
    return lax.rsqrt(jnp.mean(values * values, axis=-1, keepdims=True) + EPSILON)


def rms_back(values, gain_vec, d_norm):
    scale = inv_rms(values)
    unit = values * scale
    weighted = d_norm * gain_vec
    d_values = scale * (weighted - unit * jnp.mean(weighted * unit, axis=-1, keepdims=True))
    return d_values, d_norm * unit


def rope_tables(positions):
    inverse = ROPE_BASE ** (-(jnp.arange(HALF, dtype=F32) * 2.0 / HEAD))
    angles = positions.astype(F32)[..., None] * inverse
    return jnp.cos(angles), jnp.sin(angles)


def rotate(values, cosine, sine):
    first, second = values[:, :HALF], values[:, HALF:]
    return jnp.concatenate([first * cosine - second * sine, second * cosine + first * sine], axis=-1)


def eights(rows):
    return -(-rows // 8) * 8


def column_sum(terms):
    return jnp.sum(terms, axis=0, keepdims=True)


def call(body, grid, in_specs, out_specs, out_shape, flops, scratch=()):
    moved = sum(math.prod(one.shape) * one.dtype.itemsize for one in jax.tree.leaves(out_shape))
    return pl.pallas_call(
        body,
        grid=grid,
        in_specs=in_specs,
        out_specs=out_specs,
        out_shape=out_shape,
        scratch_shapes=list(scratch),
        compiler_params=pltpu.CompilerParams(vmem_limit_bytes=ROOM),
        cost_estimate=pl.CostEstimate(flops=flops, bytes_accessed=2 * moved, transcendentals=0),
    )


def shaped(*shape, dtype=F32):
    return jax.ShapeDtypeStruct(shape, dtype)


def whole(*shape):
    return pl.BlockSpec(shape, lambda i: (0,) * len(shape))


def rows_of(tile, width):
    return pl.BlockSpec((tile, width), lambda i: (i, 0))


def row_block(*shape):
    return pl.BlockSpec((1,) + shape, lambda i: (i,) + (0,) * len(shape))


def part_specs(tile, width, arrays):
    if len(arrays) == 1:
        return [rows_of(tile, width)]
    half = arrays[0].shape[0] // tile
    return [
        pl.BlockSpec((tile, width), lambda i: (jnp.minimum(i, half - 1), 0)),
        pl.BlockSpec((tile, width), lambda i: (jnp.maximum(i - half, 0), 0)),
    ]


def in_second():
    return pl.program_id(0) >= pl.num_programs(0) // 2


def load_part(refs):
    if len(refs) == 1:
        return refs[0][...]
    return lax.select_n(in_second(), refs[0][...], refs[1][...])


def store_part(refs, value):
    if len(refs) == 1:
        refs[0][...] = value
        return

    @pl.when(in_second() == False)
    def _():
        refs[0][...] = value

    @pl.when(in_second())
    def _():
        refs[1][...] = value


def kv_body(tok_ref, wkv_ref, gains_ref, head_ref, cos_ref, sin_ref, h_ref, kproj_ref, kv_ref):
    tokens = tok_ref[...].astype(F32)
    h = (tokens * inv_rms(tokens) * gains_ref[IN : IN + 1]).astype(BF16)
    h_ref[...] = h
    proj = mm(h, wkv_ref[...])
    k_proj = proj[:, :HEAD]
    kproj_ref[...] = k_proj
    key = rotate(k_proj * inv_rms(k_proj) * head_ref[1:2], cos_ref[...], sin_ref[...])
    kv_ref[0, :, :HEAD] = key.astype(BF16)
    kv_ref[0, :, HEAD:] = proj[:, HEAD:].astype(BF16)


def kv_step(rows, length, tokens, wkv, gains, heads, cosine, sine):
    count, width = tokens.shape
    return call(
        kv_body,
        (rows,),
        [rows_of(length, width), whole(*wkv.shape), whole(*gains.shape), whole(*heads.shape)]
        + [whole(length, HALF)] * 2,
        [rows_of(length, width), rows_of(length, HEAD), row_block(length, 2 * HEAD)],
        [shaped(count, width, dtype=BF16), shaped(count, HEAD), shaped(rows, length, 2 * HEAD, dtype=BF16)],
        2 * count * width * 2 * HEAD,
    )(tokens, wkv, gains, heads, cosine, sine)


def by_head(array):
    return jnp.concatenate([array[:, h * HEAD : (h + 1) * HEAD] for h in range(HEADS)], axis=0)


def by_lane(array):
    part = array.shape[0] // HEADS
    return jnp.concatenate([array[h * part : (h + 1) * part] for h in range(HEADS)], axis=1)


def probs_of(links, query, keys, own_ref, seg_ref):
    length = own_ref.shape[0]
    bases = links.window_bases(length)
    here = links.position(length)
    step = lax.broadcasted_iota(jnp.int32, (1, length), 1)
    segs, later = [], []
    for base in bases:
        row = seg_ref[0, pl.ds(jnp.maximum(base, 0) // length, 1), :]
        segs.append(jnp.where(base >= 0, row, -1.0))
        later.append(base - here + step)
    own_step = lax.broadcasted_iota(jnp.int32, (length, 1), 0)
    allowed = (own_ref[...] == jnp.concatenate(segs, axis=1)) & (jnp.concatenate(later, axis=1) <= own_step)
    allowed = jnp.concatenate([allowed.astype(F32)] * HEADS, axis=0) > 0.5
    scores = jnp.where(allowed, mm_t(query, keys) * SCORE_SCALE, NEG_FILL)
    powers = jnp.exp(scores - jnp.max(scores, axis=-1, keepdims=True))
    return powers * (1.0 / jnp.sum(powers, axis=-1, keepdims=True))


def attend_body(links, blocks, *refs):
    (h_ref, tok_ref, wq_ref, wo_ref, gains_ref, head_ref, cos_ref, sin_ref) = refs[:8]
    masks, kv_refs = refs[8:10], refs[10 : 10 + blocks]
    qproj_ref, query_ref, mixed_ref, attn_ref, resid_ref, *hffn_refs = refs[10 + blocks :]
    proj = mm(h_ref[...], wq_ref[...])
    qproj_ref[...] = proj
    cosine, sine = cos_ref[...], sin_ref[...]
    query = []
    for h in range(HEADS):
        one = proj[:, h * HEAD : (h + 1) * HEAD]
        query.append(rotate(one * inv_rms(one) * head_ref[0:1], cosine, sine).astype(BF16))
    query_ref[...] = jnp.concatenate(query, axis=1)
    keys = jnp.concatenate([one[0, :, :HEAD] for one in kv_refs], axis=0)
    values = jnp.concatenate([one[0, :, HEAD:] for one in kv_refs], axis=0)
    probs = probs_of(links, jnp.concatenate(query, axis=0), keys, *masks).astype(BF16)
    mixed = by_lane(mm(probs, values).astype(BF16))
    mixed_ref[...] = mixed
    attn = mm(mixed, wo_ref[...])
    attn_ref[...] = attn
    resid = tok_ref[...].astype(F32) + attn * inv_rms(attn) * gains_ref[POST_ATTN : POST_ATTN + 1]
    resid_ref[...] = resid
    store_part(hffn_refs, (resid * inv_rms(resid) * gains_ref[PRE_FFN : PRE_FFN + 1]).astype(BF16))


def mask_specs(masks):
    own, segs = masks
    return [rows_of(own.shape[0] // segs.shape[0], 1), row_block(*segs.shape[1:])]


def attend(links, rows, length, h, tokens, wq, wo, gains, heads, cosine, sine, masks, kv):
    count, width = tokens.shape
    wide = HEADS * HEAD
    window = len(kv) * length
    halves = [shaped(count // 2, width, dtype=BF16)] * 2
    return call(
        functools.partial(attend_body, links, len(kv)),
        (rows,),
        [rows_of(length, width)] * 2
        + [whole(*one.shape) for one in (wq, wo, gains, heads)]
        + [whole(length, HALF)] * 2
        + mask_specs(masks)
        + [row_block(length, 2 * HEAD)] * len(kv),
        [rows_of(length, wide)] * 3 + [rows_of(length, width)] * 2 + part_specs(length, width, halves),
        [
            shaped(count, wide),
            shaped(count, wide, dtype=BF16),
            shaped(count, wide, dtype=BF16),
            shaped(count, width),
            shaped(count, width),
            *halves,
        ],
        4 * count * wide * (width + window),
    )(h, tokens, wq, wo, gains, heads, cosine, sine, *masks, *kv)


def attend_back_body(links, blocks, *refs):
    own_refs, far_refs, refs = refs[:2], refs[2:4], refs[4:]
    (cot_ref, resid_ref, attn_ref, qproj_ref, query_ref, wo_ref, gains_ref, head_ref, cos_ref, sin_ref) = refs[:10]
    masks, kv_refs = refs[10:12], refs[12 : 12 + blocks]
    dres_ref, dattn_ref, dq_ref, sums_ref, head_sums_ref = refs[12 + blocks : 17 + blocks]
    term_refs = refs[17 + blocks :]
    d_norm, pre_terms = rms_back(resid_ref[...], gains_ref[PRE_FFN : PRE_FFN + 1], load_part(own_refs) + load_part(far_refs).astype(F32))
    d_res = cot_ref[...].astype(F32) + d_norm
    dres_ref[...] = d_res
    d_attn, post_terms = rms_back(attn_ref[...], gains_ref[POST_ATTN : POST_ATTN + 1], d_res)
    d_attn = d_attn.astype(BF16)
    dattn_ref[...] = d_attn
    d_mixed = by_head(mm_t(d_attn, wo_ref[...]).astype(BF16))
    query = by_head(query_ref[...])
    keys = jnp.concatenate([one[0, :, :HEAD] for one in kv_refs], axis=0)
    values = jnp.concatenate([one[0, :, HEAD:] for one in kv_refs], axis=0)
    probs = probs_of(links, query, keys, *masks)
    d_probs = mm_t(d_mixed, values)
    d_scores = (probs * (d_probs - jnp.sum(d_probs * probs, axis=-1, keepdims=True))).astype(BF16)
    key_terms = t_mm(d_scores, query) * SCORE_SCALE
    value_terms = t_mm(probs.astype(BF16), d_mixed)
    length = query_ref.shape[0]
    for k, ref in enumerate(term_refs):
        at = slice(k * length, (k + 1) * length)
        ref[0, :, :HEAD] = key_terms[at].astype(ref.dtype)
        ref[0, :, HEAD:] = value_terms[at].astype(ref.dtype)
    d_query = mm(d_scores, keys) * SCORE_SCALE
    cosine, sine = cos_ref[...], -sin_ref[...]
    head_sum = jnp.zeros((1, HEAD), F32)
    for h in range(HEADS):
        turned = rotate(d_query[h * length : (h + 1) * length], cosine, sine)
        lanes = slice(h * HEAD, (h + 1) * HEAD)
        d_proj, terms = rms_back(qproj_ref[:, lanes], head_ref[0:1], turned)
        dq_ref[:, lanes] = d_proj.astype(BF16)
        head_sum += column_sum(terms)

    @pl.when(pl.program_id(0) == 0)
    def _():
        sums_ref[...] = jnp.zeros_like(sums_ref)
        head_sums_ref[...] = jnp.zeros_like(head_sums_ref)

    sums_ref[POST_ATTN : POST_ATTN + 1] += column_sum(post_terms)
    sums_ref[PRE_FFN : PRE_FFN + 1] += column_sum(pre_terms)
    head_sums_ref[0:1] += head_sum


def attend_back(links, rows, length, own, far, cot, resid, attn, qproj, query, wo, gains, heads, cosine, sine, masks, kv, kinds):
    count, width = cot.shape
    wide = HEADS * HEAD
    window = len(kv) * length
    return call(
        functools.partial(attend_back_body, links, len(kv)),
        (rows,),
        part_specs(length, width, own) * 2
        + [rows_of(length, width)] * 3
        + [rows_of(length, wide)] * 2
        + [whole(*one.shape) for one in (wo, gains, heads)]
        + [whole(length, HALF)] * 2
        + mask_specs(masks)
        + [row_block(length, 2 * HEAD)] * len(kv),
        [rows_of(length, width)] * 2
        + [rows_of(length, wide), whole(8, width), whole(8, HEAD)]
        + [row_block(length, 2 * HEAD)] * len(kv),
        [
            shaped(count, width),
            shaped(count, width, dtype=BF16),
            shaped(count, wide, dtype=BF16),
            shaped(8, width),
            shaped(8, HEAD),
        ]
        + [shaped(rows, length, 2 * HEAD, dtype=kind) for kind in kinds],
        2 * count * wide * (width + 5 * window),
    )(*own, *far, cot, resid, attn, qproj, query, wo, gains, heads, cosine, sine, *masks, *kv)


def finish_body(many, *refs):
    finish_rows(refs[:many], *refs[many:])


def finish_rows(dkv_refs, kproj_ref, dq_ref, tok_ref, dres_ref, wq_ref, wkv_ref, gains_ref, head_ref, cos_ref, sin_ref,
                dkvp_ref, grad_ref, sums_ref, head_sums_ref):
    d_kv = sum(ref[0].astype(F32) for ref in dkv_refs)
    turned = rotate(d_kv[:, :HEAD], cos_ref[...], -sin_ref[...])
    d_key, key_terms = rms_back(kproj_ref[...], head_ref[1:2], turned)
    d_proj = jnp.concatenate([d_key.astype(BF16), d_kv[:, HEAD:].astype(BF16)], axis=1)
    dkvp_ref[...] = d_proj
    d_hin = mm_t(dq_ref[...], wq_ref[...]) + mm_t(d_proj, wkv_ref[...])
    d_tokens, in_terms = rms_back(tok_ref[...].astype(F32), gains_ref[IN : IN + 1], d_hin)
    grad_ref[...] = (dres_ref[...] + d_tokens).astype(BF16)

    @pl.when(pl.program_id(0) == 0)
    def _():
        sums_ref[...] = jnp.zeros_like(sums_ref)
        head_sums_ref[...] = jnp.zeros_like(head_sums_ref)

    sums_ref[IN : IN + 1] += column_sum(in_terms)
    head_sums_ref[1:2] += column_sum(key_terms)


def finish(rows, length, dkv, kproj, dq, tokens, dres, wq, wkv, gains, heads, cosine, sine):
    count, width = tokens.shape
    wide = HEADS * HEAD
    return call(
        functools.partial(finish_body, len(dkv)),
        (rows,),
        [row_block(length, 2 * HEAD)] * len(dkv)
        + [rows_of(length, HEAD), rows_of(length, wide)]
        + [rows_of(length, width)] * 2
        + [whole(*one.shape) for one in (wq, wkv, gains, heads)]
        + [whole(length, HALF)] * 2,
        [rows_of(length, 2 * HEAD), rows_of(length, width), whole(8, width), whole(8, HEAD)],
        [shaped(count, 2 * HEAD, dtype=BF16), shaped(count, width, dtype=BF16), shaped(8, width), shaped(8, HEAD)],
        2 * count * width * (wide + 2 * HEAD),
    )(*dkv, kproj, dq, tokens, dres, wq, wkv, gains, heads, cosine, sine)


def pieces_of(total, step):
    return [(k, min(step, total - k)) for k in range(0, total, step)]


def up_body(step, many, *refs):
    pair_ref, down_ref, hidden_ref, turn_ref, act_ref = refs[many : many + 5]
    h = load_part(refs[:many])
    for at, wide in pieces_of(hidden_ref.shape[1], step):
        cols = pl.ds(at, wide)
        gate = mm(h, pair_ref[0, :, cols])
        up = mm(h, pair_ref[1, :, cols])
        square = gate * gate
        bent = jnp.tanh(gate * (SLOPE + SLOPE * 0.044715 * square))
        half = 0.5 + 0.5 * bent
        act = gate * half
        d_act = half + 0.5 * gate * (1.0 - bent * bent) * (SLOPE + 3 * SLOPE * 0.044715 * square)
        hidden_ref[:, cols] = (act * up).astype(BF16)
        turn_ref[:, cols] = (up * d_act).astype(BF16)
        act_ref[:, cols] = act.astype(BF16)
    store_part(refs[many + 5 :], mm(hidden_ref[...], down_ref[...]).astype(BF16))


def ffn_forward(h, pair, down, tile=256, step=256):
    count, width = sum(one.shape[0] for one in h), h[0].shape[1]
    units = pair.shape[2]
    specs = part_specs(tile, width, h)
    hidden, turn, act, *terms = call(
        functools.partial(up_body, step, len(h)),
        (count // tile,),
        specs + [whole(2, width, units), whole(units, width)],
        [rows_of(tile, units)] * 3 + specs,
        [shaped(count, units, dtype=BF16)] * 3 + [shaped(*one.shape, dtype=BF16) for one in h],
        6 * count * width * units,
    )(*h, pair, down)
    return hidden, turn, act, terms


def down_body(step, many, *refs):
    turn_ref, act_ref, pair_ref, down_ref, pair_out = refs[many : many + 5]
    d = load_part(refs[:many])
    for at, wide in pieces_of(turn_ref.shape[1], step):
        cols = pl.ds(at, wide)
        d_hidden = mm_t(d, down_ref[cols, :])
        pair_out[0, :, cols] = (d_hidden * turn_ref[:, cols].astype(F32)).astype(BF16)
        pair_out[1, :, cols] = (d_hidden * act_ref[:, cols].astype(F32)).astype(BF16)
    store_part(refs[many + 5 :], (mm_t(pair_out[0], pair_ref[0]) + mm_t(pair_out[1], pair_ref[1])).astype(BF16))


def ffn_backward(d, turn, act, pair, down, tile=256, step=512):
    count, width = sum(one.shape[0] for one in d), d[0].shape[1]
    units = pair.shape[2]
    specs = part_specs(tile, width, d)
    d_pair, *terms = call(
        functools.partial(down_body, step, len(d)),
        (count // tile,),
        specs + [rows_of(tile, units), rows_of(tile, units), whole(2, width, units), whole(units, width)],
        [pl.BlockSpec((2, tile, units), lambda i: (0, i, 0))] + specs,
        [shaped(2, count, units, dtype=BF16)] + [shaped(*one.shape, dtype=BF16) for one in d],
        6 * count * width * units,
    )(*d, turn, act, pair, down)
    return d_pair, terms


def put(kept_ref, sent_ref, core, index, value):
    @pl.when(lax.axis_index("core") == core)
    def _():
        kept_ref[index] = value

    @pl.when(lax.axis_index("core") != core)
    def _():
        sent_ref[index] = value


def grads_body(places, sets, *refs):
    kept_ref, sent_ref = refs[-2:]
    total, at = None, 0
    for lefts, rights in sets:
        values = []
        for many in (lefts, rights):
            pieces = [ref[...] if len(ref.shape) == 2 else ref[0] for ref in refs[at : at + many]]
            values.append(jnp.concatenate(pieces, axis=0) if many > 1 else pieces[0])
            at += many
        term = t_mm(*values)
        total = term if total is None else total + term
    total = total.astype(BF16)
    tile = total.shape[0]
    for which, moves in enumerate(places):
        for k in range(sum(count for _, _, _, count in moves) // tile):

            @pl.when((pl.program_id(0) == which) & (pl.program_id(1) == k))
            def _(k=k, moves=moves):
                for core, at, row, count in moves:
                    begin, end = max(row, k * tile), min(row + count, (k + 1) * tile)
                    if begin < end:
                        to = at + begin - row
                        index = (slice(to, to + end - begin), slice(None))
                        put(kept_ref, sent_ref, core, index, total[begin - k * tile : end - k * tile])


def weight_grads(sets, places):
    rows, cols = sets[0][0][0].shape[1], sets[0][1][0].shape[2]
    count = sum(one.shape[0] for lefts, _ in sets for one in lefts)
    tile = 384 if rows % 384 == 0 else 256
    out = len(places) * rows // 2
    specs, arrays = [], []
    for lefts, rights in sets:
        specs += [pl.BlockSpec((one.shape[0], tile), lambda k, i: (0, i)) for one in lefts]
        specs += [pl.BlockSpec((1,) + one.shape[1:], lambda k, i: (k, 0, 0)) for one in rights]
        arrays += [*lefts, *rights]
    return call(
        functools.partial(grads_body, places, [(len(lefts), len(rights)) for lefts, rights in sets]),
        (len(places), rows // tile),
        specs,
        [pl.BlockSpec((out, cols), lambda k, i: (0, 0))] * 2,
        [shaped(out, cols, dtype=BF16)] * 2,
        2 * len(places) * count * rows * cols,
    )(*arrays)


def outer_body(order, shards, mixed_ref, dattn_ref, h_ref, dq_ref, kept_ref, sent_ref):
    lanes = kept_ref.shape[2]
    at = 0
    for rows, left, right in ((shards[0], mixed_ref, dattn_ref), (shards[1], h_ref, dq_ref)):
        total = t_mm(left[...], right[...]).astype(BF16)
        wide = total.shape[1]
        for core, place, number in order:
            index = (place, slice(at, at + rows), slice(0, wide))
            put(kept_ref, sent_ref, core, index, total[number * rows : (number + 1) * rows])
        for ref in (kept_ref, sent_ref):
            if wide < lanes:
                ref[:, at : at + rows, wide:] = jnp.zeros((ref.shape[0], rows, lanes - wide), BF16)
        at += rows
    for ref in (kept_ref, sent_ref):
        if at < ref.shape[1]:
            ref[:, at:, :] = jnp.zeros((ref.shape[0], ref.shape[1] - at, lanes), BF16)


def outer_grads(order, shards, mixed, d_attn, h, d_q):
    count = mixed.shape[0]
    shape = (len(order) // 2, eights(sum(shards)), max(d_attn.shape[1], d_q.shape[1]))
    return call(
        functools.partial(outer_body, order, shards),
        (1,),
        [whole(*one.shape) for one in (mixed, d_attn, h, d_q)],
        [whole(*shape)] * 2,
        [shaped(*shape, dtype=BF16)] * 2,
        2 * count * (mixed.shape[1] * d_attn.shape[1] + h.shape[1] * d_q.shape[1]),
    )(mixed, d_attn, h, d_q)


def first_body(order, shard, h_ref, dkv_ref, small_ref, kept_ref, sent_ref):
    small = small_ref[...].T.astype(BF16)
    total = t_mm(h_ref[...], dkv_ref[...]).astype(BF16)
    for core, place, number in order:
        rows = slice(number * shard, (number + 1) * shard)
        put(kept_ref, sent_ref, core, (place, slice(0, shard), slice(0, SMALL)), small[rows])
        put(kept_ref, sent_ref, core, (place, slice(0, shard), slice(SMALL, None)), total[rows])
    for ref in (kept_ref, sent_ref):
        if shard < ref.shape[1]:
            ref[:, shard:, :] = jnp.zeros((ref.shape[0], ref.shape[1] - shard, ref.shape[2]), BF16)


def first_grads(order, shard, h, d_kv, small):
    count, rows = h.shape
    shape = (len(order) // 2, eights(shard), d_kv.shape[1] + SMALL)
    return call(
        functools.partial(first_body, order, shard),
        (1,),
        [whole(*one.shape) for one in (h, d_kv, small)],
        [whole(*shape)] * 2,
        [shaped(*shape, dtype=BF16)] * 2,
        2 * count * rows * d_kv.shape[1],
    )(h, d_kv, small)


def middle_body(own_a, own_b, far_a, far_b, resid_ref, cot_ref, gains_ref, out_ref, dffn_a, dffn_b, sums_ref):
    ffn = load_part((own_a, own_b)) + load_part((far_a, far_b)).astype(F32)
    gain = gains_ref[POST_FFN : POST_FFN + 1]
    out_ref[...] = (resid_ref[...] + ffn * inv_rms(ffn) * gain).astype(BF16)
    d_ffn, terms = rms_back(ffn, gain, cot_ref[...].astype(F32))
    store_part((dffn_a, dffn_b), d_ffn.astype(BF16))

    @pl.when(pl.program_id(0) == 0)
    def _():
        sums_ref[...] = jnp.zeros_like(sums_ref)

    sums_ref[POST_FFN : POST_FFN + 1] += column_sum(terms)


def middle(rows, length, own, far, resid, cot, gains):
    count, width = resid.shape
    specs = part_specs(length, width, own)
    return call(
        middle_body,
        (rows,),
        specs * 2 + [rows_of(length, width)] * 2 + [whole(*gains.shape)],
        [rows_of(length, width)] + specs + [whole(8, width)],
        [shaped(count, width, dtype=BF16)] + [shaped(count // 2, width, dtype=BF16)] * 2 + [shaped(8, width)],
        20 * count * width,
    )(*own, *far, resid, cot, gains)


def place_body(links, shard, parts, own_ref, other_ref, *refs):
    outs, scratch = refs[:-1], refs[-1]
    depth = links.size["z"]
    at_x, at_c, at_z, at_y = (links.index(axis) for axis in AXES)
    number = 0
    for x in range(2):
        for core in range(2):
            for z in range(depth):
                for y in range(2):
                    slot = jnp.abs(at_x - x) + 2 * jnp.abs(at_y - y)
                    slot = slot * depth + jnp.remainder(at_z - z + depth, depth)
                    mine = own_ref[slot].astype(F32)
                    theirs = other_ref[slot].astype(F32)
                    piece = jnp.where(at_c == core, mine, theirs)
                    scratch[number] = piece
                    number += 1
    for part, out in zip(parts, outs, strict=True):
        for k in range(number):
            if len(part) == 4:
                first, count, at, lanes = part
                out[k * count : (k + 1) * count, :] = scratch[k, first : first + count, at : at + lanes].astype(out.dtype)
                continue
            if len(part) == 3:
                first, count, lanes = part
                if k < 2 * depth:
                    ids = scratch[(at_x * 2 + at_c) * 2 * depth + k]
                    for row in range(count):
                        out[row, k : k + 1, :] = ids[first + row : first + row + 1, :lanes]
                continue
            row, at, lanes, vectors = part[:4]
            for v in range(vectors):
                begin = at + v * lanes
                out[v : v + 1, k * lanes : (k + 1) * lanes] = scratch[k, row : row + 1, begin : begin + lanes]


def placed(links, own, other, parts):
    slots, rows, lanes = own.shape
    number = 2 * slots
    return pl.pallas_call(
        functools.partial(place_body, links, rows, parts),
        out_shape=[
            shaped(number * part[1], part[3], dtype=BF16)
            if len(part) == 4
            else shaped(part[1], slots // 2, part[2])
            if len(part) == 3
            else shaped(8, number * part[2])
            for part in parts
        ],
        scratch_shapes=[pltpu.VMEM((number, rows, lanes), F32)],
        compiler_params=pltpu.CompilerParams(vmem_limit_bytes=ROOM),
    )(own, other)


class Links:
    def __init__(self, mesh):
        self.size = dict(mesh.shape)
        self.pairs_only = self.size["x"] == 2 and self.size["y"] == 2

    def index(self, axis):
        return lax.axis_index(axis)

    def swap(self, array, axis):
        return lax.ppermute(array, axis, SWAP)

    def shift(self, array, step):
        depth = self.size["z"]
        pairs = [(i, i + step) for i in range(depth) if 0 <= i + step < depth]
        return lax.ppermute(array, "z", pairs)

    def turn(self, array, step):
        depth = self.size["z"]
        return lax.ppermute(array, "z", [(i, (i + step) % depth) for i in range(depth)])

    def ordered(self, own, other, axis):
        first = self.index(axis) == 0
        return jnp.where(first, jnp.stack([own, other]), jnp.stack([other, own]))

    def along_z(self, array):
        return jnp.stack([array] + [self.turn(array, k) for k in range(1, self.size["z"])])

    def across_plane(self, along):
        if not self.pairs_only:
            return along
        across = lax.ppermute(along, PLANE, [(k, 3 - k) for k in range(4)])
        return jnp.concatenate([along, self.swap(along, "x"), self.swap(along, "y"), across])

    def placed(self, array, own, parts, other=None):
        if self.pairs_only:
            other = self.swap(own, "core") if other is None else other
            return placed(self, own, other, parts)
        full = lax.all_gather(array, AXES, axis=0)
        cuts = []
        for part in parts:
            if len(part) == 4:
                r, n, c, w = part
                cuts.append(full[:, r : r + n, c : c + w].reshape(-1, w))
            elif len(part) == 3:
                r, n, w = part
                blocks = self.size["z"] * self.size["y"]
                at = (self.index("x") * 2 + self.index("core")) * blocks
                ids = lax.dynamic_slice_in_dim(full[:, r : r + n, :w], at, blocks)
                cuts.append(jnp.swapaxes(ids, 0, 1).astype(F32))
            else:
                r, c, w, n = part[:4]
                rows = jnp.swapaxes(full[:, r, c : c + n * w].reshape(-1, n, w), 0, 1).reshape(n, -1)
                cuts.append(jnp.pad(rows.astype(F32), ((0, 8 - n), (0, 0))))
        return cuts

    def order(self, axes):
        found = []
        counts = [self.size[axis] for axis in AXES]
        for number in range(math.prod(counts)):
            at, rest = {}, number
            for axis, many in zip(AXES[::-1], counts[::-1], strict=True):
                at[axis], rest = rest % many, rest // many
            place = 0
            for axis in axes:
                place = place * self.size[axis] + at[axis]
            found.append((at["core"], place, number))
        return found

    def gather_cz(self, array, dim):
        return lax.all_gather(array, ("core", "z"), axis=dim, tiled=True)

    def sum_halves(self, array, axis, dim):
        if self.size[axis] == 2:
            at = self.index(axis)
            sent = self.swap(lax.dynamic_index_in_dim(array, 1 - at, dim, False), axis)
            kept = lax.dynamic_index_in_dim(array, at, dim, False)
            return (kept.astype(F32) + sent.astype(F32)).astype(array.dtype)
        return lax.psum_scatter(array, axis, scatter_dimension=dim, tiled=False)

    def sum_cores(self, kept, sent):
        return (kept.astype(F32) + self.swap(sent, "core").astype(F32)).astype(kept.dtype)

    def sum_z(self, array, dim):
        depth = self.size["z"]
        z = self.index("z")

        def block(k):
            return lax.dynamic_index_in_dim(array, jnp.remainder(z + k, depth), dim, False)

        total = block(0).astype(F32)
        for k in range(1, depth):
            total = total + self.turn(block(k), k).astype(F32)
        return total

    def sum_z_low(self, array):
        return lax.psum_scatter(array, "z", scatter_dimension=0, tiled=True)

    def planes(self, array):
        sx, sy, sz = (self.size[axis] for axis in "xyz")
        return self.sum_halves(array.reshape((sx, sy, sz) + array.shape[1:]), "x", 0)

    def to_members(self, array):
        count = self.size["x"] * self.size["y"]
        got = lax.all_to_all(array.reshape((count, -1) + array.shape[2:]), PLANE, 0, 0, tiled=True)
        return got.reshape((count, self.size["z"]) + array.shape[1:])

    def exchange(self, array):
        count = self.size["x"] * self.size["y"]
        flat = array.reshape((count,) + array.shape[2:])
        return lax.all_to_all(flat, PLANE, 0, 0, tiled=True).reshape(array.shape)

    def over_plane(self, halves, first):
        if not self.pairs_only:
            return [first([lax.all_gather(jnp.concatenate(halves), PLANE, axis=0, tiled=True)])]
        upper, lower = halves
        size = 2 * upper.shape[0]
        near = lax.optimization_barrier((self.swap(upper, "x"), self.swap(lower, "y")))
        near = jnp.concatenate([upper, near[0], lower, near[1]])
        upper, lower, near = lax.optimization_barrier((near[:size], near[size:], near))
        upper, lower, done = lax.optimization_barrier((self.swap(upper, "y"), self.swap(lower, "x"), first([near])))
        return [done, first([upper, lower])]

    def sum_plane(self, parts, held=(), beside=(None, None)):
        works = [work or (lambda *given: ()) for work in beside]
        if not self.pairs_only:
            total = lax.psum_scatter(parts[0][0], PLANE, scatter_dimension=0, tiled=True).astype(F32)
            half = total.shape[0] // 2
            empty = [jnp.zeros((half, total.shape[1]), BF16)] * 2
            return [total[:half], total[half:]], empty, works[1](*works[0](*held))
        (near,), (upper, lower) = parts
        quarter = upper.shape[0] // 2
        upper, lower, held = lax.optimization_barrier((upper, lower, tuple(held)))
        upper, lower, extra = lax.optimization_barrier((self.swap(upper, "y"), self.swap(lower, "x"), works[0](*held)))
        at = [near[k * quarter : (k + 1) * quarter].astype(F32) for k in range(4)]
        own = [at[0] + upper[:quarter].astype(F32), at[2] + lower[:quarter].astype(F32)]
        upper = (at[1] + upper[quarter:].astype(F32)).astype(BF16)
        lower = (at[3] + lower[quarter:].astype(F32)).astype(BF16)
        upper, lower, extra = lax.optimization_barrier((upper, lower, extra))
        upper, lower, extra = lax.optimization_barrier((self.swap(upper, "x"), self.swap(lower, "y"), works[1](*extra)))
        return own, [upper, lower], extra

    def position(self, length):
        return (self.index("z") * self.size["y"] + self.index("y")) * length

    def window_bases(self, length):
        z, y, wide = self.index("z"), self.index("y"), self.size["y"]
        span = wide * length
        reach = -(-(DOC_LIMIT - 1) // span)
        base = self.position(length)
        if wide == 2 and reach == 2:
            cross = jnp.where(y == 0, z * span - length, z * span)
            return [base, base - span, base - 2 * span, cross, cross - span]
        return [(z - k) * span + j * length for k in range(reach + 1) for j in range(wide)]

    def window(self, array, length, beside):
        wide = self.size["y"]
        reach = -(-(DOC_LIMIT - 1) // (wide * length))
        if wide == 2 and reach == 2:
            first = self.index("y") == 0
            one, two, extra = lax.optimization_barrier((self.shift(array, 1), self.shift(array, 2), beside[0]()))
            near = self.swap(jnp.where(first, array, one), "y")
            far = self.swap(jnp.where(first, one, two), "y")
            near, far, extra = lax.optimization_barrier((near, far, beside[1](extra)))
            return [array, one, two, near, far], extra
        along = [lax.all_gather(array, "y", axis=0)]
        for _ in range(reach):
            along.append(self.shift(along[-1], 1))
        return [level[j] for level in along for j in range(wide)], beside[1](beside[0]())

    def window_kinds(self, length):
        if self.size["y"] == 2 and 2 * length * 2 >= DOC_LIMIT - 1 > 2 * length:
            return [F32, F32, F32, BF16, BF16]
        return [F32] * len(self.window_bases(length))

    def window_back(self, terms, length, beside=()):
        wide = self.size["y"]
        span = wide * length
        reach = -(-(DOC_LIMIT - 1) // span)
        results = []

        def follow(*arrays):
            if len(results) < len(beside):
                results.append(beside[len(results)](*(results[-1] if results else ())))
                *arrays, results[-1] = lax.optimization_barrier((*arrays, results[-1]))
            return arrays

        if wide == 2 and reach == 2:
            first = self.index("y") == 0
            own, one, two, near, far = terms
            far, near = follow(self.swap(far, "y"), self.swap(near, "y"))
            far, near = far.astype(F32), near.astype(F32)
            two = (two + jnp.where(first, 0.0, far)).astype(BF16)
            one = (one + jnp.where(first, far, near)).astype(BF16)
            own = own + jnp.where(first, near, 0.0)
            two, one, own = follow(self.shift(two, -2), self.shift(one, -1), own)
            return [own, one, two], results
        total = None
        for k in range(reach, -1, -1):
            level = jnp.stack(terms[k * wide : (k + 1) * wide])
            total = level if total is None else level + self.shift(total.astype(BF16), -1).astype(F32)
        total = lax.psum_scatter(total.astype(BF16), "y", scatter_dimension=0, tiled=False).astype(F32)
        for _ in beside:
            (total,) = follow(total)
        return [total], results


def on_device(
    links,
    tokens,
    segment_ids,
    w_query,
    w_key,
    w_value,
    w_out,
    w_gate,
    w_up,
    w_down,
    g_in,
    g_post_attn,
    g_pre_ffn,
    g_post_ffn,
    g_query,
    g_key,
    cotangent,
):
    rows, length, width = tokens.shape
    count = rows * length
    size = links.size
    sx, sc, sz, sy = (size[axis] for axis in AXES)
    parts = sx * sc * sz * sy
    shard = w_gate.shape[0]
    hidden_shard = w_down.shape[0]
    chunk = -(-hidden_shard // 16) * 16
    units = sc * sz * chunk
    head_shard = g_query.shape[0]
    tokens_flat = tokens.reshape(count, width)
    cot_flat = cotangent.reshape(count, width)

    step = jnp.arange(length, dtype=jnp.int32)
    pos_own = links.position(length) + step
    cosine, sine = rope_tables(pos_own)

    lanes = 2 * HEAD + SMALL
    vectors = jnp.concatenate([g_in, g_post_attn, g_pre_ffn, g_post_ffn, g_query, g_key])
    vectors = lax.optimization_barrier(jnp.pad(vectors, (0, 2 * HEAD - vectors.shape[0])))[None]
    seg_rows = jnp.pad(segment_ids.astype(F32), ((0, 0), (0, 2 * HEAD - length)))
    used = shard + rows + 1
    kv_shard = jnp.concatenate([jnp.concatenate([w_key, w_value], axis=1), seg_rows, vectors]).astype(BF16)
    kv_shard = jnp.pad(kv_shard, ((0, eights(used) - used), (0, 0)))
    own_ids = segment_ids.astype(F32).reshape(count, 1)
    kv_shard, own_ids, w_gate, w_up, w_query, w_out = lax.optimization_barrier(
        (kv_shard, own_ids, w_gate, w_up, w_query, w_out)
    )
    kv_along = links.along_z(kv_shard)
    full_down = links.gather_cz(jnp.pad(w_down.astype(BF16), ((0, chunk - hidden_shard), (0, 0))), 0)

    def columns(weight):
        split = weight.astype(BF16).reshape(shard, sx, sc, sz, sy, hidden_shard)
        split = jnp.pad(split, ((0, 0),) * 5 + ((0, chunk - hidden_shard),))
        return jnp.transpose(split, (1, 4, 0, 2, 3, 5)).reshape(sx, sy, shard, units)

    pair = jnp.stack([columns(w_gate), columns(w_up)], axis=2)
    wide = max(width, HEADS * HEAD)
    q_shard = jnp.pad(w_query.astype(BF16), ((0, 0), (0, wide - HEADS * HEAD)))
    o_shard = jnp.pad(w_out.astype(BF16), ((0, 0), (0, wide - width)))
    out_shard = w_out.shape[0]
    used = out_shard + shard
    qo_shard = jnp.pad(jnp.concatenate([o_shard, q_shard]), ((0, eights(used) - used), (0, 0)))
    pair, qo_shard, kv_along = lax.optimization_barrier((pair, qo_shard, kv_along))
    kv_own, pair, qo_shard = lax.optimization_barrier((links.across_plane(kv_along), pair, qo_shard))
    full_kv, gains, heads, seg_all = links.placed(
        kv_shard,
        kv_own,
        (
            (0, shard, 0, 2 * HEAD),
            (shard + rows, 0, shard, 4, True),
            (shard + rows, 4 * shard, head_shard, 2, True),
            (shard, rows, length),
        ),
    )
    h_in, k_proj, kv_low = kv_step(rows, length, tokens_flat, full_kv, gains, heads, cosine, sine)
    kv_low, qo_along, pair = lax.optimization_barrier((kv_low, links.along_z(qo_shard), links.exchange(pair)))
    pair = jnp.transpose(pair, (2, 0, 1, 3, 4)).reshape(2 * sx, sy * shard, units)
    kv, qo = links.window(
        kv_low,
        length,
        (
            lambda: (links.across_plane(qo_along),),
            lambda qo: (qo[0], links.swap(qo[0], "core") if links.pairs_only else qo[0]),
        ),
    )
    masks = (own_ids, seg_all)
    kv[2], pair = lax.optimization_barrier((kv[2], pair))
    full_pair = links.gather_cz(pair, 1).reshape(2, width, units)
    full_out, full_query = links.placed(
        qo_shard, qo[0], ((0, out_shard, 0, width), (out_shard, shard, 0, HEADS * HEAD)), qo[1]
    )

    q_proj, query, mixed, attn, resid, *h_ffn = attend(
        links, rows, length, h_in, tokens_flat, full_query, full_out, gains, heads, cosine, sine, masks, kv
    )
    parts_up = links.over_plane(h_ffn, lambda part: (part, *ffn_forward(part, full_pair, full_down)))
    h_parts, hidden, turn, act, ffn_terms = zip(*parts_up, strict=True)
    own, far, _ = links.sum_plane(ffn_terms)
    output, *d_ffn, sums_ffn = middle(rows, length, own, far, resid, cot_flat, gains)

    pending = list(zip(turn, act, strict=True))

    def back(part):
        return (part, *ffn_backward(part, *pending.pop(0), full_pair, full_down))

    d_parts, d_pairs, d_terms = zip(*links.over_plane(d_ffn, back), strict=True)
    block = sy * shard
    places = [
        [
            (c, ((z * 2 + k) * sx + x) * block, ((x * sc + c) * sz + z) * block, block)
            for x in range(sx)
            for c in range(sc)
            for z in range(sz)
        ]
        for k in range(2)
    ]
    half = units // 2
    down_places = [(c, 0, c * half, half) for c in range(sc)]

    def pair_down(kept, sent):
        sets = [([left], [one[None] for one in part]) for left, part in zip(hidden, d_parts, strict=True)]
        low = weight_grads(sets, [down_places])
        return (kept, links.swap(sent, "core"), *low)

    def pair_grads(*pairs):
        return weight_grads([(part, [pair]) for part, pair in zip(h_parts, pairs, strict=True)], places)

    own, far, (kept, got, *grad_down) = links.sum_plane(d_terms, d_pairs, (pair_grads, pair_down))
    own, far, half_pair = lax.optimization_barrier((own, far, (kept.astype(F32) + got.astype(F32)).astype(BF16)))
    grad_pair = links.sum_z_low(half_pair)

    def by_member(sums):
        return jnp.transpose(sums.reshape(2, sx, sy, shard, units), (1, 2, 0, 3, 4))

    def unpacked(got):
        got = got.reshape(sx, sy, 2, shard, sc, sz, chunk)[..., :hidden_shard]
        return jnp.transpose(got, (2, 3, 0, 4, 5, 1, 6)).reshape(2, shard, parts * hidden_shard).astype(F32)

    d_res, d_attn, d_qproj, sums_attn, heads_attn, *terms = attend_back(
        links, rows, length, own, far, cot_flat, resid, attn, q_proj, query, full_out, gains, heads, cosine, sine, masks, kv,
        links.window_kinds(length),
    )
    d_kv, beside = links.window_back(
        terms,
        length,
        (
            lambda: (
                links.sum_cores(*outer_grads(links.order("xyz"), (out_shard, shard), mixed, d_attn, h_in, d_qproj)),
                links.sum_cores(*grad_down),
            ),
            lambda second, low: (links.planes(second), low, grad_pair),
        ),
    )
    second, low, grad_pair = beside[1]
    grad_down = links.sum_z_low(low)[:hidden_shard].astype(F32)

    d_kvproj, grad_tokens, sums_in, heads_in = finish(
        rows, length, d_kv, k_proj, d_qproj, tokens_flat, d_res, full_query, full_kv, gains, heads, cosine, sine
    )
    gain_terms = (sums_ffn + sums_attn + sums_in)[:4]
    head_terms = (heads_attn + heads_in)[:2].reshape(2, parts, head_shard)
    head_terms = jnp.pad(head_terms, ((0, 0), (0, 0), (0, shard - head_shard))).reshape(2, width)
    small_terms = jnp.pad(jnp.concatenate([gain_terms, head_terms]), ((0, SMALL - 6), (0, 0)))
    first_grad = first_grads(links.order("xyz"), shard, h_in, d_kvproj, small_terms)
    first_grad, second, got_pair = lax.optimization_barrier(
        (first_grad, links.sum_halves(second, "y", 0), links.exchange(by_member(grad_pair)))
    )
    first_core = links.sum_cores(*first_grad)
    first_got, second_sum, grad_down = lax.optimization_barrier(
        (links.to_members(first_core), links.sum_z(second, 0), grad_down)
    )
    first_sum = links.sum_z(jnp.sum(first_got.astype(F32), axis=0).astype(BF16), 0)
    grad_pair = unpacked(got_pair)
    return (
        output.reshape(tokens.shape),
        grad_tokens.reshape(tokens.shape),
        second_sum[out_shard : out_shard + shard, : HEADS * HEAD],
        first_sum[:shard, SMALL : SMALL + HEAD],
        first_sum[:shard, SMALL + HEAD :],
        second_sum[:out_shard, :width],
        grad_pair[0],
        grad_pair[1],
        grad_down,
        *(first_sum[:shard, k] for k in range(4)),
        *(first_sum[:head_shard, 4 + k] for k in range(2)),
    )


def solution(mesh):
    plane = mesh.shape["dp"] // 2
    by_chip = Mesh(mesh.devices.reshape(plane, 2, -1, plane), AXES)
    links = Links(by_chip)
    placed = P(("x", "core"), ("z", "y"), None)
    matrix = P(AXES, None)
    vector = P(AXES)
    in_specs = (placed, P(("x", "core"), ("z", "y"))) + (matrix,) * 7 + (vector,) * 6 + (placed,)
    out_specs = (placed, placed) + (matrix,) * 7 + (vector,) * 6

    def step(*arguments):
        return on_device(links, *arguments)

    return jax.shard_map(step, mesh=by_chip, in_specs=in_specs, out_specs=out_specs, check_vma=False)
```
